128 devices in a mesh: dp: 8 (over x, core), ctx: 4 (over y), head: 4 (over z).
Axes of the slice: x: 4, y: 4, z: 4, core: 2. Of those that a mesh axis runs over, the one named last changes fastest.
Arguments:
- tokens: bfloat16 [8, 1024, 2048], P('dp', 'ctx'), may hold values from -6 to 6
- proj_weights: bfloat16 [3, 2048, 1024], P(None, None, 'head'), may hold values from -0.125 to 0.125
- init_weight: float32 [8, 128, 128], P('head'), may hold values from -0.5 to 0.5
- base_rates: float32 [8], P('head'), may hold values from 0.005 to 1
- gate_values: float32 [8, 8, 1024], P('dp', 'head', 'ctx'), may hold values from 0.3 to 480
- out_gain: float32 [8, 128], P('head'), may hold values from 0.5 to 1.5
- cotangent: bfloat16 [8, 1024, 1024], P('dp', 'ctx', 'head'), may hold values from -6 to 6
Outputs:
- grad_tokens: bfloat16 [8, 1024, 2048], P('dp', 'ctx', 'head')
- grad_proj: float32 [3, 2048, 1024], P(None, None, 'head')
- grad_init: float32 [8, 128, 128], P('head')
- grad_gain: float32 [8, 128], P('head')
- grad_rates: float32 [8], P('head')
- grad_gates: float32 [8, 8, 1024], P('dp', 'head', 'ctx')
The draws below stay inside these ranges and needn't reach their ends.
All inputs are finite; a program needn't handle non-finite values.
Results may differ from the reference program's by a relative error of at most 0.0072.
Values sent between devices are 32-bit elements; how exact they have to be, the bound alone decides.
No kernel may reach another device: no remote copies, remote signals or barrier semaphores. Data moves between devices by JAX's collectives and lax.ppermute only.
A program may use at most 64 MiB of HBM per device.

```python
import jax
import jax.numpy as jnp
from jax import lax

D = 2048
HS = 128
MB = 16
HEADS = 8
SEQS = 8
LEN = 1024


def draw_base_rates(key, part):
    uniform_key = jax.random.fold_in(key, 11)
    exponent = jax.random.uniform(uniform_key, (HEADS,), jnp.float32, jnp.log(0.005), jnp.log(1.0))
    return jnp.clip(jnp.exp(exponent), 0.005, 1.0)


def draw_gate_values(key, part):
    base_key = jax.random.fold_in(key, 21)
    start_key = jax.random.fold_in(key, 22)
    level_key = jax.random.fold_in(key, 23)
    baseline = jax.random.uniform(base_key, (SEQS, HEADS, LEN), jnp.float32, 0.5, 1.0)
    starts = jax.random.randint(start_key, (SEQS, HEADS, 2), 0, LEN // MB - 3) * MB
    places = jnp.arange(LEN, dtype=jnp.int32)
    inside = jnp.any((places[None, None, None, :] >= starts[..., None]) & (places[None, None, None, :] < starts[..., None] + 3 * MB), axis=2)
    levels = jax.random.uniform(level_key, (SEQS, HEADS, LEN), jnp.float32, 300.0, 480.0)
    return jnp.where(inside, levels, baseline)


def block_levels(rng, dims, shards, low, top_value):
    loudness = 1.0
    for axis_at, blocks in shards:
        steps = jax.random.uniform(jax.random.fold_in(jax.random.fold_in(rng, 6), axis_at), (blocks,), jnp.float32, low / len(shards), top_value / len(shards))
        loudness = loudness * jnp.repeat(jnp.exp(steps), dims[axis_at] // blocks).reshape((-1,) + (1,) * (len(dims) - 1 - axis_at))
    return loudness


def gaussian(stream_key, dims, scale, reach, cuts=(), held_as=jnp.bfloat16):
    factor_of = block_levels(stream_key, dims, cuts, -0.22, 0.18) if cuts else 1.0
    result = jax.random.normal(stream_key, dims, jnp.float32) * scale * factor_of
    return jnp.minimum(jnp.maximum(result, -reach), reach).astype(held_as)


def setup_inputs(seed: int = 0) -> dict:
    seeds = jax.random.split(jax.random.key(seed), 8)
    return {
        "tokens": gaussian(seeds[0], (SEQS, LEN, D), 1.0, 6.0, ((0, 8), (1, 4))),
        "proj_weights": gaussian(seeds[1], (3, D, HEADS * HS), D ** -0.5, 0.125, ((2, 4),)),
        "init_weight": gaussian(seeds[2], (HEADS, HS, HS), HS ** -0.5, 0.5, ((0, 4),), jnp.float32),
        "base_rates": draw_base_rates(jax.random.fold_in(seeds[7], 71), 0),
        "gate_values": draw_gate_values(jax.random.fold_in(seeds[7], 71), 0),
        "out_gain": jnp.clip(1.0 + 0.1 * jax.random.normal(seeds[5], (HEADS, HS), jnp.float32), 0.5, 1.5),
        "cotangent": gaussian(seeds[6], (SEQS, LEN, HEADS * HS), 1.0, 6.0, ((0, 8), (1, 4), (2, 4))),
    }


EXACT_MODE = lax.Precision.HIGHEST

def matmul_hi(left, right):
    return jnp.matmul(left, right, precision=EXACT_MODE)

def one_head(query_rows, key_rows, value_rows, first_weight, rate_value, gate_row, gain_row):
    norm_inv = lax.rsqrt(lax.optimization_barrier(jnp.sum(key_rows * key_rows, -1, keepdims=True)) + 1e-06)
    keys = key_rows * norm_inv
    boosted = rate_value * gate_row
    step_rate = boosted / (1.0 + boosted)
    block_count = query_rows.shape[0] // MB
    query_blocks = query_rows.reshape(block_count, MB, HS)
    key_blocks = keys.reshape(block_count, MB, HS)
    value_blocks = value_rows.reshape(block_count, MB, HS)
    rate_blocks = step_rate.reshape(block_count, MB)
    causal = jnp.tril(jnp.ones((MB, MB), jnp.float32))

    def advance(weight, pieces):
        query_block, key_block, value_block, rate_block = pieces
        mixing = matmul_hi(query_block, key_block.T) * causal * rate_block[None, :]
        residual = value_block - matmul_hi(key_block, weight)
        inner_out = matmul_hi(query_block, weight) + matmul_hi(mixing, residual)
        weight = weight + matmul_hi(key_block.T, rate_block[:, None] * residual)
        return (weight, inner_out)
    _, outputs = lax.scan(advance, first_weight, (query_blocks, key_blocks, value_blocks, rate_blocks))
    inner_out = outputs.reshape(-1, HS)
    centred = inner_out - lax.optimization_barrier(jnp.mean(inner_out, -1, keepdims=True))
    normed = centred * lax.rsqrt(lax.optimization_barrier(jnp.mean(centred * centred, -1, keepdims=True)) + 1e-05)
    return query_rows + gain_row * normed

def reference(tokens, proj_weights, init_weight, base_rates, gate_values, out_gain, cotangent):
    flattened = tokens.reshape(-1, D)
    projected = [jnp.dot(flattened, proj_weights[which], preferred_element_type=jnp.float32).astype(jnp.bfloat16) for which in range(3)]

    def heads_first(array):
        return array.reshape(SEQS, LEN, HEADS, HS).transpose(2, 0, 1, 3)

    def per_head(pieces):
        query_all, key_all, value_all, first_weight, rate_value, gate_rows, gain_row, upstream = pieces

        def forward(query_f, key_f, value_f, weight_f, rate_f, gate_f, gain_f):
            return jax.vmap(one_head, in_axes=(0, 0, 0, None, None, 0, None))(query_f, key_f, value_f, weight_f, rate_f, gate_f, gain_f)
        _, pullback = jax.vjp(forward, query_all.astype(jnp.float32), key_all.astype(jnp.float32), value_all.astype(jnp.float32), first_weight, rate_value, gate_rows, gain_row)
        return pullback(upstream.astype(jnp.float32))
    grads = lax.map(per_head, (heads_first(projected[0]), heads_first(projected[1]), heads_first(projected[2]), init_weight, base_rates, gate_values.transpose(1, 0, 2), out_gain, heads_first(cotangent)))
    grad_query, grad_keyraw, grad_value, grad_first, grad_rate, grad_gatev, grad_gainv = grads

    def back_rows(array):
        return array.transpose(1, 2, 0, 3).reshape(SEQS * LEN, HEADS * HS).astype(jnp.bfloat16)
    local_grads = [back_rows(grad_query), back_rows(grad_keyraw), back_rows(grad_value)]
    grad_proj = jnp.stack([lax.dot_general(flattened, local_grads[which], (((0,), (0,)), ((), ())), preferred_element_type=jnp.float32) for which in range(3)])
    token_sum = jnp.dot(local_grads[0], proj_weights[0].T, preferred_element_type=jnp.float32)
    token_sum = token_sum + jnp.dot(local_grads[1], proj_weights[1].T, preferred_element_type=jnp.float32)
    token_sum = token_sum + jnp.dot(local_grads[2], proj_weights[2].T, preferred_element_type=jnp.float32)
    grad_tokens = token_sum.astype(jnp.bfloat16).reshape(SEQS, LEN, D)
    return (grad_tokens, grad_proj, grad_first, grad_gainv, grad_rate, grad_gatev.transpose(1, 0, 2))
```

```python
import functools

import jax
import jax.numpy as jnp
from jax import lax
from jax.experimental import pallas as pl
from jax.experimental.pallas import tpu as pltpu
from jax.sharding import PartitionSpec as P

MB = 16
HS = 128
F32 = jnp.float32
BF = jnp.bfloat16
NN = (((1,), (0,)), ((), ()))
NT = (((1,), (1,)), ((), ()))
TN = (((0,), (0,)), ((), ()))


def dot(a, b, dims, passes):
    ah = a.astype(BF)
    bh = b.astype(BF)
    result = lax.dot_general(ah, bh, dims, preferred_element_type=F32)
    if passes == 3:
        al = (a - ah.astype(F32)).astype(BF)
        bl = (b - bh.astype(F32)).astype(BF)
        result = result + (
            lax.dot_general(ah, bl, dims, preferred_element_type=F32)
            + lax.dot_general(al, bh, dims, preferred_element_type=F32)
        )
    return result


def places(n):
    return (
        lax.broadcasted_iota(jnp.int32, (n, n), 0),
        lax.broadcasted_iota(jnp.int32, (n, n), 1),
    )


def to_col(row):
    i, j = places(row.shape[1])
    return jnp.sum(jnp.where(i == j, row, 0.0), axis=1, keepdims=True)


def to_row(col):
    i, j = places(col.shape[0])
    return jnp.sum(jnp.where(i == j, col, 0.0), axis=0, keepdims=True)


def unit_lower_inverses(lowers):
    n = lowers[0].shape[0]
    i, j = places(n)
    size = 2 * MB
    same = (i // size) == (j // size)
    inverses = [jnp.where(i == j, 1.0, 0.0) - jnp.where(same, low, 0.0) for low in lowers]
    while size < n:
        pair = ((i // (2 * size)) == (j // (2 * size))) & ((i // size) != (j // size))
        corners = [jnp.where(pair, low, 0.0) for low in lowers]
        halves = [dot(inv, corner, NN, 3) for inv, corner in zip(inverses, corners)]
        inverses = [inv - dot(half, inv, NN, 3) for inv, half in zip(inverses, halves)]
        size *= 2
    return inverses


def span(h):
    return slice(h * HS, (h + 1) * HS)


def rates_of(base_ref, gate_ref, h):
    boost = base_ref[h] * gate_ref[0, h : h + 1, :]
    return boost, boost / (1.0 + boost)


def maps_kernel(
    ctx_ref, base_ref, tok_ref, wk_ref, wv_ref, gate_ref, init_ref,
    k_ref, v_ref, ninv_ref, gram_ref, inv_ref, bt_ref, d_ref, send_ref, o_ref,
):
    tok = tok_ref[0]
    kraw_all = jnp.dot(tok, wk_ref[0], preferred_element_type=F32).astype(BF).astype(F32)
    v_all = jnp.dot(tok, wv_ref[0], preferred_element_type=F32).astype(BF).astype(F32)
    n = kraw_all.shape[0]
    i, j = places(n)
    strict = (i // MB) > (j // MB)
    heads = range(init_ref.shape[0])
    ks, kts, es, lows = [], [], [], []
    for h in heads:
        kraw = kraw_all[:, span(h)]
        ninv = lax.rsqrt(jnp.sum(kraw * kraw, -1, keepdims=True) + 1e-06)
        k = kraw * ninv
        kt = k.T
        _, e = rates_of(base_ref, gate_ref, h)
        gram = dot(k, kt, NN, 3)
        ninv_ref[h] = jnp.broadcast_to(ninv, (n, HS))
        k_ref[:, span(h)] = k
        gram_ref[h] = gram
        ks.append(k)
        kts.append(kt)
        es.append(e)
        lows.append(jnp.where(strict, gram * e, 0.0))
    v_ref[...] = v_all
    inverses = unit_lower_inverses(lows)
    a, b = places(HS)
    for h in heads:
        bt = dot(kts[h] * es[h], inverses[h], NN, 3)
        inv_ref[h] = inverses[h]
        bt_ref[h] = bt
        decay = jnp.where(a == b, 1.0, 0.0) - dot(bt, ks[h], NN, 3)
        offset = dot(bt, v_all[:, span(h)], NN, 3)
        d_ref[h] = decay
        o_ref[h] = offset
        first = dot(decay, init_ref[h], NN, 3) + offset
        send_ref[h] = jnp.where(ctx_ref[0] == 0, first, offset)


def reach_kernel(base_ref, tok_ref, wq_ref, gate_ref, k_ref, v_ref, inv_ref,
                 q_ref, score_ref, rv_ref, y_ref, qt_ref, zv_ref):
    q_all = jnp.dot(tok_ref[0], wq_ref[0], preferred_element_type=F32).astype(BF).astype(F32)
    n = q_all.shape[0]
    i, j = places(n)
    q_ref[...] = q_all
    for h in range(inv_ref.shape[0]):
        q = q_all[:, span(h)]
        k = k_ref[:, span(h)]
        _, e = rates_of(base_ref, gate_ref, h)
        score = dot(q, k, NT, 3)
        mix = jnp.where(i >= j, score * e, 0.0)
        inv = inv_ref[h]
        rv = dot(inv, v_ref[:, span(h)], NN, 3)
        y = dot(inv, k, NN, 3)
        score_ref[h] = score
        rv_ref[:, span(h)] = rv
        y_ref[:, span(h)] = y
        qt_ref[:, span(h)] = q - dot(mix, y, NN, 3)
        zv_ref[:, span(h)] = dot(mix, rv, NN, 3)


def step_kernel(d_ref, w_ref, o_ref, out_ref, *, transposed):
    for h in range(d_ref.shape[0]):
        out_ref[h] = o_ref[h] + dot(d_ref[h], w_ref[h], TN if transposed else NN, 3)


def norm_kernel(
    ctx_ref, init_ref, near_ref, mid_ref, far_ref, rd_ref, qt_ref, zv_ref, up_ref, gain_ref,
    w_ref, h_ref, p_ref, dgain_ref,
):
    ctx = ctx_ref[0]
    for h in range(init_ref.shape[0]):
        last = dot(rd_ref[h], far_ref[h], NN, 3) + near_ref[h]
        start = jnp.where(
            ctx == 0, init_ref[h], jnp.where(ctx == 1, near_ref[h], jnp.where(ctx == 2, mid_ref[h], last))
        )
        w_ref[h] = start
        qt = qt_ref[:, span(h)]
        z = dot(qt, start, NN, 3) + zv_ref[:, span(h)]
        up = up_ref[0, :, span(h)].astype(F32)
        centred = z - jnp.mean(z, -1, keepdims=True)
        inv_std = lax.rsqrt(jnp.mean(centred * centred, -1, keepdims=True) + 1e-05)
        normed = centred * inv_std
        weighted = up * gain_ref[h : h + 1, :]
        back = inv_std * (
            weighted
            - jnp.mean(weighted, -1, keepdims=True)
            - normed * jnp.mean(weighted * normed, -1, keepdims=True)
        )
        h_ref[:, span(h)] = back
        p_ref[h] = dot(qt, back, TN, 3)
        dgain_ref[h : h + 1, :] = jnp.sum(up * normed, axis=0, keepdims=True)


def query_kernel(
    base_ref, gate_ref, w_ref, h_ref, up_ref, q_ref, score_ref, rv_ref, y_ref, k_ref, inv_ref,
    dq_ref, r_ref, x_ref, dk_ref, de_ref,
):
    n = h_ref.shape[0]
    i, j = places(n)
    for h in range(w_ref.shape[0]):
        w = w_ref[h]
        back = h_ref[:, span(h)]
        k = k_ref[:, span(h)]
        q = q_ref[:, span(h)]
        score = score_ref[h]
        _, e = rates_of(base_ref, gate_ref, h)
        mix = jnp.where(i >= j, score * e, 0.0)
        r = rv_ref[:, span(h)] - dot(y_ref[:, span(h)], w, NN, 3)
        r_ref[:, span(h)] = r
        d_mix = jnp.where(i >= j, dot(back, r, NT, 3), 0.0)
        d_score = d_mix * e
        dq = up_ref[0, :, span(h)].astype(F32) + dot(back, w, NT, 3) + dot(d_score, k, NN, 3)
        dq_ref[:, span(h)] = dq.astype(BF)
        x_ref[:, span(h)] = dot(inv_ref[h], dot(mix, back, TN, 3), TN, 3)
        dk_ref[:, span(h)] = dot(d_score, q, TN, 3)
        de_ref[h : h + 1, :] = jnp.sum(d_mix * score, axis=0, keepdims=True)


def keys_kernel(
    ctx_ref, base_ref, gate_ref, rp_ref, mid_ref, far_ref, rd_ref, p_ref, d_ref, w_ref, k_ref, ninv_ref,
    gram_ref, bt_ref, r_ref, x_ref, dk_ref, de_ref, dgain_ref,
    dkraw_ref, dv_ref, gates_ref, extra_ref,
):
    ctx = ctx_ref[0]
    n = k_ref.shape[0]
    i, j = places(n)
    strict = (i // MB) > (j // MB)
    extra_ref[...] = jnp.zeros_like(extra_ref)
    for h in range(w_ref.shape[0]):
        first = rp_ref[h] + dot(rd_ref[h], far_ref[h], TN, 3)
        end = jnp.where(
            ctx == 0, first, jnp.where(ctx == 1, mid_ref[h], jnp.where(ctx == 2, rp_ref[h], 0.0))
        )
        extra_ref[h, 0:HS, :] = jnp.where(ctx == 0, p_ref[h] + dot(d_ref[h], end, TN, 3), 0.0)
        w = w_ref[h]
        k = k_ref[:, span(h)]
        r = r_ref[:, span(h)]
        boost, e = rates_of(base_ref, gate_ref, h)
        x = x_ref[:, span(h)] + dot(bt_ref[h], end, TN, 3)
        dv_ref[:, span(h)] = x.astype(BF)
        d_low = jnp.where(strict, -dot(x, r, NT, 3), 0.0)
        d_gram = d_low * e
        dk = (
            dk_ref[:, span(h)]
            - dot(x, w, NT, 3)
            + to_col(e) * dot(r, end, NT, 3)
            + dot(d_gram + d_gram.T, k, NN, 3)
        )
        pull = to_row(jnp.sum(r * dot(k, end, NN, 3), axis=1, keepdims=True))
        de = de_ref[h : h + 1, :] + jnp.sum(d_low * gram_ref[h], axis=0, keepdims=True) + pull
        draw = ninv_ref[h] * (dk - k * jnp.sum(k * dk, -1, keepdims=True))
        dkraw_ref[:, span(h)] = draw.astype(BF)
        d_boost = de / ((1.0 + boost) * (1.0 + boost))
        gates_ref[0, h : h + 1, :] = d_boost * base_ref[h]
        extra_ref[h, HS : HS + 1, :] = dgain_ref[h : h + 1, :]
        extra_ref[h, HS + 1 : HS + 2, :] = jnp.broadcast_to(
            jnp.sum(d_boost * gate_ref[0, h : h + 1, :], axis=1, keepdims=True), (1, HS)
        )


VM = pl.BlockSpec(memory_space=pltpu.VMEM)
SM = pl.BlockSpec(memory_space=pltpu.SMEM)
PARAMS = pltpu.CompilerParams(vmem_limit_bytes=48 * 1024 * 1024)


def shape(*dims, dtype=F32):
    return jax.ShapeDtypeStruct(dims, dtype)


def whole(kernel, outs, specs):
    return pl.pallas_call(
        kernel,
        out_shape=outs,
        in_specs=specs,
        out_specs=jax.tree.map(lambda _: VM, outs),
        compiler_params=PARAMS,
    )


def part(which, dims):
    return pl.BlockSpec((1,) + dims, lambda i: (which, 0, 0))


def full(*dims):
    return pl.BlockSpec(dims, lambda i: (0,) * len(dims))


def body(tokens, proj_weights, init_weight, base_rates, gate_values, out_gain, cotangent):
    n = tokens.shape[1]
    model = tokens.shape[2]
    heads = init_weight.shape[0]
    wide = heads * HS
    ctx = lax.axis_index("ctx")
    ctx_arr = ctx.astype(jnp.int32).reshape(1)

    wide_f32 = shape(n, wide)
    square = shape(heads, n, n)
    small = shape(heads, HS, HS)
    wspec = functools.partial(part, dims=(model, wide))

    k, v, ninv, gram, inv, bt, decay, send, offset = pl.pallas_call(
        maps_kernel,
        grid=(1,),
        out_shape=(wide_f32, wide_f32, shape(heads, n, HS), square, square, shape(heads, HS, n), small, small, small),
        in_specs=[SM, SM, full(1, n, model), wspec(1), wspec(2), full(1, heads, n), full(heads, HS, HS)],
        out_specs=(
            full(n, wide), full(n, wide), full(heads, n, HS), full(heads, n, n), full(heads, n, n),
            full(heads, HS, n), full(heads, HS, HS), full(heads, HS, HS), full(heads, HS, HS),
        ),
        compiler_params=PARAMS,
    )(ctx_arr, base_rates, tokens, proj_weights, proj_weights, gate_values, init_weight)

    near = lax.ppermute(send, "ctx", [(0, 1), (2, 3)])
    moved = lax.ppermute(decay, "ctx", [(2, 3), (1, 0)])

    q, score, rv, y, qt, zv = pl.pallas_call(
        reach_kernel,
        grid=(1,),
        out_shape=(wide_f32, square, wide_f32, wide_f32, wide_f32, wide_f32),
        in_specs=[SM, full(1, n, model), wspec(0), full(1, heads, n), full(n, wide), full(n, wide), full(heads, n, n)],
        out_specs=(full(n, wide), full(heads, n, n), full(n, wide), full(n, wide), full(n, wide), full(n, wide)),
        compiler_params=PARAMS,
    )(base_rates, tokens, proj_weights, gate_values, k, v, inv)

    second = whole(functools.partial(step_kernel, transposed=False), small, [VM] * 3)(decay, near, offset)
    mid = lax.ppermute(second, "ctx", [(1, 2)])
    far = lax.ppermute(second, "ctx", [(1, 3)])

    w, back, pulled, dgain = whole(
        norm_kernel, (small, wide_f32, small, shape(heads, HS)), [SM] + [VM] * 9
    )(ctx_arr, init_weight, near, mid, far, moved, qt, zv, cotangent, out_gain)

    back_near = lax.ppermute(pulled, "ctx", [(3, 2), (1, 0)])

    dq, r, x, dk, de = whole(
        query_kernel,
        (shape(n, wide, dtype=BF), wide_f32, wide_f32, wide_f32, shape(heads, n)),
        [SM] + [VM] * 10,
    )(base_rates, gate_values, w, back, cotangent, q, score, rv, y, k, inv)

    back_second = whole(functools.partial(step_kernel, transposed=True), small, [VM] * 3)(decay, back_near, pulled)
    back_mid = lax.ppermute(back_second, "ctx", [(2, 1)])
    back_far = lax.ppermute(back_second, "ctx", [(2, 0)])

    dkraw, dv, grad_gates, extra = whole(
        keys_kernel,
        (shape(n, wide, dtype=BF), shape(n, wide, dtype=BF), shape(1, heads, n), shape(heads, HS + 8, HS)),
        [SM, SM] + [VM] * 17,
    )(ctx_arr, base_rates, gate_values, back_near, back_mid, back_far, moved, pulled, decay, w, k, ninv, gram, bt, r, x,
      dk, de, dgain)

    flat = tokens[0]
    local = jnp.concatenate([dq, dkraw, dv], axis=1)
    proj_terms = jnp.stack(
        [
            lax.dot_general(flat, d, (((0,), (0,)), ((), ())), preferred_element_type=F32)
            for d in (dq, dkraw, dv)
        ]
    )
    grad_proj, extra = lax.psum((proj_terms, extra), ("dp", "ctx"))
    weights = jnp.concatenate([proj_weights[0], proj_weights[1], proj_weights[2]], axis=1)
    summed = lax.dot_general(weights, local, (((1,), (1,)), ((), ())), preferred_element_type=F32)
    token_rows = lax.psum_scatter(summed, "head", scatter_dimension=0, tiled=True)
    grad_tokens = token_rows.T.astype(BF).reshape(1, n, -1)
    return (grad_tokens, grad_proj, extra[:, :HS], extra[:, HS], extra[:, HS + 1, 0], grad_gates)


def solution(mesh):
    in_specs = (
        P("dp", "ctx", None),
        P(None, None, "head"),
        P("head", None, None),
        P("head"),
        P("dp", "head", "ctx"),
        P("head", None),
        P("dp", "ctx", "head"),
    )
    out_specs = (
        P("dp", "ctx", "head"),
        P(None, None, "head"),
        P("head", None, None),
        P("head", None),
        P("head"),
        P("dp", "head", "ctx"),
    )
    return jax.shard_map(body, mesh=mesh, in_specs=in_specs, out_specs=out_specs, check_vma=False)
```

```python
import functools

import jax
import jax.numpy as jnp
from jax import lax
from jax.experimental import pallas as pl
from jax.experimental.pallas import tpu as pltpu
from jax.sharding import PartitionSpec as P

MB = 16
HS = 128
RING = 4
TURNS = (0, 1, 3, 2)
CHUNK = 256
PIECE = 24
EXTRA = 2 * RING * PIECE
F32 = jnp.float32
BF = jnp.bfloat16
NN = (((1,), (0,)), ((), ()))
NT = (((1,), (1,)), ((), ()))
TN = (((0,), (0,)), ((), ()))


def dot(a, b, dims, passes):
    ah = a.astype(BF)
    bh = b.astype(BF)
    result = lax.dot_general(ah, bh, dims, preferred_element_type=F32)
    if passes == 3:
        al = (a - ah.astype(F32)).astype(BF)
        bl = (b - bh.astype(F32)).astype(BF)
        result = result + (
            lax.dot_general(ah, bl, dims, preferred_element_type=F32)
            + lax.dot_general(al, bh, dims, preferred_element_type=F32)
        )
    return result


def places(n):
    return (
        lax.broadcasted_iota(jnp.int32, (n, n), 0),
        lax.broadcasted_iota(jnp.int32, (n, n), 1),
    )


def to_col(row):
    i, j = places(row.shape[1])
    return jnp.sum(jnp.where(i == j, row, 0.0), axis=1, keepdims=True)


def to_row(col):
    i, j = places(col.shape[0])
    return jnp.sum(jnp.where(i == j, col, 0.0), axis=0, keepdims=True)


def unit_lower_inverses(lowers):
    n = lowers[0].shape[0]
    i, j = places(n)
    size = 2 * MB
    same = (i // size) == (j // size)
    inverses = [jnp.where(i == j, 1.0, 0.0) - jnp.where(same, low, 0.0) for low in lowers]
    while size < n:
        pair = ((i // (2 * size)) == (j // (2 * size))) & ((i // size) != (j // size))
        corners = [jnp.where(pair, low, 0.0) for low in lowers]
        halves = [dot(inv, corner, NN, 3) for inv, corner in zip(inverses, corners)]
        inverses = [inv - dot(half, inv, NN, 3) for inv, half in zip(inverses, halves)]
        size *= 2
    return inverses


def span(h):
    return slice(h * HS, (h + 1) * HS)


def rates_of(base_ref, gate_ref, h):
    boost = base_ref[h] * gate_ref[0, h : h + 1, :]
    return boost, boost / (1.0 + boost)


def maps_kernel(
    ctx_ref, base_ref, tok_ref, wk_ref, wv_ref, gate_ref, init_ref,
    k_ref, v_ref, ninv_ref, gram_ref, inv_ref, bt_ref, d_ref, send_ref, o_ref,
):
    tok = tok_ref[0]
    kraw_all = jnp.dot(tok, wk_ref[0], preferred_element_type=F32).astype(BF).astype(F32)
    v_all = jnp.dot(tok, wv_ref[0], preferred_element_type=F32).astype(BF).astype(F32)
    n = kraw_all.shape[0]
    i, j = places(n)
    strict = (i // MB) > (j // MB)
    heads = range(init_ref.shape[0])
    ks, kts, es, lows = [], [], [], []
    for h in heads:
        kraw = kraw_all[:, span(h)]
        ninv = lax.rsqrt(jnp.sum(kraw * kraw, -1, keepdims=True) + 1e-06)
        k = kraw * ninv
        kt = k.T
        _, e = rates_of(base_ref, gate_ref, h)
        gram = dot(k, kt, NN, 3)
        ninv_ref[h] = jnp.broadcast_to(ninv, (n, HS))
        k_ref[:, span(h)] = k
        gram_ref[h] = gram
        ks.append(k)
        kts.append(kt)
        es.append(e)
        lows.append(jnp.where(strict, gram * e, 0.0))
    v_ref[...] = v_all
    inverses = unit_lower_inverses(lows)
    a, b = places(HS)
    for h in heads:
        bt = dot(kts[h] * es[h], inverses[h], NN, 3)
        inv_ref[h] = inverses[h]
        bt_ref[h] = bt
        decay = jnp.where(a == b, 1.0, 0.0) - dot(bt, ks[h], NN, 3)
        offset = dot(bt, v_all[:, span(h)], NN, 3)
        d_ref[h] = decay
        o_ref[h] = offset
        first = dot(decay, init_ref[h], NN, 3) + offset
        send_ref[h] = jnp.where(ctx_ref[0] == 0, first, offset)


def reach_kernel(base_ref, tok_ref, wq_ref, gate_ref, k_ref, v_ref, inv_ref,
                 q_ref, score_ref, rv_ref, y_ref, qt_ref, zv_ref):
    q_all = jnp.dot(tok_ref[0], wq_ref[0], preferred_element_type=F32).astype(BF).astype(F32)
    n = q_all.shape[0]
    i, j = places(n)
    q_ref[...] = q_all
    for h in range(inv_ref.shape[0]):
        q = q_all[:, span(h)]
        k = k_ref[:, span(h)]
        _, e = rates_of(base_ref, gate_ref, h)
        score = dot(q, k, NT, 3)
        mix = jnp.where(i >= j, score * e, 0.0)
        inv = inv_ref[h]
        rv = dot(inv, v_ref[:, span(h)], NN, 3)
        y = dot(inv, k, NN, 3)
        score_ref[h] = score
        rv_ref[:, span(h)] = rv
        y_ref[:, span(h)] = y
        qt_ref[:, span(h)] = q - dot(mix, y, NN, 3)
        zv_ref[:, span(h)] = dot(mix, rv, NN, 3)


def step_kernel(d_ref, w_ref, o_ref, out_ref, *, transposed):
    for h in range(d_ref.shape[0]):
        out_ref[h] = o_ref[h] + dot(d_ref[h], w_ref[h], TN if transposed else NN, 3)


def norm_kernel(
    ctx_ref, init_ref, near_ref, mid_ref, far_ref, rd_ref, qt_ref, zv_ref, up_ref, gain_ref,
    w_ref, h_ref, p_ref, dgain_ref,
):
    ctx = ctx_ref[0]
    for h in range(init_ref.shape[0]):
        last = dot(rd_ref[h], far_ref[h], NN, 3) + near_ref[h]
        start = jnp.where(
            ctx == 0, init_ref[h], jnp.where(ctx == 1, near_ref[h], jnp.where(ctx == 2, mid_ref[h], last))
        )
        w_ref[h] = start
        qt = qt_ref[:, span(h)]
        z = dot(qt, start, NN, 3) + zv_ref[:, span(h)]
        up = up_ref[0, :, span(h)].astype(F32)
        centred = z - jnp.mean(z, -1, keepdims=True)
        inv_std = lax.rsqrt(jnp.mean(centred * centred, -1, keepdims=True) + 1e-05)
        normed = centred * inv_std
        weighted = up * gain_ref[h : h + 1, :]
        back = inv_std * (
            weighted
            - jnp.mean(weighted, -1, keepdims=True)
            - normed * jnp.mean(weighted * normed, -1, keepdims=True)
        )
        h_ref[:, span(h)] = back
        p_ref[h] = dot(qt, back, TN, 3)
        dgain_ref[h : h + 1, :] = jnp.sum(up * normed, axis=0, keepdims=True)


def query_kernel(
    base_ref, gate_ref, w_ref, h_ref, up_ref, q_ref, score_ref, rv_ref, y_ref, k_ref, inv_ref,
    dq_ref, r_ref, x_ref, dk_ref, de_ref,
):
    n = h_ref.shape[0]
    i, j = places(n)
    for h in range(w_ref.shape[0]):
        w = w_ref[h]
        back = h_ref[:, span(h)]
        k = k_ref[:, span(h)]
        q = q_ref[:, span(h)]
        score = score_ref[h]
        _, e = rates_of(base_ref, gate_ref, h)
        mix = jnp.where(i >= j, score * e, 0.0)
        r = rv_ref[:, span(h)] - dot(y_ref[:, span(h)], w, NN, 3)
        r_ref[:, span(h)] = r
        d_mix = jnp.where(i >= j, dot(back, r, NT, 3), 0.0)
        d_score = d_mix * e
        dq = up_ref[0, :, span(h)].astype(F32) + dot(back, w, NT, 3) + dot(d_score, k, NN, 3)
        dq_ref[:, span(h)] = dq.astype(BF).astype(F32)
        x_ref[:, span(h)] = dot(inv_ref[h], dot(mix, back, TN, 3), TN, 3)
        dk_ref[:, span(h)] = dot(d_score, q, TN, 3)
        de_ref[h : h + 1, :] = jnp.sum(d_mix * score, axis=0, keepdims=True)


def keys_kernel(
    ctx_ref, base_ref, gate_ref, rp_ref, mid_ref, far_ref, rd_ref, p_ref, d_ref, w_ref, k_ref, ninv_ref,
    gram_ref, bt_ref, r_ref, x_ref, dk_ref, de_ref, dgain_ref,
    dkraw_ref, dv_ref, gates_ref,
):
    ctx = ctx_ref[0]
    n = k_ref.shape[0]
    i, j = places(n)
    strict = (i // MB) > (j // MB)
    dkraw_ref[n + HS : n + EXTRA, :] = jnp.zeros((EXTRA - HS, dkraw_ref.shape[1]), F32)
    for h in range(w_ref.shape[0]):
        first = rp_ref[h] + dot(rd_ref[h], far_ref[h], TN, 3)
        end = jnp.where(
            ctx == 0, first, jnp.where(ctx == 1, mid_ref[h], jnp.where(ctx == 2, rp_ref[h], 0.0))
        )
        dkraw_ref[n : n + HS, span(h)] = jnp.where(ctx == 0, p_ref[h] + dot(d_ref[h], end, TN, 3), 0.0)
        w = w_ref[h]
        k = k_ref[:, span(h)]
        r = r_ref[:, span(h)]
        boost, e = rates_of(base_ref, gate_ref, h)
        x = x_ref[:, span(h)] + dot(bt_ref[h], end, TN, 3)
        dv_ref[:, span(h)] = x.astype(BF).astype(F32)
        d_low = jnp.where(strict, -dot(x, r, NT, 3), 0.0)
        d_gram = d_low * e
        dk = (
            dk_ref[:, span(h)]
            - dot(x, w, NT, 3)
            + to_col(e) * dot(r, end, NT, 3)
            + dot(d_gram + d_gram.T, k, NN, 3)
        )
        pull = to_row(jnp.sum(r * dot(k, end, NN, 3), axis=1, keepdims=True))
        de = de_ref[h : h + 1, :] + jnp.sum(d_low * gram_ref[h], axis=0, keepdims=True) + pull
        draw = ninv_ref[h] * (dk - k * jnp.sum(k * dk, -1, keepdims=True))
        dkraw_ref[0:n, span(h)] = draw.astype(BF).astype(F32)
        d_boost = de / ((1.0 + boost) * (1.0 + boost))
        gates_ref[0, h : h + 1, :] = d_boost * base_ref[h]
        dkraw_ref[n + HS : n + HS + 1, span(h)] = dgain_ref[h : h + 1, :]
        dkraw_ref[n + HS + 1 : n + HS + 2, span(h)] = jnp.broadcast_to(
            jnp.sum(d_boost * gate_ref[0, h : h + 1, :], axis=1, keepdims=True), (1, HS)
        )


def turn_kernel(own_ref, other_ref, out_ref):
    n = own_ref.shape[0]
    out_ref[:, 0:n] = own_ref[...].T.astype(BF)
    out_ref[:, n : 2 * n] = other_ref[...].T.astype(BF)


def product_kernel(pos_ref, tokt_ref, own_ref, other_ref, *out_refs):
    n = tokt_ref.shape[1] // 2
    d = jnp.concatenate([own_ref[0:n, :], other_ref[0:n, :]], axis=0).astype(BF)
    for turn, out_ref in zip(TURNS, out_refs):
        at = (pos_ref[1] + turn) & (RING - 1)
        rows = pl.ds(pl.multiple_of(at * CHUNK, CHUNK), CHUNK)
        out_ref[0:CHUNK, :] = jnp.dot(tokt_ref[rows, :], d, preferred_element_type=F32)
        if own_ref.shape[0] > n:
            extra = pl.ds(pl.multiple_of(n + (pos_ref[0] * RING + at) * PIECE, 8), PIECE)
            out_ref[CHUNK : CHUNK + PIECE, :] = own_ref[extra, :] + other_ref[extra, :]


def token_kernel(pos_ref, w_ref, dq_ref, dk_ref, dv_ref, *out_refs):
    n = dq_ref.shape[0]
    ds = [dq_ref[...].astype(BF), dk_ref[0:n, :].astype(BF), dv_ref[...].astype(BF)]
    span_rows = w_ref.shape[1] // RING
    for turn, out_ref in zip(TURNS, out_refs):
        at = (pos_ref[3] + turn) & (RING - 1)
        rows = pl.ds(pl.multiple_of(at * span_rows, span_rows), span_rows)
        total = lax.dot_general(ds[0], w_ref[0, rows, :], NT, preferred_element_type=F32)
        total = total + lax.dot_general(ds[1], w_ref[1, rows, :], NT, preferred_element_type=F32)
        out_ref[...] = total + lax.dot_general(ds[2], w_ref[2, rows, :], NT, preferred_element_type=F32)


def place_kernel(pos_ref, *refs):
    pieces = [refs[8 * s : 8 * s + 8] for s in range(3)]
    out_ref, init_ref, gain_ref, rates_ref, extra_ref, sem, extra_sem = refs[24:]
    copies = []
    for s in range(3):
        for m in range(8):
            half, turn = m // RING, TURNS[m % RING]
            core = pos_ref[0] if half == 0 else 1 - pos_ref[0]
            at = core * RING + ((pos_ref[1 + half] + turn) & (RING - 1))
            rows = pl.ds(pl.multiple_of(at * CHUNK, CHUNK), CHUNK)
            copies.append(
                pltpu.make_async_copy(pieces[s][m].at[pl.ds(0, CHUNK), :], out_ref.at[s, rows, :], sem.at[s, m])
            )
            if s == 1:
                rows = pl.ds(pl.multiple_of(at * PIECE, 8), PIECE)
                copies.append(
                    pltpu.make_async_copy(
                        pieces[s][m].at[pl.ds(CHUNK, PIECE), :], extra_ref.at[rows, :], extra_sem.at[m]
                    )
                )
    for copy in copies:
        copy.start()
    for copy in copies:
        copy.wait()
    for h in range(init_ref.shape[0]):
        init_ref[h] = extra_ref[0:HS, span(h)]
        gain_ref[h : h + 1, :] = extra_ref[HS : HS + 1, span(h)]
        rates_ref[h : h + 1, :] = extra_ref[HS + 1 : HS + 2, span(h)]


def moves(first, by):
    pairs = []
    for x in range(RING):
        for core in range(2):
            for y in range(RING):
                along_x = (core == 0) == first
                to_x = (x + by) % RING if along_x else x
                to_y = y if along_x else (y + by) % RING
                pairs.append(((x * 2 + core) * RING + y, (to_x * 2 + core) * RING + to_y))
    return pairs


def round_turn(chunks, first):
    return [
        lax.ppermute(chunk, ("dp", "ctx"), moves(first, turn)) for chunk, turn in zip(chunks, TURNS[1:])
    ]


def swap(value):
    return lax.ppermute(value, "dp", [(i, i ^ 1) for i in range(2 * RING)])


def reduce_stream(pos, tokt, d):
    other = swap(d)
    rows = CHUNK + (PIECE if d.shape[0] > CHUNK else 0)
    piece = shape(rows, d.shape[1])
    own, *away = whole(product_kernel, (piece,) * RING, [SM] + [VM] * 3)(pos, tokt, d, other)
    from_back, from_ahead, from_far = round_turn(away, True)
    part_sum = (own + from_far) + (from_back + from_ahead)
    from_back, from_ahead, from_far = round_turn([part_sum] * 3, False)
    total = (part_sum + from_far) + (from_back + from_ahead)
    from_back, from_ahead, from_far = round_turn([total] * 3, True)
    mine = [total, from_ahead, from_back, from_far]
    return mine + [swap(piece) for piece in mine]


VM = pl.BlockSpec(memory_space=pltpu.VMEM)
SM = pl.BlockSpec(memory_space=pltpu.SMEM)
PARAMS = pltpu.CompilerParams(vmem_limit_bytes=32 * 1024 * 1024)


def shape(*dims, dtype=F32):
    return jax.ShapeDtypeStruct(dims, dtype)


def whole(kernel, outs, specs):
    return pl.pallas_call(
        kernel,
        out_shape=outs,
        in_specs=specs,
        out_specs=jax.tree.map(lambda _: VM, outs),
        compiler_params=PARAMS,
    )


def part(which, dims):
    return pl.BlockSpec((1,) + dims, lambda i: (which, 0, 0))


def full(*dims):
    return pl.BlockSpec(dims, lambda i: (0,) * len(dims))


def body(tokens, proj_weights, init_weight, base_rates, gate_values, out_gain, cotangent):
    n = tokens.shape[1]
    model = tokens.shape[2]
    heads = init_weight.shape[0]
    wide = heads * HS
    ctx = lax.axis_index("ctx")
    ctx_arr = ctx.astype(jnp.int32).reshape(1)
    dp = lax.axis_index("dp")
    core, x_at = dp % 2, dp // 2
    pos = jnp.stack(
        [core, jnp.where(core == 0, x_at, ctx), jnp.where(core == 0, ctx, x_at), lax.axis_index("head")]
    ).astype(jnp.int32)
    half = model // 2
    own_half = lax.dynamic_slice_in_dim(tokens[0], core * half, half, 1).astype(F32)
    other_half = lax.dynamic_slice_in_dim(tokens[0], (1 - core) * half, half, 1).astype(F32)
    got_half = swap(other_half)

    wide_f32 = shape(n, wide)
    square = shape(heads, n, n)
    small = shape(heads, HS, HS)
    wspec = functools.partial(part, dims=(model, wide))

    k, v, ninv, gram, inv, bt, decay, send, offset = pl.pallas_call(
        maps_kernel,
        grid=(1,),
        out_shape=(wide_f32, wide_f32, shape(heads, n, HS), square, square, shape(heads, HS, n), small, small, small),
        in_specs=[SM, SM, full(1, n, model), wspec(1), wspec(2), full(1, heads, n), full(heads, HS, HS)],
        out_specs=(
            full(n, wide), full(n, wide), full(heads, n, HS), full(heads, n, n), full(heads, n, n),
            full(heads, HS, n), full(heads, HS, HS), full(heads, HS, HS), full(heads, HS, HS),
        ),
        compiler_params=PARAMS,
    )(ctx_arr, base_rates, tokens, proj_weights, proj_weights, gate_values, init_weight)

    near = lax.ppermute(send, "ctx", [(0, 1), (2, 3)])
    moved = lax.ppermute(decay, "ctx", [(2, 3), (1, 0)])

    q, score, rv, y, qt, zv = pl.pallas_call(
        reach_kernel,
        grid=(1,),
        out_shape=(wide_f32, square, wide_f32, wide_f32, wide_f32, wide_f32),
        in_specs=[SM, full(1, n, model), wspec(0), full(1, heads, n), full(n, wide), full(n, wide), full(heads, n, n)],
        out_specs=(full(n, wide), full(heads, n, n), full(n, wide), full(n, wide), full(n, wide), full(n, wide)),
        compiler_params=PARAMS,
    )(base_rates, tokens, proj_weights, gate_values, k, v, inv)

    second = whole(functools.partial(step_kernel, transposed=False), small, [VM] * 3)(decay, near, offset)
    mid = lax.ppermute(second, "ctx", [(1, 2)])
    far = lax.ppermute(second, "ctx", [(1, 3)])

    w, back, pulled, dgain = whole(
        norm_kernel, (small, wide_f32, small, shape(heads, HS)), [SM] + [VM] * 9
    )(ctx_arr, init_weight, near, mid, far, moved, qt, zv, cotangent, out_gain)

    back_near = lax.ppermute(pulled, "ctx", [(3, 2), (1, 0)])

    dq, r, x, dk, de = whole(
        query_kernel,
        (wide_f32, wide_f32, wide_f32, wide_f32, shape(heads, n)),
        [SM] + [VM] * 10,
    )(base_rates, gate_values, w, back, cotangent, q, score, rv, y, k, inv)

    back_second = whole(functools.partial(step_kernel, transposed=True), small, [VM] * 3)(decay, back_near, pulled)
    back_mid = lax.ppermute(back_second, "ctx", [(2, 1)])
    back_far = lax.ppermute(back_second, "ctx", [(2, 0)])

    dkraw, dv, grad_gates = whole(
        keys_kernel,
        (shape(n + EXTRA, wide), wide_f32, shape(1, heads, n)),
        [SM, SM] + [VM] * 17,
    )(ctx_arr, base_rates, gate_values, back_near, back_mid, back_far, moved, pulled, decay, w, k, ninv, gram, bt, r, x,
      dk, de, dgain)

    tokt = whole(turn_kernel, shape(half, 2 * n, dtype=BF), [VM] * 2)(own_half, got_half)
    query_pieces = reduce_stream(pos, tokt, dq)
    value_pieces = reduce_stream(pos, tokt, dv)
    key_pieces = reduce_stream(pos, tokt, dkraw)

    quarter = shape(n, model // RING)
    own, *away = whole(token_kernel, (quarter,) * RING, [SM] + [VM] * 4)(pos, proj_weights, dq, dkraw, dv)
    from_back, from_ahead, from_far = [
        lax.ppermute(chunk, "head", [(i, (i + turn) % RING) for i in range(RING)])
        for chunk, turn in zip(away, TURNS[1:])
    ]
    grad_tokens = ((own + from_far) + (from_back + from_ahead)).astype(BF).reshape(1, n, -1)

    anywhere = pl.BlockSpec(memory_space=pl.ANY)
    grad_proj, grad_init, grad_gain, rates = pl.pallas_call(
        place_kernel,
        out_shape=(shape(3, model, wide), small, shape(heads, HS), shape(heads, HS)),
        in_specs=[SM] + [anywhere] * 24,
        out_specs=(anywhere, VM, VM, VM),
        scratch_shapes=[
            pltpu.VMEM((EXTRA, wide), F32), pltpu.SemaphoreType.DMA((3, 8)), pltpu.SemaphoreType.DMA((8,))
        ],
        compiler_params=PARAMS,
    )(pos, *query_pieces, *key_pieces, *value_pieces)
    return (grad_tokens, grad_proj, grad_init, grad_gain, rates[:, 0], grad_gates)


def solution(mesh):
    in_specs = (
        P("dp", "ctx", None),
        P(None, None, "head"),
        P("head", None, None),
        P("head"),
        P("dp", "head", "ctx"),
        P("head", None),
        P("dp", "ctx", "head"),
    )
    out_specs = (
        P("dp", "ctx", "head"),
        P(None, None, "head"),
        P("head", None, None),
        P("head", None),
        P("head"),
        P("dp", "head", "ctx"),
    )
    return jax.shard_map(body, mesh=mesh, in_specs=in_specs, out_specs=out_specs, check_vma=False)
```

```python
import functools

import jax
import jax.numpy as jnp
from jax import lax
from jax.experimental import pallas as pl
from jax.experimental.pallas import tpu as pltpu
from jax.sharding import PartitionSpec as P

MB = 16
HS = 128
RING = 4
TURNS = (0, 1, 3, 2)
CHUNK = 256
PIECE = 24
EXTRA = 2 * RING * PIECE
F32 = jnp.float32
BF = jnp.bfloat16
NN = (((1,), (0,)), ((), ()))
NT = (((1,), (1,)), ((), ()))
TN = (((0,), (0,)), ((), ()))


def dot(a, b, dims, passes):
    ah = a.astype(BF)
    bh = b.astype(BF)
    result = lax.dot_general(ah, bh, dims, preferred_element_type=F32)
    if passes == 3:
        al = (a - ah.astype(F32)).astype(BF)
        bl = (b - bh.astype(F32)).astype(BF)
        result = result + (
            lax.dot_general(ah, bl, dims, preferred_element_type=F32)
            + lax.dot_general(al, bh, dims, preferred_element_type=F32)
        )
    return result


def places(n):
    return (
        lax.broadcasted_iota(jnp.int32, (n, n), 0),
        lax.broadcasted_iota(jnp.int32, (n, n), 1),
    )


def to_col(row):
    i, j = places(row.shape[1])
    return jnp.sum(jnp.where(i == j, row, 0.0), axis=1, keepdims=True)


def to_row(col):
    i, j = places(col.shape[0])
    return jnp.sum(jnp.where(i == j, col, 0.0), axis=0, keepdims=True)


def unit_lower_inverses(lowers):
    n = lowers[0].shape[0]
    i, j = places(n)
    size = 2 * MB
    same = (i // size) == (j // size)
    inverses = [jnp.where(i == j, 1.0, 0.0) - jnp.where(same, low, 0.0) for low in lowers]
    while size < n:
        pair = ((i // (2 * size)) == (j // (2 * size))) & ((i // size) != (j // size))
        corners = [jnp.where(pair, low, 0.0) for low in lowers]
        halves = [dot(inv, corner, NN, 3) for inv, corner in zip(inverses, corners)]
        inverses = [inv - dot(half, inv, NN, 3) for inv, half in zip(inverses, halves)]
        size *= 2
    return inverses


def span(h):
    return slice(h * HS, (h + 1) * HS)


def rates_of(base_ref, gate_ref, h):
    boost = base_ref[h] * gate_ref[0, h : h + 1, :]
    return boost, boost / (1.0 + boost)


def maps_kernel(
    pos_ref, base_ref, tok_ref, wk_ref, wv_ref, gate_ref, init_ref,
    k_ref, v_ref, ninv_ref, gram_ref, inv_ref, bt_ref, d_ref, send_ref, o_ref, half_ref,
):
    half = tok_ref.shape[2] // 2
    columns = pl.ds(pl.multiple_of((1 - pos_ref[0]) * half, half), half)
    half_ref[...] = tok_ref[0, :, columns].astype(F32)
    tok = tok_ref[0]
    kraw_all = jnp.dot(tok, wk_ref[0], preferred_element_type=F32).astype(BF).astype(F32)
    v_all = jnp.dot(tok, wv_ref[0], preferred_element_type=F32).astype(BF).astype(F32)
    n = kraw_all.shape[0]
    i, j = places(n)
    strict = (i // MB) > (j // MB)
    heads = range(init_ref.shape[0])
    ks, kts, es, lows = [], [], [], []
    for h in heads:
        kraw = kraw_all[:, span(h)]
        ninv = lax.rsqrt(jnp.sum(kraw * kraw, -1, keepdims=True) + 1e-06)
        k = kraw * ninv
        kt = k.T
        _, e = rates_of(base_ref, gate_ref, h)
        gram = dot(k, kt, NN, 3)
        ninv_ref[h] = jnp.broadcast_to(ninv, (n, HS))
        k_ref[:, span(h)] = k
        gram_ref[h] = gram
        ks.append(k)
        kts.append(kt)
        es.append(e)
        lows.append(jnp.where(strict, gram * e, 0.0))
    v_ref[...] = v_all
    inverses = unit_lower_inverses(lows)
    a, b = places(HS)
    for h in heads:
        bt = dot(kts[h] * es[h], inverses[h], NN, 3)
        inv_ref[h] = inverses[h]
        bt_ref[h] = bt
        decay = jnp.where(a == b, 1.0, 0.0) - dot(bt, ks[h], NN, 3)
        offset = dot(bt, v_all[:, span(h)], NN, 3)
        d_ref[h] = decay
        o_ref[h] = offset
        first = dot(decay, init_ref[h], NN, 3) + offset
        send_ref[h] = jnp.where(pos_ref[4] == 0, first, offset)


def reach_kernel(
    pos_ref, base_ref, tok_ref, wq_ref, gate_ref, k_ref, v_ref, inv_ref,
    q_ref, score_ref, rv_ref, y_ref, qt_ref, zv_ref, tokt_ref,
):
    half = tok_ref.shape[2] // 2
    columns = pl.ds(pl.multiple_of(pos_ref[0] * half, half), half)
    tokt_ref[...] = tok_ref[0, :, columns].astype(F32).T.astype(BF)
    q_all = jnp.dot(tok_ref[0], wq_ref[0], preferred_element_type=F32).astype(BF).astype(F32)
    n = q_all.shape[0]
    i, j = places(n)
    q_ref[...] = q_all
    for h in range(inv_ref.shape[0]):
        q = q_all[:, span(h)]
        k = k_ref[:, span(h)]
        _, e = rates_of(base_ref, gate_ref, h)
        score = dot(q, k, NT, 3)
        mix = jnp.where(i >= j, score * e, 0.0)
        inv = inv_ref[h]
        rv = dot(inv, v_ref[:, span(h)], NN, 3)
        y = dot(inv, k, NN, 3)
        score_ref[h] = score
        rv_ref[:, span(h)] = rv
        y_ref[:, span(h)] = y
        qt_ref[:, span(h)] = q - dot(mix, y, NN, 3)
        zv_ref[:, span(h)] = dot(mix, rv, NN, 3)


def step_kernel(d_ref, w_ref, o_ref, after_ref, out_ref, *, transposed):
    del after_ref
    for h in range(d_ref.shape[0]):
        out_ref[h] = o_ref[h] + dot(d_ref[h], w_ref[h], TN if transposed else NN, 3)


def norm_kernel(
    pos_ref, init_ref, near_ref, mid_ref, far_ref, rd_ref, qt_ref, zv_ref, up_ref, gain_ref, after_ref,
    w_ref, h_ref, p_ref, dgain_ref,
):
    del after_ref
    ctx = pos_ref[4]
    for h in range(init_ref.shape[0]):
        last = dot(rd_ref[h], far_ref[h], NN, 3) + near_ref[h]
        start = jnp.where(
            ctx == 0, init_ref[h], jnp.where(ctx == 1, near_ref[h], jnp.where(ctx == 2, mid_ref[h], last))
        )
        w_ref[h] = start
        qt = qt_ref[:, span(h)]
        z = dot(qt, start, NN, 3) + zv_ref[:, span(h)]
        up = up_ref[0, :, span(h)].astype(F32)
        centred = z - jnp.mean(z, -1, keepdims=True)
        inv_std = lax.rsqrt(jnp.mean(centred * centred, -1, keepdims=True) + 1e-05)
        normed = centred * inv_std
        weighted = up * gain_ref[h : h + 1, :]
        back = inv_std * (
            weighted
            - jnp.mean(weighted, -1, keepdims=True)
            - normed * jnp.mean(weighted * normed, -1, keepdims=True)
        )
        h_ref[:, span(h)] = back
        p_ref[h] = dot(qt, back, TN, 3)
        dgain_ref[h : h + 1, :] = jnp.sum(up * normed, axis=0, keepdims=True)


def query_kernel(
    base_ref, gate_ref, w_ref, h_ref, up_ref, q_ref, score_ref, rv_ref, y_ref, k_ref, inv_ref,
    dq_ref, r_ref, x_ref, dk_ref, de_ref,
):
    n = h_ref.shape[0]
    i, j = places(n)
    for h in range(w_ref.shape[0]):
        w = w_ref[h]
        back = h_ref[:, span(h)]
        k = k_ref[:, span(h)]
        q = q_ref[:, span(h)]
        score = score_ref[h]
        _, e = rates_of(base_ref, gate_ref, h)
        mix = jnp.where(i >= j, score * e, 0.0)
        r = rv_ref[:, span(h)] - dot(y_ref[:, span(h)], w, NN, 3)
        r_ref[:, span(h)] = r
        d_mix = jnp.where(i >= j, dot(back, r, NT, 3), 0.0)
        d_score = d_mix * e
        dq = up_ref[0, :, span(h)].astype(F32) + dot(back, w, NT, 3) + dot(d_score, k, NN, 3)
        dq_ref[:, span(h)] = dq.astype(BF).astype(F32)
        x_ref[:, span(h)] = dot(inv_ref[h], dot(mix, back, TN, 3), TN, 3)
        dk_ref[:, span(h)] = dot(d_score, q, TN, 3)
        de_ref[h : h + 1, :] = jnp.sum(d_mix * score, axis=0, keepdims=True)


def keys_kernel(
    pos_ref, base_ref, gate_ref, rp_ref, mid_ref, far_ref, rd_ref, p_ref, d_ref, w_ref, k_ref, ninv_ref,
    gram_ref, bt_ref, r_ref, x_ref, dk_ref, de_ref, dgain_ref, after_ref,
    both_ref, gates_ref,
):
    del after_ref
    ctx = pos_ref[4]
    n = k_ref.shape[0]
    i, j = places(n)
    strict = (i // MB) > (j // MB)
    both_ref[2 * n + HS : 2 * n + EXTRA, :] = jnp.zeros((EXTRA - HS, both_ref.shape[1]), F32)
    for h in range(w_ref.shape[0]):
        first = rp_ref[h] + dot(rd_ref[h], far_ref[h], TN, 3)
        end = jnp.where(
            ctx == 0, first, jnp.where(ctx == 1, mid_ref[h], jnp.where(ctx == 2, rp_ref[h], 0.0))
        )
        both_ref[2 * n : 2 * n + HS, span(h)] = jnp.where(ctx == 0, p_ref[h] + dot(d_ref[h], end, TN, 3), 0.0)
        w = w_ref[h]
        k = k_ref[:, span(h)]
        r = r_ref[:, span(h)]
        boost, e = rates_of(base_ref, gate_ref, h)
        x = x_ref[:, span(h)] + dot(bt_ref[h], end, TN, 3)
        both_ref[n : 2 * n, span(h)] = x.astype(BF).astype(F32)
        d_low = jnp.where(strict, -dot(x, r, NT, 3), 0.0)
        d_gram = d_low * e
        dk = (
            dk_ref[:, span(h)]
            - dot(x, w, NT, 3)
            + to_col(e) * dot(r, end, NT, 3)
            + dot(d_gram + d_gram.T, k, NN, 3)
        )
        pull = to_row(jnp.sum(r * dot(k, end, NN, 3), axis=1, keepdims=True))
        de = de_ref[h : h + 1, :] + jnp.sum(d_low * gram_ref[h], axis=0, keepdims=True) + pull
        draw = ninv_ref[h] * (dk - k * jnp.sum(k * dk, -1, keepdims=True))
        both_ref[0:n, span(h)] = draw.astype(BF).astype(F32)
        d_boost = de / ((1.0 + boost) * (1.0 + boost))
        gates_ref[0, h : h + 1, :] = d_boost * base_ref[h]
        both_ref[2 * n + HS : 2 * n + HS + 1, span(h)] = dgain_ref[h : h + 1, :]
        both_ref[2 * n + HS + 1 : 2 * n + HS + 2, span(h)] = jnp.broadcast_to(
            jnp.sum(d_boost * gate_ref[0, h : h + 1, :], axis=1, keepdims=True), (1, HS)
        )


def turn_kernel(other_ref, out_ref):
    out_ref[...] = other_ref[...].T.astype(BF)


def product_kernel(pos_ref, tokt_ref, other_tokt_ref, own_ref, other_ref, *out_refs):
    n = tokt_ref.shape[1]
    count = own_ref.shape[0] // n
    if count > 1:
        count = (own_ref.shape[0] - EXTRA) // n
    for turn, out_ref in zip(TURNS, out_refs):
        at = (pos_ref[1] + turn) & (RING - 1)
        rows = pl.ds(pl.multiple_of(at * CHUNK, CHUNK), CHUNK)
        for m in range(count):
            out_ref[m * CHUNK : (m + 1) * CHUNK, :] = jnp.dot(
                tokt_ref[rows, :], own_ref[m * n : (m + 1) * n, :].astype(BF), preferred_element_type=F32
            ) + jnp.dot(
                other_tokt_ref[rows, :], other_ref[m * n : (m + 1) * n, :].astype(BF), preferred_element_type=F32
            )
        if count > 1:
            extra = pl.ds(pl.multiple_of(count * n + (pos_ref[0] * RING + at) * PIECE, 8), PIECE)
            out_ref[count * CHUNK : count * CHUNK + PIECE, :] = own_ref[extra, :] + other_ref[extra, :]


def token_kernel(pos_ref, w_ref, dq_ref, both_ref, *out_refs):
    n = dq_ref.shape[0]
    ds = [dq_ref[...].astype(BF), both_ref[0:n, :].astype(BF), both_ref[n : 2 * n, :].astype(BF)]
    span_rows = w_ref.shape[1] // RING
    for turn, out_ref in zip(TURNS, out_refs):
        at = (pos_ref[3] + turn) & (RING - 1)
        rows = pl.ds(pl.multiple_of(at * span_rows, span_rows), span_rows)
        total = lax.dot_general(ds[0], w_ref[0, rows, :], NT, preferred_element_type=F32)
        total = total + lax.dot_general(ds[1], w_ref[1, rows, :], NT, preferred_element_type=F32)
        out_ref[...] = total + lax.dot_general(ds[2], w_ref[2, rows, :], NT, preferred_element_type=F32)


def place_kernel(pos_ref, *refs):
    out_ref, init_ref, gain_ref, rates_ref, extra_ref, sem, extra_sem = refs[16:]
    copies = []
    for m in range(8):
        half, turn = m // RING, TURNS[m % RING]
        core = pos_ref[0] if half == 0 else 1 - pos_ref[0]
        at = core * RING + ((pos_ref[1 + half] + turn) & (RING - 1))
        rows = pl.ds(pl.multiple_of(at * CHUNK, CHUNK), CHUNK)
        for s in range(3):
            piece = refs[m] if s == 0 else refs[8 + m]
            start = 0 if s == 0 else (s - 1) * CHUNK
            copies.append(
                pltpu.make_async_copy(piece.at[pl.ds(start, CHUNK), :], out_ref.at[s, rows, :], sem.at[s, m])
            )
        rows = pl.ds(pl.multiple_of(at * PIECE, 8), PIECE)
        copies.append(
            pltpu.make_async_copy(
                refs[8 + m].at[pl.ds(2 * CHUNK, PIECE), :], extra_ref.at[rows, :], extra_sem.at[m]
            )
        )
    for copy in copies:
        copy.start()
    for copy in copies:
        copy.wait()
    for h in range(init_ref.shape[0]):
        init_ref[h] = extra_ref[0:HS, span(h)]
        gain_ref[h : h + 1, :] = extra_ref[HS : HS + 1, span(h)]
        rates_ref[h : h + 1, :] = extra_ref[HS + 1 : HS + 2, span(h)]


def moves(first, by):
    pairs = []
    for x in range(RING):
        for core in range(2):
            for y in range(RING):
                along_x = (core == 0) == first
                to_x = (x + by) % RING if along_x else x
                to_y = y if along_x else (y + by) % RING
                pairs.append(((x * 2 + core) * RING + y, (to_x * 2 + core) * RING + to_y))
    return pairs


def round_turn(chunks, first):
    return [
        lax.ppermute(chunk, ("dp", "ctx"), moves(first, turn)) for chunk, turn in zip(chunks, TURNS[1:])
    ]


def swap(value):
    return lax.ppermute(value, "dp", [(i, i ^ 1) for i in range(2 * RING)])


def reduce_products(pos, tokt, other_tokt, d):
    other = swap(d)
    rows = d.shape[0] if d.shape[0] == CHUNK else 2 * CHUNK + PIECE
    return whole(product_kernel, (vmem(rows, d.shape[1]),) * RING, [SM] + [VM] * 4)(
        pos, tokt, other_tokt, d, other
    )


def reduce_stream(products):
    own, *away = products
    from_back, from_ahead, from_far = round_turn(away, True)
    part_sum = (own + from_far) + (from_back + from_ahead)
    from_back, from_ahead, from_far = round_turn([part_sum] * 3, False)
    total = (part_sum + from_far) + (from_back + from_ahead)
    from_back, from_ahead, from_far = round_turn([total] * 3, True)
    mine = [total, from_ahead, from_back, from_far]
    return mine + [swap(piece) for piece in mine]


VM = pl.BlockSpec(memory_space=pltpu.VMEM)
SM = pl.BlockSpec(memory_space=pltpu.SMEM)
PARAMS = pltpu.CompilerParams(vmem_limit_bytes=20 * 1024 * 1024)


def shape(*dims, dtype=F32):
    return jax.ShapeDtypeStruct(dims, dtype)


def vmem(*dims, dtype=F32):
    return pltpu.VMEM(dims, dtype)


def hbm(value):
    return pltpu.with_memory_space_constraint(value, pltpu.HBM)


def whole(kernel, outs, specs):
    return pl.pallas_call(
        kernel,
        out_shape=outs,
        in_specs=specs,
        out_specs=tuple(VM for _ in outs) if isinstance(outs, tuple) else VM,
        compiler_params=PARAMS,
    )


def part(which, dims):
    return pl.BlockSpec((1,) + dims, lambda i: (which, 0, 0))


def full(*dims):
    return pl.BlockSpec(dims, lambda i: (0,) * len(dims))


def body(tokens, proj_weights, init_weight, base_rates, gate_values, out_gain, cotangent):
    n = tokens.shape[1]
    model = tokens.shape[2]
    heads = init_weight.shape[0]
    wide = heads * HS
    ctx = lax.axis_index("ctx")
    dp = lax.axis_index("dp")
    core, x_at = dp % 2, dp // 2
    pos = jnp.stack(
        [core, jnp.where(core == 0, x_at, ctx), jnp.where(core == 0, ctx, x_at), lax.axis_index("head"), ctx]
    ).astype(jnp.int32)
    half = model // 2

    wide_f32 = vmem(n, wide)
    square = vmem(heads, n, n)
    small = vmem(heads, HS, HS)
    wspec = functools.partial(part, dims=(model, wide))
    tokens = hbm(tokens)
    proj_weights = hbm(proj_weights)
    anywhere = pl.BlockSpec(memory_space=pl.ANY)

    k, v, ninv, gram, inv, bt, decay, send, offset, other_half = pl.pallas_call(
        maps_kernel,
        grid=(1,),
        out_shape=(
            wide_f32, wide_f32, vmem(heads, n, HS), square, square, vmem(heads, HS, n), small, small, small,
            vmem(n, half),
        ),
        in_specs=[SM, SM, full(1, n, model), wspec(1), wspec(2), full(1, heads, n), full(heads, HS, HS)],
        out_specs=(VM,) * 10,
        compiler_params=PARAMS,
    )(pos, hbm(base_rates), tokens, proj_weights, proj_weights, hbm(gate_values), hbm(init_weight))

    near = lax.ppermute(send, "ctx", [(0, 1), (2, 3)])
    moved = lax.ppermute(decay, "ctx", [(2, 3), (1, 0)])
    got_half = swap(other_half)

    q, score, rv, y, qt, zv, tokt = pl.pallas_call(
        reach_kernel,
        grid=(1,),
        out_shape=(wide_f32, square, wide_f32, wide_f32, wide_f32, wide_f32, vmem(half, n, dtype=BF)),
        in_specs=[SM, SM, full(1, n, model), wspec(0), full(1, heads, n), VM, VM, VM],
        out_specs=(VM,) * 7,
        compiler_params=PARAMS,
    )(pos, base_rates, tokens, proj_weights, gate_values, k, v, inv)

    second = whole(functools.partial(step_kernel, transposed=False), small, [VM] * 3 + [anywhere])(
        decay, near, offset, qt
    )
    mid = lax.ppermute(second, "ctx", [(1, 2)])
    far = lax.ppermute(second, "ctx", [(1, 3)])
    other_tokt = whole(turn_kernel, vmem(half, n, dtype=BF), [VM])(got_half)

    w, back, pulled, dgain = whole(
        norm_kernel, (small, wide_f32, small, vmem(heads, HS)), [SM] + [VM] * 9 + [anywhere]
    )(pos, init_weight, near, mid, far, moved, qt, zv, cotangent, out_gain, other_tokt)

    back_near = lax.ppermute(pulled, "ctx", [(3, 2), (1, 0)])

    dq, r, x, dk, de = whole(
        query_kernel, (wide_f32, wide_f32, wide_f32, wide_f32, vmem(heads, n)), [SM] + [VM] * 10
    )(base_rates, gate_values, w, back, cotangent, q, score, rv, y, k, inv)

    back_second = whole(functools.partial(step_kernel, transposed=True), small, [VM] * 3 + [anywhere])(
        decay, back_near, pulled, de
    )
    back_mid = lax.ppermute(back_second, "ctx", [(2, 1)])
    back_far = lax.ppermute(back_second, "ctx", [(2, 0)])
    query_products = reduce_products(pos, tokt, other_tokt, dq)

    both, grad_gates = whole(
        keys_kernel, (vmem(2 * n + EXTRA, wide), shape(1, heads, n)), [SM, SM] + [VM] * 17 + [anywhere]
    )(pos, base_rates, gate_values, back_near, back_mid, back_far, moved, pulled, decay, w, k, ninv, gram, bt, r, x,
      dk, de, dgain, query_products[0])

    both_products = reduce_products(pos, tokt, other_tokt, both)
    query_pieces = reduce_stream(query_products)
    both_pieces = reduce_stream(both_products)

    quarter = vmem(n, model // RING)
    own, *away = pl.pallas_call(
        token_kernel,
        grid=(1,),
        out_shape=(quarter,) * RING,
        in_specs=[SM, full(3, model, wide), VM, VM],
        out_specs=(VM,) * RING,
        compiler_params=PARAMS,
    )(pos, proj_weights, dq, both)
    from_back, from_ahead, from_far = [
        lax.ppermute(chunk, "head", [(i, (i + turn) % RING) for i in range(RING)])
        for chunk, turn in zip(away, TURNS[1:])
    ]
    grad_tokens = ((own + from_far) + (from_back + from_ahead)).astype(BF).reshape(1, n, -1)

    grad_proj, grad_init, grad_gain, rates = pl.pallas_call(
        place_kernel,
        out_shape=(shape(3, model, wide), shape(heads, HS, HS), shape(heads, HS), shape(heads, HS)),
        in_specs=[SM] + [anywhere] * 16,
        out_specs=(anywhere, VM, VM, VM),
        scratch_shapes=[
            pltpu.VMEM((EXTRA, wide), F32), pltpu.SemaphoreType.DMA((3, 8)), pltpu.SemaphoreType.DMA((8,))
        ],
        compiler_params=PARAMS,
    )(pos, *query_pieces, *both_pieces)
    return (grad_tokens, grad_proj, grad_init, grad_gain, rates[:, 0], grad_gates)


def solution(mesh):
    in_specs = (
        P("dp", "ctx", None),
        P(None, None, "head"),
        P("head", None, None),
        P("head"),
        P("dp", "head", "ctx"),
        P("head", None),
        P("dp", "ctx", "head"),
    )
    out_specs = (
        P("dp", "ctx", "head"),
        P(None, None, "head"),
        P("head", None, None),
        P("head", None),
        P("head"),
        P("dp", "head", "ctx"),
    )
    return jax.shard_map(body, mesh=mesh, in_specs=in_specs, out_specs=out_specs, check_vma=False)
```

```python
import functools

import jax
import jax.numpy as jnp
from jax import lax
from jax.experimental import pallas as pl
from jax.experimental.pallas import tpu as pltpu
from jax.sharding import PartitionSpec as P

MB = 16
HS = 128
RING = 4
TURNS = (0, 1, 3, 2)
CHUNK = 256
PIECE = 24
EXTRA = 2 * RING * PIECE
F32 = jnp.float32
BF = jnp.bfloat16
NN = (((1,), (0,)), ((), ()))
NT = (((1,), (1,)), ((), ()))
TN = (((0,), (0,)), ((), ()))


def dot(a, b, dims, passes):
    ah = a.astype(BF)
    bh = b.astype(BF)
    result = lax.dot_general(ah, bh, dims, preferred_element_type=F32)
    if passes == 3:
        al = (a - ah.astype(F32)).astype(BF)
        bl = (b - bh.astype(F32)).astype(BF)
        result = result + (
            lax.dot_general(ah, bl, dims, preferred_element_type=F32)
            + lax.dot_general(al, bh, dims, preferred_element_type=F32)
        )
    return result


def places(n):
    return (
        lax.broadcasted_iota(jnp.int32, (n, n), 0),
        lax.broadcasted_iota(jnp.int32, (n, n), 1),
    )


def to_col(row):
    i, j = places(row.shape[1])
    return jnp.sum(jnp.where(i == j, row, 0.0), axis=1, keepdims=True)


def to_row(col):
    i, j = places(col.shape[0])
    return jnp.sum(jnp.where(i == j, col, 0.0), axis=0, keepdims=True)


def unit_lower_inverses(lowers):
    n = lowers[0].shape[0]
    i, j = places(n)
    size = 2 * MB
    same = (i // size) == (j // size)
    inverses = [jnp.where(i == j, 1.0, 0.0) - jnp.where(same, low, 0.0) for low in lowers]
    while size < n:
        pair = ((i // (2 * size)) == (j // (2 * size))) & ((i // size) != (j // size))
        corners = [jnp.where(pair, low, 0.0) for low in lowers]
        halves = [dot(inv, corner, NN, 3) for inv, corner in zip(inverses, corners)]
        inverses = [inv - dot(half, inv, NN, 3) for inv, half in zip(inverses, halves)]
        size *= 2
    return inverses


def span(h):
    return slice(h * HS, (h + 1) * HS)


def rates_of(base_ref, gate_ref, h):
    boost = base_ref[h] * gate_ref[0, h : h + 1, :]
    return boost, boost / (1.0 + boost)


def maps_kernel(
    pos_ref, base_ref, tok_ref, wk_ref, wv_ref, gate_ref, init_ref,
    k_ref, v_ref, ninv_ref, gram_ref, inv_ref, bt_ref, d_ref, send_ref, o_ref, half_ref,
):
    half = tok_ref.shape[2] // 2
    columns = pl.ds(pl.multiple_of((1 - pos_ref[0]) * half, half), half)
    half_ref[...] = tok_ref[0, :, columns].astype(F32)
    tok = tok_ref[0]
    kraw_all = jnp.dot(tok, wk_ref[0], preferred_element_type=F32).astype(BF).astype(F32)
    v_all = jnp.dot(tok, wv_ref[0], preferred_element_type=F32).astype(BF).astype(F32)
    n = kraw_all.shape[0]
    i, j = places(n)
    strict = (i // MB) > (j // MB)
    heads = range(init_ref.shape[0])
    ks, kts, es, lows = [], [], [], []
    for h in heads:
        kraw = kraw_all[:, span(h)]
        ninv = lax.rsqrt(jnp.sum(kraw * kraw, -1, keepdims=True) + 1e-06)
        k = kraw * ninv
        kt = k.T
        _, e = rates_of(base_ref, gate_ref, h)
        gram = dot(k, kt, NN, 3)
        ninv_ref[h] = jnp.broadcast_to(ninv, (n, HS))
        k_ref[:, span(h)] = k
        gram_ref[h] = gram
        ks.append(k)
        kts.append(kt)
        es.append(e)
        lows.append(jnp.where(strict, gram * e, 0.0))
    v_ref[...] = v_all
    inverses = unit_lower_inverses(lows)
    a, b = places(HS)
    for h in heads:
        bt = dot(kts[h] * es[h], inverses[h], NN, 3)
        inv_ref[h] = inverses[h]
        bt_ref[h] = bt
        decay = jnp.where(a == b, 1.0, 0.0) - dot(bt, ks[h], NN, 3)
        offset = dot(bt, v_all[:, span(h)], NN, 3)
        d_ref[h] = decay
        o_ref[h] = offset
        first = dot(decay, init_ref[h], NN, 3) + offset
        send_ref[h] = jnp.where(pos_ref[4] == 0, first, offset)


def reach_kernel(
    pos_ref, base_ref, tok_ref, wq_ref, gate_ref, k_ref, v_ref, inv_ref,
    q_ref, score_ref, rv_ref, y_ref, qt_ref, zv_ref, tokt_ref,
):
    half = tok_ref.shape[2] // 2
    columns = pl.ds(pl.multiple_of(pos_ref[0] * half, half), half)
    tokt_ref[...] = tok_ref[0, :, columns].astype(F32).T.astype(BF)
    q_all = jnp.dot(tok_ref[0], wq_ref[0], preferred_element_type=F32).astype(BF).astype(F32)
    n = q_all.shape[0]
    i, j = places(n)
    q_ref[...] = q_all
    for h in range(inv_ref.shape[0]):
        q = q_all[:, span(h)]
        k = k_ref[:, span(h)]
        _, e = rates_of(base_ref, gate_ref, h)
        score = dot(q, k, NT, 3)
        mix = jnp.where(i >= j, score * e, 0.0)
        inv = inv_ref[h]
        rv = dot(inv, v_ref[:, span(h)], NN, 3)
        y = dot(inv, k, NN, 3)
        score_ref[h] = score
        rv_ref[:, span(h)] = rv
        y_ref[:, span(h)] = y
        qt_ref[:, span(h)] = q - dot(mix, y, NN, 3)
        zv_ref[:, span(h)] = dot(mix, rv, NN, 3)


def step_kernel(d_ref, w_ref, o_ref, after_ref, out_ref, *, transposed):
    del after_ref
    for h in range(d_ref.shape[0]):
        out_ref[h] = o_ref[h] + dot(d_ref[h], w_ref[h], TN if transposed else NN, 3)


def norm_kernel(
    pos_ref, init_ref, near_ref, mid_ref, far_ref, rd_ref, qt_ref, zv_ref, up_ref, gain_ref, after_ref,
    w_ref, h_ref, p_ref, dgain_ref,
):
    del after_ref
    ctx = pos_ref[4]
    for h in range(init_ref.shape[0]):
        last = dot(rd_ref[h], far_ref[h], NN, 3) + near_ref[h]
        start = jnp.where(
            ctx == 0, init_ref[h], jnp.where(ctx == 1, near_ref[h], jnp.where(ctx == 2, mid_ref[h], last))
        )
        w_ref[h] = start
        qt = qt_ref[:, span(h)]
        z = dot(qt, start, NN, 3) + zv_ref[:, span(h)]
        up = up_ref[0, :, span(h)].astype(F32)
        centred = z - jnp.mean(z, -1, keepdims=True)
        inv_std = lax.rsqrt(jnp.mean(centred * centred, -1, keepdims=True) + 1e-05)
        normed = centred * inv_std
        weighted = up * gain_ref[h : h + 1, :]
        back = inv_std * (
            weighted
            - jnp.mean(weighted, -1, keepdims=True)
            - normed * jnp.mean(weighted * normed, -1, keepdims=True)
        )
        h_ref[:, span(h)] = back
        p_ref[h] = dot(qt, back, TN, 3)
        dgain_ref[h : h + 1, :] = jnp.sum(up * normed, axis=0, keepdims=True)


def query_kernel(
    base_ref, gate_ref, w_ref, h_ref, up_ref, q_ref, score_ref, rv_ref, y_ref, k_ref, inv_ref,
    dq_ref, r_ref, x_ref, dk_ref, de_ref,
):
    n = h_ref.shape[0]
    i, j = places(n)
    for h in range(w_ref.shape[0]):
        w = w_ref[h]
        back = h_ref[:, span(h)]
        k = k_ref[:, span(h)]
        q = q_ref[:, span(h)]
        score = score_ref[h]
        _, e = rates_of(base_ref, gate_ref, h)
        mix = jnp.where(i >= j, score * e, 0.0)
        r = rv_ref[:, span(h)] - dot(y_ref[:, span(h)], w, NN, 3)
        r_ref[:, span(h)] = r
        d_mix = jnp.where(i >= j, dot(back, r, NT, 3), 0.0)
        d_score = d_mix * e
        dq = up_ref[0, :, span(h)].astype(F32) + dot(back, w, NT, 3) + dot(d_score, k, NN, 3)
        dq_ref[:, span(h)] = dq.astype(BF).astype(F32)
        x_ref[:, span(h)] = dot(inv_ref[h], dot(mix, back, TN, 3), TN, 3)
        dk_ref[:, span(h)] = dot(d_score, q, TN, 3)
        de_ref[h : h + 1, :] = jnp.sum(d_mix * score, axis=0, keepdims=True)


def keys_kernel(
    pos_ref, base_ref, gate_ref, rp_ref, mid_ref, far_ref, rd_ref, p_ref, d_ref, w_ref, k_ref, ninv_ref,
    gram_ref, bt_ref, r_ref, x_ref, dk_ref, de_ref, dgain_ref, dq_ref,
    all_ref, gates_ref,
):
    ctx = pos_ref[4]
    n = k_ref.shape[0]
    i, j = places(n)
    strict = (i // MB) > (j // MB)
    all_ref[0:n, :] = dq_ref[...]
    all_ref[3 * n + HS : 3 * n + EXTRA, :] = jnp.zeros((EXTRA - HS, all_ref.shape[1]), F32)
    for h in range(w_ref.shape[0]):
        first = rp_ref[h] + dot(rd_ref[h], far_ref[h], TN, 3)
        end = jnp.where(
            ctx == 0, first, jnp.where(ctx == 1, mid_ref[h], jnp.where(ctx == 2, rp_ref[h], 0.0))
        )
        all_ref[3 * n : 3 * n + HS, span(h)] = jnp.where(ctx == 0, p_ref[h] + dot(d_ref[h], end, TN, 3), 0.0)
        w = w_ref[h]
        k = k_ref[:, span(h)]
        r = r_ref[:, span(h)]
        boost, e = rates_of(base_ref, gate_ref, h)
        x = x_ref[:, span(h)] + dot(bt_ref[h], end, TN, 3)
        all_ref[2 * n : 3 * n, span(h)] = x.astype(BF).astype(F32)
        d_low = jnp.where(strict, -dot(x, r, NT, 3), 0.0)
        d_gram = d_low * e
        dk = (
            dk_ref[:, span(h)]
            - dot(x, w, NT, 3)
            + to_col(e) * dot(r, end, NT, 3)
            + dot(d_gram + d_gram.T, k, NN, 3)
        )
        pull = to_row(jnp.sum(r * dot(k, end, NN, 3), axis=1, keepdims=True))
        de = de_ref[h : h + 1, :] + jnp.sum(d_low * gram_ref[h], axis=0, keepdims=True) + pull
        draw = ninv_ref[h] * (dk - k * jnp.sum(k * dk, -1, keepdims=True))
        all_ref[n : 2 * n, span(h)] = draw.astype(BF).astype(F32)
        d_boost = de / ((1.0 + boost) * (1.0 + boost))
        gates_ref[0, h : h + 1, :] = d_boost * base_ref[h]
        all_ref[3 * n + HS : 3 * n + HS + 1, span(h)] = dgain_ref[h : h + 1, :]
        all_ref[3 * n + HS + 1 : 3 * n + HS + 2, span(h)] = jnp.broadcast_to(
            jnp.sum(d_boost * gate_ref[0, h : h + 1, :], axis=1, keepdims=True), (1, HS)
        )


def turn_kernel(other_ref, out_ref):
    out_ref[...] = other_ref[...].T.astype(BF)


def product_kernel(pos_ref, tokt_ref, other_tokt_ref, own_ref, other_ref, *out_refs):
    n = tokt_ref.shape[1]
    for turn, out_ref in zip(TURNS, out_refs):
        at = (pos_ref[1] + turn) & (RING - 1)
        rows = pl.ds(pl.multiple_of(at * CHUNK, CHUNK), CHUNK)
        for m in range(3):
            out_ref[m * CHUNK : (m + 1) * CHUNK, :] = jnp.dot(
                tokt_ref[rows, :], own_ref[m * n : (m + 1) * n, :].astype(BF), preferred_element_type=F32
            ) + jnp.dot(
                other_tokt_ref[rows, :], other_ref[m * n : (m + 1) * n, :].astype(BF), preferred_element_type=F32
            )
        extra = pl.ds(pl.multiple_of(3 * n + (pos_ref[0] * RING + at) * PIECE, 8), PIECE)
        out_ref[3 * CHUNK : 3 * CHUNK + PIECE, :] = own_ref[extra, :] + other_ref[extra, :]


def token_kernel(w_ref, all_ref, out_ref, held_ref, sem):
    n = out_ref.shape[1]
    ds = [all_ref[m * n : (m + 1) * n, :].astype(BF) for m in range(3)]
    span_rows = w_ref.shape[1] // RING
    copies = []
    for at in range(RING):
        rows = slice(at * span_rows, (at + 1) * span_rows)
        total = lax.dot_general(ds[0], w_ref[0, rows, :], NT, preferred_element_type=F32)
        total = total + lax.dot_general(ds[1], w_ref[1, rows, :], NT, preferred_element_type=F32)
        held_ref[at] = total + lax.dot_general(ds[2], w_ref[2, rows, :], NT, preferred_element_type=F32)
        copies.append(pltpu.make_async_copy(held_ref.at[at], out_ref.at[at], sem.at[at]))
        copies[-1].start()
    for copy in copies:
        copy.wait()


def sum_kernel(own_ref, back_ref, ahead_ref, far_ref, out_ref):
    out_ref[...] = (own_ref[...] + far_ref[...]) + (back_ref[...] + ahead_ref[...])


def place_kernel(pos_ref, *refs, half):
    pieces = refs[:RING]
    out_ref, extra_ref, sem = refs[-3:]
    core = pos_ref[0] if half == 0 else 1 - pos_ref[0]
    copies = []
    for m, piece in enumerate(pieces):
        at = core * RING + ((pos_ref[1 + half] + TURNS[m]) & (RING - 1))
        rows = pl.ds(pl.multiple_of(at * CHUNK, CHUNK), CHUNK)
        for s in range(3):
            copies.append(
                pltpu.make_async_copy(piece.at[pl.ds(s * CHUNK, CHUNK), :], out_ref.at[s, rows, :], sem.at[s, m])
            )
    for copy in copies:
        copy.start()
    for m, piece in enumerate(pieces):
        at = (pos_ref[1 + half] + TURNS[m]) & (RING - 1)
        extra_ref[pl.ds(pl.multiple_of(at * PIECE, 8), PIECE), :] = piece[3 * CHUNK : 3 * CHUNK + PIECE, :]
    for copy in copies:
        copy.wait()


def small_kernel(pos_ref, own_ref, other_ref, init_ref, gain_ref, rates_ref, extra_ref):
    rows = own_ref.shape[0]
    extra_ref[pl.ds(pl.multiple_of(pos_ref[0] * rows, 8), rows), :] = own_ref[...]
    extra_ref[pl.ds(pl.multiple_of((1 - pos_ref[0]) * rows, 8), rows), :] = other_ref[...]
    for h in range(init_ref.shape[0]):
        init_ref[h] = extra_ref[0:HS, span(h)]
        gain_ref[h : h + 1, :] = extra_ref[HS : HS + 1, span(h)]
        rates_ref[h : h + 1, :] = extra_ref[HS + 1 : HS + 2, span(h)]


def moves(first, by):
    pairs = []
    for x in range(RING):
        for core in range(2):
            for y in range(RING):
                along_x = (core == 0) == first
                to_x = (x + by) % RING if along_x else x
                to_y = y if along_x else (y + by) % RING
                pairs.append(((x * 2 + core) * RING + y, (to_x * 2 + core) * RING + to_y))
    return pairs


def round_turn(chunks, first):
    return [
        lax.ppermute(chunk, ("dp", "ctx"), moves(first, turn)) for chunk, turn in zip(chunks, TURNS[1:])
    ]


def swap(value):
    return lax.ppermute(value, "dp", [(i, i ^ 1) for i in range(2 * RING)])


VM = pl.BlockSpec(memory_space=pltpu.VMEM)
SM = pl.BlockSpec(memory_space=pltpu.SMEM)
PARAMS = pltpu.CompilerParams(vmem_limit_bytes=20 * 1024 * 1024)


def shape(*dims, dtype=F32):
    return jax.ShapeDtypeStruct(dims, dtype)


def vmem(*dims, dtype=F32):
    return pltpu.VMEM(dims, dtype)


def hbm(value):
    return pltpu.with_memory_space_constraint(value, pltpu.HBM)


def whole(kernel, outs, specs):
    return pl.pallas_call(
        kernel,
        out_shape=outs,
        in_specs=specs,
        out_specs=tuple(VM for _ in outs) if isinstance(outs, tuple) else VM,
        compiler_params=PARAMS,
    )


def part(which, dims):
    return pl.BlockSpec((1,) + dims, lambda i: (which, 0, 0))


def full(*dims):
    return pl.BlockSpec(dims, lambda i: (0,) * len(dims))


def body(tokens, proj_weights, init_weight, base_rates, gate_values, out_gain, cotangent):
    n = tokens.shape[1]
    model = tokens.shape[2]
    heads = init_weight.shape[0]
    wide = heads * HS
    ctx = lax.axis_index("ctx")
    dp = lax.axis_index("dp")
    core, x_at = dp % 2, dp // 2
    pos = jnp.stack(
        [core, jnp.where(core == 0, x_at, ctx), jnp.where(core == 0, ctx, x_at), lax.axis_index("head"), ctx]
    ).astype(jnp.int32)
    half = model // 2

    wide_f32 = vmem(n, wide)
    square = vmem(heads, n, n)
    small = vmem(heads, HS, HS)
    wspec = functools.partial(part, dims=(model, wide))
    tokens = hbm(tokens)
    raw_weights = proj_weights
    proj_weights = hbm(proj_weights)
    anywhere = pl.BlockSpec(memory_space=pl.ANY)

    k, v, ninv, gram, inv, bt, decay, send, offset, other_half = pl.pallas_call(
        maps_kernel,
        grid=(1,),
        out_shape=(
            wide_f32, wide_f32, vmem(heads, n, HS), square, square, vmem(heads, HS, n), small, small, small,
            vmem(n, half),
        ),
        in_specs=[SM, SM, full(1, n, model), wspec(1), wspec(2), full(1, heads, n), full(heads, HS, HS)],
        out_specs=(VM,) * 10,
        compiler_params=PARAMS,
    )(pos, hbm(base_rates), tokens, proj_weights, proj_weights, hbm(gate_values), hbm(init_weight))

    near = lax.ppermute(send, "ctx", [(0, 1), (2, 3)])
    moved = lax.ppermute(decay, "ctx", [(2, 3), (1, 0)])
    got_half = swap(other_half)

    q, score, rv, y, qt, zv, tokt = pl.pallas_call(
        reach_kernel,
        grid=(1,),
        out_shape=(wide_f32, square, wide_f32, wide_f32, wide_f32, wide_f32, vmem(half, n, dtype=BF)),
        in_specs=[SM, SM, full(1, n, model), wspec(0), full(1, heads, n), VM, VM, VM],
        out_specs=(VM,) * 7,
        compiler_params=PARAMS,
    )(pos, base_rates, tokens, proj_weights, gate_values, k, v, inv)

    second = whole(functools.partial(step_kernel, transposed=False), small, [VM] * 3 + [anywhere])(
        decay, near, offset, qt
    )
    mid = lax.ppermute(second, "ctx", [(1, 2)])
    far = lax.ppermute(second, "ctx", [(1, 3)])
    other_tokt = whole(turn_kernel, vmem(half, n, dtype=BF), [VM])(got_half)

    w, back, pulled, dgain = whole(
        norm_kernel, (small, wide_f32, small, vmem(heads, HS)), [SM] + [VM] * 9 + [anywhere]
    )(pos, init_weight, near, mid, far, moved, qt, zv, cotangent, out_gain, other_tokt)

    back_near = lax.ppermute(pulled, "ctx", [(3, 2), (1, 0)])

    dq, r, x, dk, de = whole(
        query_kernel, (wide_f32, wide_f32, wide_f32, wide_f32, vmem(heads, n)), [SM] + [VM] * 10
    )(base_rates, gate_values, w, back, cotangent, q, score, rv, y, k, inv)

    back_second = whole(functools.partial(step_kernel, transposed=True), small, [VM] * 3 + [anywhere])(
        decay, back_near, pulled, de
    )
    back_mid = lax.ppermute(back_second, "ctx", [(2, 1)])
    back_far = lax.ppermute(back_second, "ctx", [(2, 0)])

    grads, grad_gates = whole(
        keys_kernel, (vmem(3 * n + EXTRA, wide), shape(1, heads, n)), [SM, SM] + [VM] * 18
    )(pos, base_rates, gate_values, back_near, back_mid, back_far, moved, pulled, decay, w, k, ninv, gram, bt, r, x,
      dk, de, dgain, dq)

    chunk = vmem(3 * CHUNK + PIECE, wide)
    own, *away = whole(product_kernel, (chunk,) * RING, [SM] + [VM] * 4)(
        pos, tokt, other_tokt, grads, swap(grads)
    )
    away = round_turn(away, True)
    summed = pl.pallas_call(
        token_kernel,
        out_shape=shape(RING, n, model // RING),
        in_specs=[VM, VM],
        out_specs=anywhere,
        scratch_shapes=[pltpu.VMEM((RING, n, model // RING), F32), pltpu.SemaphoreType.DMA((RING,))],
        compiler_params=PARAMS,
    )(raw_weights, grads)
    grad_tokens = lax.psum_scatter(summed, "head", scatter_dimension=0, tiled=True).astype(BF)

    part_sum = whole(sum_kernel, chunk, [VM] * 4)(own, *away)
    total = whole(sum_kernel, chunk, [VM] * 4)(part_sum, *round_turn([part_sum] * 3, False))
    from_back, from_ahead, from_far = round_turn([total] * 3, True)
    mine = [total, from_ahead, from_back, from_far]
    others = [swap(piece) for piece in mine]

    out, extra = shape(3, model, wide), vmem(EXTRA // 2, wide)
    scratch = [pltpu.SemaphoreType.DMA((3, RING))]
    placed, own_extra = pl.pallas_call(
        functools.partial(place_kernel, half=0),
        out_shape=(out, extra),
        in_specs=[SM] + [VM] * RING,
        out_specs=(anywhere, VM),
        scratch_shapes=scratch,
        compiler_params=PARAMS,
    )(pos, *mine)
    grad_proj, other_extra = pl.pallas_call(
        functools.partial(place_kernel, half=1),
        out_shape=(out, extra),
        in_specs=[SM] + [VM] * RING + [anywhere],
        out_specs=(anywhere, VM),
        scratch_shapes=scratch,
        input_output_aliases={RING + 1: 0},
        compiler_params=PARAMS,
    )(pos, *others, placed)
    grad_init, grad_gain, rates = pl.pallas_call(
        small_kernel,
        out_shape=(shape(heads, HS, HS), shape(heads, HS), shape(heads, HS)),
        in_specs=[SM, VM, VM],
        out_specs=(VM, VM, VM),
        scratch_shapes=[pltpu.VMEM((EXTRA, wide), F32)],
        compiler_params=PARAMS,
    )(pos, own_extra, other_extra)
    return (grad_tokens, grad_proj, grad_init, grad_gain, rates[:, 0], grad_gates)


def solution(mesh):
    in_specs = (
        P("dp", "ctx", None),
        P(None, None, "head"),
        P("head", None, None),
        P("head"),
        P("dp", "head", "ctx"),
        P("head", None),
        P("dp", "ctx", "head"),
    )
    out_specs = (
        P("dp", "ctx", "head"),
        P(None, None, "head"),
        P("head", None, None),
        P("head", None),
        P("head"),
        P("dp", "head", "ctx"),
    )
    return jax.shard_map(body, mesh=mesh, in_specs=in_specs, out_specs=out_specs, check_vma=False)
```

```python
import functools

import jax
import jax.numpy as jnp
from jax import lax
from jax.experimental import pallas as pl
from jax.experimental.pallas import tpu as pltpu
from jax.sharding import PartitionSpec as P

MB = 16
HS = 128
RING = 4
TURNS = (0, 1, 3, 2)
CHUNK = 256
PIECE = 24
EXTRA = 2 * RING * PIECE
F32 = jnp.float32
BF = jnp.bfloat16
NN = (((1,), (0,)), ((), ()))
NT = (((1,), (1,)), ((), ()))
TN = (((0,), (0,)), ((), ()))


def dot(a, b, dims, passes):
    ah = a.astype(BF)
    bh = b.astype(BF)
    result = lax.dot_general(ah, bh, dims, preferred_element_type=F32)
    if passes == 3:
        al = (a - ah.astype(F32)).astype(BF)
        bl = (b - bh.astype(F32)).astype(BF)
        result = result + (
            lax.dot_general(ah, bl, dims, preferred_element_type=F32)
            + lax.dot_general(al, bh, dims, preferred_element_type=F32)
        )
    return result


def places(n):
    return (
        lax.broadcasted_iota(jnp.int32, (n, n), 0),
        lax.broadcasted_iota(jnp.int32, (n, n), 1),
    )


def to_col(row):
    i, j = places(row.shape[1])
    return jnp.sum(jnp.where(i == j, row, 0.0), axis=1, keepdims=True)


def to_row(col):
    i, j = places(col.shape[0])
    return jnp.sum(jnp.where(i == j, col, 0.0), axis=0, keepdims=True)


def unit_lower_inverses(lowers):
    n = lowers[0].shape[0]
    i, j = places(n)
    size = 2 * MB
    same = (i // size) == (j // size)
    inverses = [jnp.where(i == j, 1.0, 0.0) - jnp.where(same, low, 0.0) for low in lowers]
    while size < n:
        pair = ((i // (2 * size)) == (j // (2 * size))) & ((i // size) != (j // size))
        corners = [jnp.where(pair, low, 0.0) for low in lowers]
        halves = [dot(inv, corner, NN, 3) for inv, corner in zip(inverses, corners)]
        inverses = [inv - dot(half, inv, NN, 3) for inv, half in zip(inverses, halves)]
        size *= 2
    return inverses


def span(h):
    return slice(h * HS, (h + 1) * HS)


def rates_of(base_ref, gate_ref, h):
    boost = base_ref[h] * gate_ref[0, h : h + 1, :]
    return boost, boost / (1.0 + boost)


def maps_kernel(
    pos_ref, base_ref, tok_ref, wk_ref, wv_ref, gate_ref, init_ref,
    k_ref, v_ref, ninv_ref, gram_ref, inv_ref, bt_ref, d_ref, send_ref, o_ref, half_ref,
):
    half = tok_ref.shape[2] // 2
    columns = pl.ds(pl.multiple_of((1 - pos_ref[0]) * half, half), half)
    half_ref[...] = tok_ref[0, :, columns].astype(F32)
    tok = tok_ref[0]
    kraw_all = jnp.dot(tok, wk_ref[0], preferred_element_type=F32).astype(BF).astype(F32)
    v_all = jnp.dot(tok, wv_ref[0], preferred_element_type=F32).astype(BF).astype(F32)
    n = kraw_all.shape[0]
    i, j = places(n)
    strict = (i // MB) > (j // MB)
    heads = range(init_ref.shape[0])
    ks, kts, es, lows = [], [], [], []
    for h in heads:
        kraw = kraw_all[:, span(h)]
        ninv = lax.rsqrt(jnp.sum(kraw * kraw, -1, keepdims=True) + 1e-06)
        k = kraw * ninv
        kt = k.T
        _, e = rates_of(base_ref, gate_ref, h)
        gram = dot(k, kt, NN, 3)
        ninv_ref[h] = jnp.broadcast_to(ninv, (n, HS))
        k_ref[:, span(h)] = k
        gram_ref[h] = gram
        ks.append(k)
        kts.append(kt)
        es.append(e)
        lows.append(jnp.where(strict, gram * e, 0.0))
    v_ref[...] = v_all
    inverses = unit_lower_inverses(lows)
    a, b = places(HS)
    for h in heads:
        bt = dot(kts[h] * es[h], inverses[h], NN, 3)
        inv_ref[h] = inverses[h]
        bt_ref[h] = bt
        decay = jnp.where(a == b, 1.0, 0.0) - dot(bt, ks[h], NN, 3)
        offset = dot(bt, v_all[:, span(h)], NN, 3)
        d_ref[h] = decay
        o_ref[h] = offset
        first = dot(decay, init_ref[h], NN, 3) + offset
        send_ref[h] = jnp.where(pos_ref[4] == 0, first, offset)


def reach_kernel(
    pos_ref, base_ref, tok_ref, wq_ref, gate_ref, k_ref, v_ref, inv_ref,
    q_ref, score_ref, rv_ref, y_ref, qt_ref, zv_ref, tokt_ref,
):
    half = tok_ref.shape[2] // 2
    columns = pl.ds(pl.multiple_of(pos_ref[0] * half, half), half)
    tokt_ref[...] = tok_ref[0, :, columns].astype(F32).T.astype(BF)
    q_all = jnp.dot(tok_ref[0], wq_ref[0], preferred_element_type=F32).astype(BF).astype(F32)
    n = q_all.shape[0]
    i, j = places(n)
    q_ref[...] = q_all
    for h in range(inv_ref.shape[0]):
        q = q_all[:, span(h)]
        k = k_ref[:, span(h)]
        _, e = rates_of(base_ref, gate_ref, h)
        score = dot(q, k, NT, 3)
        mix = jnp.where(i >= j, score * e, 0.0)
        inv = inv_ref[h]
        rv = dot(inv, v_ref[:, span(h)], NN, 3)
        y = dot(inv, k, NN, 3)
        score_ref[h] = score
        rv_ref[:, span(h)] = rv
        y_ref[:, span(h)] = y
        qt_ref[:, span(h)] = q - dot(mix, y, NN, 3)
        zv_ref[:, span(h)] = dot(mix, rv, NN, 3)


def step_kernel(d_ref, w_ref, o_ref, after_ref, out_ref, *, transposed):
    del after_ref
    for h in range(d_ref.shape[0]):
        out_ref[h] = o_ref[h] + dot(d_ref[h], w_ref[h], TN if transposed else NN, 3)


def norm_kernel(
    pos_ref, init_ref, near_ref, mid_ref, far_ref, rd_ref, qt_ref, zv_ref, up_ref, gain_ref, after_ref,
    w_ref, h_ref, p_ref, dgain_ref,
):
    del after_ref
    ctx = pos_ref[4]
    for h in range(init_ref.shape[0]):
        last = dot(rd_ref[h], far_ref[h], NN, 3) + near_ref[h]
        start = jnp.where(
            ctx == 0, init_ref[h], jnp.where(ctx == 1, near_ref[h], jnp.where(ctx == 2, mid_ref[h], last))
        )
        w_ref[h] = start
        qt = qt_ref[:, span(h)]
        z = dot(qt, start, NN, 3) + zv_ref[:, span(h)]
        up = up_ref[0, :, span(h)].astype(F32)
        centred = z - jnp.mean(z, -1, keepdims=True)
        inv_std = lax.rsqrt(jnp.mean(centred * centred, -1, keepdims=True) + 1e-05)
        normed = centred * inv_std
        weighted = up * gain_ref[h : h + 1, :]
        back = inv_std * (
            weighted
            - jnp.mean(weighted, -1, keepdims=True)
            - normed * jnp.mean(weighted * normed, -1, keepdims=True)
        )
        h_ref[:, span(h)] = back
        p_ref[h] = dot(qt, back, TN, 3)
        dgain_ref[h : h + 1, :] = jnp.sum(up * normed, axis=0, keepdims=True)


def query_kernel(
    base_ref, gate_ref, w_ref, h_ref, up_ref, q_ref, score_ref, rv_ref, y_ref, k_ref, inv_ref,
    dq_ref, r_ref, x_ref, dk_ref, de_ref,
):
    n = h_ref.shape[0]
    i, j = places(n)
    for h in range(w_ref.shape[0]):
        w = w_ref[h]
        back = h_ref[:, span(h)]
        k = k_ref[:, span(h)]
        q = q_ref[:, span(h)]
        score = score_ref[h]
        _, e = rates_of(base_ref, gate_ref, h)
        mix = jnp.where(i >= j, score * e, 0.0)
        r = rv_ref[:, span(h)] - dot(y_ref[:, span(h)], w, NN, 3)
        r_ref[:, span(h)] = r
        d_mix = jnp.where(i >= j, dot(back, r, NT, 3), 0.0)
        d_score = d_mix * e
        dq = up_ref[0, :, span(h)].astype(F32) + dot(back, w, NT, 3) + dot(d_score, k, NN, 3)
        dq_ref[:, span(h)] = dq.astype(BF).astype(F32)
        x_ref[:, span(h)] = dot(inv_ref[h], dot(mix, back, TN, 3), TN, 3)
        dk_ref[:, span(h)] = dot(d_score, q, TN, 3)
        de_ref[h : h + 1, :] = jnp.sum(d_mix * score, axis=0, keepdims=True)


def keys_kernel(
    pos_ref, base_ref, gate_ref, rp_ref, mid_ref, far_ref, rd_ref, p_ref, d_ref, w_ref, k_ref, ninv_ref,
    gram_ref, bt_ref, r_ref, x_ref, dk_ref, de_ref, dgain_ref, dq_ref,
    all_ref, gates_ref,
):
    ctx = pos_ref[4]
    n = k_ref.shape[0]
    i, j = places(n)
    strict = (i // MB) > (j // MB)
    all_ref[0:n, :] = dq_ref[...]
    all_ref[3 * n + HS : 3 * n + EXTRA, :] = jnp.zeros((EXTRA - HS, all_ref.shape[1]), F32)
    for h in range(w_ref.shape[0]):
        first = rp_ref[h] + dot(rd_ref[h], far_ref[h], TN, 3)
        end = jnp.where(
            ctx == 0, first, jnp.where(ctx == 1, mid_ref[h], jnp.where(ctx == 2, rp_ref[h], 0.0))
        )
        all_ref[3 * n : 3 * n + HS, span(h)] = jnp.where(ctx == 0, p_ref[h] + dot(d_ref[h], end, TN, 3), 0.0)
        w = w_ref[h]
        k = k_ref[:, span(h)]
        r = r_ref[:, span(h)]
        boost, e = rates_of(base_ref, gate_ref, h)
        x = x_ref[:, span(h)] + dot(bt_ref[h], end, TN, 3)
        all_ref[2 * n : 3 * n, span(h)] = x.astype(BF).astype(F32)
        d_low = jnp.where(strict, -dot(x, r, NT, 3), 0.0)
        d_gram = d_low * e
        dk = (
            dk_ref[:, span(h)]
            - dot(x, w, NT, 3)
            + to_col(e) * dot(r, end, NT, 3)
            + dot(d_gram + d_gram.T, k, NN, 3)
        )
        pull = to_row(jnp.sum(r * dot(k, end, NN, 3), axis=1, keepdims=True))
        de = de_ref[h : h + 1, :] + jnp.sum(d_low * gram_ref[h], axis=0, keepdims=True) + pull
        draw = ninv_ref[h] * (dk - k * jnp.sum(k * dk, -1, keepdims=True))
        all_ref[n : 2 * n, span(h)] = draw.astype(BF).astype(F32)
        d_boost = de / ((1.0 + boost) * (1.0 + boost))
        gates_ref[0, h : h + 1, :] = d_boost * base_ref[h]
        all_ref[3 * n + HS : 3 * n + HS + 1, span(h)] = dgain_ref[h : h + 1, :]
        all_ref[3 * n + HS + 1 : 3 * n + HS + 2, span(h)] = jnp.broadcast_to(
            jnp.sum(d_boost * gate_ref[0, h : h + 1, :], axis=1, keepdims=True), (1, HS)
        )


def turn_kernel(other_ref, out_ref):
    out_ref[...] = other_ref[...].T.astype(BF)


def product_kernel(pos_ref, tokt_ref, other_tokt_ref, own_ref, other_ref, *out_refs):
    n = tokt_ref.shape[1]
    for turn, out_ref in zip(TURNS, out_refs):
        at = (pos_ref[1] + turn) & (RING - 1)
        rows = pl.ds(pl.multiple_of(at * CHUNK, CHUNK), CHUNK)
        for m in range(3):
            out_ref[m * CHUNK : (m + 1) * CHUNK, :] = jnp.dot(
                tokt_ref[rows, :], own_ref[m * n : (m + 1) * n, :].astype(BF), preferred_element_type=F32
            ) + jnp.dot(
                other_tokt_ref[rows, :], other_ref[m * n : (m + 1) * n, :].astype(BF), preferred_element_type=F32
            )
        extra = pl.ds(pl.multiple_of(3 * n + (pos_ref[0] * RING + at) * PIECE, 8), PIECE)
        out_ref[3 * CHUNK : 3 * CHUNK + PIECE, :] = own_ref[extra, :] + other_ref[extra, :]


def token_kernel(pos_ref, w_ref, all_ref, *out_refs):
    n = out_refs[0].shape[0]
    ds = [all_ref[m * n : (m + 1) * n, :].astype(BF) for m in range(3)]
    quarter = w_ref.shape[1] // RING
    for turn, out_ref in zip(TURNS, out_refs):
        at = (pos_ref[3] + turn) & (RING - 1)
        rows = pl.ds(pl.multiple_of(at * quarter, quarter), quarter)
        total = lax.dot_general(ds[0], w_ref[0, rows, :], NT, preferred_element_type=F32)
        total = total + lax.dot_general(ds[1], w_ref[1, rows, :], NT, preferred_element_type=F32)
        out_ref[...] = total + lax.dot_general(ds[2], w_ref[2, rows, :], NT, preferred_element_type=F32)


def sum_kernel(own_ref, back_ref, ahead_ref, far_ref, *refs):
    refs[-1][...] = (own_ref[...] + far_ref[...]) + (back_ref[...] + ahead_ref[...])


def place_kernel(pos_ref, *refs, which):
    pieces = refs[: len(which)]
    out_ref, sem = refs[-2:]
    copies = []
    for g, ((half, m), piece) in enumerate(zip(which, pieces)):
        core = pos_ref[0] if half == 0 else 1 - pos_ref[0]
        at = core * RING + ((pos_ref[1 + half] + TURNS[m]) & (RING - 1))
        rows = pl.ds(pl.multiple_of(at * CHUNK, CHUNK), CHUNK)
        for s in range(3):
            copies.append(
                pltpu.make_async_copy(piece.at[pl.ds(s * CHUNK, CHUNK), :], out_ref.at[s, rows, :], sem.at[s, g])
            )
    for copy in copies:
        copy.start()
    for copy in copies:
        copy.wait()


def last_kernel(pos_ref, *refs, which):
    pieces = refs[: 2 * RING]
    out_ref, init_ref, gain_ref, rates_ref, extra_ref, sem = refs[-6:]
    copies = []
    for g, (half, m) in enumerate(which):
        core = pos_ref[0] if half == 0 else 1 - pos_ref[0]
        at = core * RING + ((pos_ref[1 + half] + TURNS[m]) & (RING - 1))
        rows = pl.ds(pl.multiple_of(at * CHUNK, CHUNK), CHUNK)
        for s in range(3):
            copies.append(
                pltpu.make_async_copy(
                    pieces[half * RING + m].at[pl.ds(s * CHUNK, CHUNK), :], out_ref.at[s, rows, :], sem.at[s, g]
                )
            )
    for copy in copies:
        copy.start()
    for p, piece in enumerate(pieces):
        core = pos_ref[0] if p < RING else 1 - pos_ref[0]
        at = core * RING + ((pos_ref[1 + p // RING] + TURNS[p % RING]) & (RING - 1))
        extra_ref[pl.ds(pl.multiple_of(at * PIECE, 8), PIECE), :] = piece[3 * CHUNK : 3 * CHUNK + PIECE, :]
    for h in range(init_ref.shape[0]):
        init_ref[h] = extra_ref[0:HS, span(h)]
        gain_ref[h : h + 1, :] = extra_ref[HS : HS + 1, span(h)]
        rates_ref[h] = extra_ref[HS + 1, h * HS]
    for copy in copies:
        copy.wait()


def moves(first, by):
    pairs = []
    for x in range(RING):
        for core in range(2):
            for y in range(RING):
                along_x = (core == 0) == first
                to_x = (x + by) % RING if along_x else x
                to_y = y if along_x else (y + by) % RING
                pairs.append(((x * 2 + core) * RING + y, (to_x * 2 + core) * RING + to_y))
    return pairs


def round_turn(chunks, first):
    return [
        lax.ppermute(chunk, ("dp", "ctx"), moves(first, turn)) for chunk, turn in zip(chunks, TURNS[1:])
    ]


def swap(value):
    return lax.ppermute(value, "dp", [(i, i ^ 1) for i in range(2 * RING)])


VM = pl.BlockSpec(memory_space=pltpu.VMEM)
SM = pl.BlockSpec(memory_space=pltpu.SMEM)
PARAMS = pltpu.CompilerParams(vmem_limit_bytes=20 * 1024 * 1024)


def shape(*dims, dtype=F32):
    return jax.ShapeDtypeStruct(dims, dtype)


def vmem(*dims, dtype=F32):
    return pltpu.VMEM(dims, dtype)


def hbm(value):
    return pltpu.with_memory_space_constraint(value, pltpu.HBM)


def whole(kernel, outs, specs):
    return pl.pallas_call(
        kernel,
        out_shape=outs,
        in_specs=specs,
        out_specs=tuple(VM for _ in outs) if isinstance(outs, tuple) else VM,
        compiler_params=PARAMS,
    )


def part(which, dims):
    return pl.BlockSpec((1,) + dims, lambda i: (which, 0, 0))


def full(*dims):
    return pl.BlockSpec(dims, lambda i: (0,) * len(dims))


def body(tokens, proj_weights, init_weight, base_rates, gate_values, out_gain, cotangent):
    n = tokens.shape[1]
    model = tokens.shape[2]
    heads = init_weight.shape[0]
    wide = heads * HS
    ctx = lax.axis_index("ctx")
    dp = lax.axis_index("dp")
    core, x_at = dp % 2, dp // 2
    pos = jnp.stack(
        [core, jnp.where(core == 0, x_at, ctx), jnp.where(core == 0, ctx, x_at), lax.axis_index("head"), ctx]
    ).astype(jnp.int32)
    half = model // 2

    wide_f32 = vmem(n, wide)
    square = vmem(heads, n, n)
    small = vmem(heads, HS, HS)
    wspec = functools.partial(part, dims=(model, wide))
    tokens = hbm(tokens)
    raw_weights = proj_weights
    proj_weights = hbm(proj_weights)
    anywhere = pl.BlockSpec(memory_space=pl.ANY)

    k, v, ninv, gram, inv, bt, decay, send, offset, other_half = pl.pallas_call(
        maps_kernel,
        grid=(1,),
        out_shape=(
            wide_f32, wide_f32, vmem(heads, n, HS), square, square, vmem(heads, HS, n), small, small, small,
            vmem(n, half),
        ),
        in_specs=[SM, SM, full(1, n, model), wspec(1), wspec(2), full(1, heads, n), full(heads, HS, HS)],
        out_specs=(VM,) * 10,
        compiler_params=PARAMS,
    )(pos, hbm(base_rates), tokens, proj_weights, proj_weights, hbm(gate_values), hbm(init_weight))

    near = lax.ppermute(send, "ctx", [(0, 1), (2, 3)])
    moved = lax.ppermute(decay, "ctx", [(2, 3), (1, 0)])
    got_half = swap(other_half)

    q, score, rv, y, qt, zv, tokt = pl.pallas_call(
        reach_kernel,
        grid=(1,),
        out_shape=(wide_f32, square, wide_f32, wide_f32, wide_f32, wide_f32, vmem(half, n, dtype=BF)),
        in_specs=[SM, SM, full(1, n, model), wspec(0), full(1, heads, n), VM, VM, VM],
        out_specs=(VM,) * 7,
        compiler_params=PARAMS,
    )(pos, base_rates, tokens, proj_weights, gate_values, k, v, inv)

    second = whole(functools.partial(step_kernel, transposed=False), small, [VM] * 3 + [anywhere])(
        decay, near, offset, qt
    )
    mid = lax.ppermute(second, "ctx", [(1, 2)])
    far = lax.ppermute(second, "ctx", [(1, 3)])
    other_tokt = whole(turn_kernel, vmem(half, n, dtype=BF), [VM])(got_half)

    w, back, pulled, dgain = whole(
        norm_kernel, (small, wide_f32, small, vmem(heads, HS)), [SM] + [VM] * 9 + [anywhere]
    )(pos, init_weight, near, mid, far, moved, qt, zv, cotangent, out_gain, other_tokt)

    back_near = lax.ppermute(pulled, "ctx", [(3, 2), (1, 0)])

    dq, r, x, dk, de = whole(
        query_kernel, (wide_f32, wide_f32, wide_f32, wide_f32, vmem(heads, n)), [SM] + [VM] * 10
    )(base_rates, gate_values, w, back, cotangent, q, score, rv, y, k, inv)

    back_second = whole(functools.partial(step_kernel, transposed=True), small, [VM] * 3 + [anywhere])(
        decay, back_near, pulled, de
    )
    back_mid = lax.ppermute(back_second, "ctx", [(2, 1)])
    back_far = lax.ppermute(back_second, "ctx", [(2, 0)])

    grads, grad_gates = whole(
        keys_kernel, (vmem(3 * n + EXTRA, wide), shape(1, heads, n)), [SM, SM] + [VM] * 18
    )(pos, base_rates, gate_values, back_near, back_mid, back_far, moved, pulled, decay, w, k, ninv, gram, bt, r, x,
      dk, de, dgain, dq)

    chunk = vmem(3 * CHUNK + PIECE, wide)
    own, *away = whole(product_kernel, (chunk,) * RING, [SM] + [VM] * 4)(
        pos, tokt, other_tokt, grads, swap(grads)
    )
    away = round_turn(away, True)
    quarters = whole(token_kernel, (vmem(n, model // RING),) * RING, [SM, VM, VM])(pos, raw_weights, grads)
    from_back, from_ahead, from_far = [
        lax.ppermute(terms, "head", [(i, (i + turn) % RING) for i in range(RING)])
        for terms, turn in zip(quarters[1:], TURNS[1:])
    ]
    grad_tokens = ((quarters[0] + from_far) + (from_back + from_ahead)).astype(BF).reshape(1, n, -1)

    part_sum = whole(sum_kernel, chunk, [VM] * 4 + [anywhere] * 2)(own, *away, from_back, from_ahead)
    total = whole(sum_kernel, chunk, [VM] * 4 + [anywhere])(part_sum, *round_turn([part_sum] * 3, False), grad_tokens)
    from_back, from_ahead, from_far = round_turn([total] * 3, True)
    mine = [total, from_ahead, from_back, from_far]
    others = [swap(piece) for piece in mine]

    out = shape(3, model, wide)
    placed = None
    for which in (((0, 0), (0, 1), (0, 2), (0, 3), (1, 0), (1, 3)),):
        given = [(mine, others)[half][m] for half, m in which] + ([] if placed is None else [placed])
        placed = pl.pallas_call(
            functools.partial(place_kernel, which=which),
            out_shape=out,
            in_specs=[SM] + [VM] * len(which) + [anywhere] * (len(given) - len(which)),
            out_specs=anywhere,
            scratch_shapes=[pltpu.SemaphoreType.DMA((3, len(which)))],
            input_output_aliases={} if placed is None else {len(which) + 1: 0},
            compiler_params=PARAMS,
        )(pos, *given)
    which = ((1, 1), (1, 2))
    grad_proj, grad_init, grad_gain, grad_rates = pl.pallas_call(
        functools.partial(last_kernel, which=which),
        out_shape=(out, shape(heads, HS, HS), shape(heads, HS), shape(heads)),
        in_specs=[SM] + [VM] * 8 + [anywhere],
        out_specs=(anywhere, VM, VM, SM),
        scratch_shapes=[pltpu.VMEM((EXTRA, wide), F32), pltpu.SemaphoreType.DMA((3, len(which)))],
        input_output_aliases={9: 0},
        compiler_params=PARAMS,
    )(pos, *mine, *others, placed)
    return (grad_tokens, grad_proj, grad_init, grad_gain, grad_rates, grad_gates)


def solution(mesh):
    in_specs = (
        P("dp", "ctx", None),
        P(None, None, "head"),
        P("head", None, None),
        P("head"),
        P("dp", "head", "ctx"),
        P("head", None),
        P("dp", "ctx", "head"),
    )
    out_specs = (
        P("dp", "ctx", "head"),
        P(None, None, "head"),
        P("head", None, None),
        P("head", None),
        P("head"),
        P("dp", "head", "ctx"),
    )
    return jax.shard_map(body, mesh=mesh, in_specs=in_specs, out_specs=out_specs, check_vma=False)
```

```python
import functools

import jax
import jax.numpy as jnp
from jax import lax
from jax.experimental import pallas as pl
from jax.experimental.pallas import tpu as pltpu
from jax.sharding import PartitionSpec as P

MB = 16
HS = 128
RING = 4
TURNS = (0, 1, 3, 2)
CHUNK = 256
SLICE = CHUNK // RING
PIECE = 32
EXTRA = 2 * RING * PIECE
F32 = jnp.float32
BF = jnp.bfloat16
NN = (((1,), (0,)), ((), ()))
NT = (((1,), (1,)), ((), ()))
TN = (((0,), (0,)), ((), ()))


def dot(a, b, dims, passes):
    ah = a.astype(BF)
    bh = b.astype(BF)
    result = lax.dot_general(ah, bh, dims, preferred_element_type=F32)
    if passes == 3:
        al = (a - ah.astype(F32)).astype(BF)
        bl = (b - bh.astype(F32)).astype(BF)
        result = result + (
            lax.dot_general(ah, bl, dims, preferred_element_type=F32)
            + lax.dot_general(al, bh, dims, preferred_element_type=F32)
        )
    return result


def places(n):
    return (
        lax.broadcasted_iota(jnp.int32, (n, n), 0),
        lax.broadcasted_iota(jnp.int32, (n, n), 1),
    )


def to_col(row):
    i, j = places(row.shape[1])
    return jnp.sum(jnp.where(i == j, row, 0.0), axis=1, keepdims=True)


def to_row(col):
    i, j = places(col.shape[0])
    return jnp.sum(jnp.where(i == j, col, 0.0), axis=0, keepdims=True)


def unit_lower_inverses(lowers):
    n = lowers[0].shape[0]
    i, j = places(n)
    size = 2 * MB
    same = (i // size) == (j // size)
    inverses = [jnp.where(i == j, 1.0, 0.0) - jnp.where(same, low, 0.0) for low in lowers]
    while size < n:
        pair = ((i // (2 * size)) == (j // (2 * size))) & ((i // size) != (j // size))
        corners = [jnp.where(pair, low, 0.0) for low in lowers]
        halves = [dot(inv, corner, NN, 3) for inv, corner in zip(inverses, corners)]
        inverses = [inv - dot(half, inv, NN, 3) for inv, half in zip(inverses, halves)]
        size *= 2
    return inverses


def span(h):
    return slice(h * HS, (h + 1) * HS)


def rates_of(base_ref, gate_ref, h):
    boost = base_ref[h] * gate_ref[0, h : h + 1, :]
    return boost, boost / (1.0 + boost)


def maps_kernel(
    pos_ref, base_ref, tok_ref, wk_ref, wv_ref, gate_ref, init_ref,
    k_ref, v_ref, ninv_ref, gram_ref, inv_ref, bt_ref, d_ref, send_ref, o_ref, half_ref,
):
    half = tok_ref.shape[2] // 2
    columns = pl.ds(pl.multiple_of((1 - pos_ref[0]) * half, half), half)
    half_ref[...] = tok_ref[0, :, columns].astype(F32)
    tok = tok_ref[0]
    kraw_all = jnp.dot(tok, wk_ref[0], preferred_element_type=F32).astype(BF).astype(F32)
    v_all = jnp.dot(tok, wv_ref[0], preferred_element_type=F32).astype(BF).astype(F32)
    n = kraw_all.shape[0]
    i, j = places(n)
    strict = (i // MB) > (j // MB)
    heads = range(init_ref.shape[0])
    ks, kts, es, lows = [], [], [], []
    for h in heads:
        kraw = kraw_all[:, span(h)]
        ninv = lax.rsqrt(jnp.sum(kraw * kraw, -1, keepdims=True) + 1e-06)
        k = kraw * ninv
        kt = k.T
        _, e = rates_of(base_ref, gate_ref, h)
        gram = dot(k, kt, NN, 3)
        ninv_ref[h] = jnp.broadcast_to(ninv, (n, HS))
        k_ref[:, span(h)] = k
        gram_ref[h] = gram
        ks.append(k)
        kts.append(kt)
        es.append(e)
        lows.append(jnp.where(strict, gram * e, 0.0))
    v_ref[...] = v_all
    inverses = unit_lower_inverses(lows)
    a, b = places(HS)
    for h in heads:
        bt = dot(kts[h] * es[h], inverses[h], NN, 3)
        inv_ref[h] = inverses[h]
        bt_ref[h] = bt
        decay = jnp.where(a == b, 1.0, 0.0) - dot(bt, ks[h], NN, 3)
        offset = dot(bt, v_all[:, span(h)], NN, 3)
        d_ref[h] = decay
        o_ref[h] = offset
        first = dot(decay, init_ref[h], NN, 3) + offset
        send_ref[h] = jnp.where(pos_ref[4] == 0, first, offset)


def reach_kernel(
    pos_ref, base_ref, tok_ref, wq_ref, gate_ref, k_ref, v_ref, inv_ref,
    q_ref, score_ref, rv_ref, y_ref, qt_ref, zv_ref, tokt_ref,
):
    half = tok_ref.shape[2] // 2
    columns = pl.ds(pl.multiple_of(pos_ref[0] * half, half), half)
    tokt_ref[...] = tok_ref[0, :, columns].astype(F32).T.astype(BF)
    q_all = jnp.dot(tok_ref[0], wq_ref[0], preferred_element_type=F32).astype(BF).astype(F32)
    n = q_all.shape[0]
    i, j = places(n)
    q_ref[...] = q_all
    for h in range(inv_ref.shape[0]):
        q = q_all[:, span(h)]
        k = k_ref[:, span(h)]
        _, e = rates_of(base_ref, gate_ref, h)
        score = dot(q, k, NT, 3)
        mix = jnp.where(i >= j, score * e, 0.0)
        inv = inv_ref[h]
        rv = dot(inv, v_ref[:, span(h)], NN, 3)
        y = dot(inv, k, NN, 3)
        score_ref[h] = score
        rv_ref[:, span(h)] = rv
        y_ref[:, span(h)] = y
        qt_ref[:, span(h)] = q - dot(mix, y, NN, 3)
        zv_ref[:, span(h)] = dot(mix, rv, NN, 3)


def step_kernel(d_ref, w_ref, o_ref, after_ref, out_ref, *, transposed):
    del after_ref
    for h in range(d_ref.shape[0]):
        out_ref[h] = o_ref[h] + dot(d_ref[h], w_ref[h], TN if transposed else NN, 3)


def norm_kernel(
    pos_ref, init_ref, near_ref, mid_ref, far_ref, rd_ref, qt_ref, zv_ref, up_ref, gain_ref, after_ref,
    w_ref, h_ref, p_ref, dgain_ref,
):
    del after_ref
    ctx = pos_ref[4]
    for h in range(init_ref.shape[0]):
        last = dot(rd_ref[h], far_ref[h], NN, 3) + near_ref[h]
        start = jnp.where(
            ctx == 0, init_ref[h], jnp.where(ctx == 1, near_ref[h], jnp.where(ctx == 2, mid_ref[h], last))
        )
        w_ref[h] = start
        qt = qt_ref[:, span(h)]
        z = dot(qt, start, NN, 3) + zv_ref[:, span(h)]
        up = up_ref[0, :, span(h)].astype(F32)
        centred = z - jnp.mean(z, -1, keepdims=True)
        inv_std = lax.rsqrt(jnp.mean(centred * centred, -1, keepdims=True) + 1e-05)
        normed = centred * inv_std
        weighted = up * gain_ref[h : h + 1, :]
        back = inv_std * (
            weighted
            - jnp.mean(weighted, -1, keepdims=True)
            - normed * jnp.mean(weighted * normed, -1, keepdims=True)
        )
        h_ref[:, span(h)] = back
        p_ref[h] = dot(qt, back, TN, 3)
        dgain_ref[h : h + 1, :] = jnp.sum(up * normed, axis=0, keepdims=True)


def query_kernel(
    base_ref, gate_ref, w_ref, h_ref, up_ref, q_ref, score_ref, rv_ref, y_ref, k_ref, inv_ref,
    dq_ref, r_ref, x_ref, dk_ref, de_ref,
):
    n = h_ref.shape[0]
    i, j = places(n)
    for h in range(w_ref.shape[0]):
        w = w_ref[h]
        back = h_ref[:, span(h)]
        k = k_ref[:, span(h)]
        q = q_ref[:, span(h)]
        score = score_ref[h]
        _, e = rates_of(base_ref, gate_ref, h)
        mix = jnp.where(i >= j, score * e, 0.0)
        r = rv_ref[:, span(h)] - dot(y_ref[:, span(h)], w, NN, 3)
        r_ref[:, span(h)] = r
        d_mix = jnp.where(i >= j, dot(back, r, NT, 3), 0.0)
        d_score = d_mix * e
        dq = up_ref[0, :, span(h)].astype(F32) + dot(back, w, NT, 3) + dot(d_score, k, NN, 3)
        dq_ref[:, span(h)] = dq.astype(BF).astype(F32)
        x_ref[:, span(h)] = dot(inv_ref[h], dot(mix, back, TN, 3), TN, 3)
        dk_ref[:, span(h)] = dot(d_score, q, TN, 3)
        de_ref[h : h + 1, :] = jnp.sum(d_mix * score, axis=0, keepdims=True)


def keys_kernel(
    pos_ref, base_ref, gate_ref, rp_ref, mid_ref, far_ref, rd_ref, p_ref, d_ref, w_ref, k_ref, ninv_ref,
    gram_ref, bt_ref, r_ref, x_ref, dk_ref, de_ref, dgain_ref, dq_ref,
    all_ref, gates_ref,
):
    ctx = pos_ref[4]
    n = k_ref.shape[0]
    i, j = places(n)
    strict = (i // MB) > (j // MB)
    all_ref[0:n, :] = dq_ref[...]
    all_ref[3 * n + HS : 3 * n + EXTRA, :] = jnp.zeros((EXTRA - HS, all_ref.shape[1]), F32)
    for h in range(w_ref.shape[0]):
        first = rp_ref[h] + dot(rd_ref[h], far_ref[h], TN, 3)
        end = jnp.where(
            ctx == 0, first, jnp.where(ctx == 1, mid_ref[h], jnp.where(ctx == 2, rp_ref[h], 0.0))
        )
        all_ref[3 * n : 3 * n + HS, span(h)] = jnp.where(ctx == 0, p_ref[h] + dot(d_ref[h], end, TN, 3), 0.0)
        w = w_ref[h]
        k = k_ref[:, span(h)]
        r = r_ref[:, span(h)]
        boost, e = rates_of(base_ref, gate_ref, h)
        x = x_ref[:, span(h)] + dot(bt_ref[h], end, TN, 3)
        all_ref[2 * n : 3 * n, span(h)] = x.astype(BF).astype(F32)
        d_low = jnp.where(strict, -dot(x, r, NT, 3), 0.0)
        d_gram = d_low * e
        dk = (
            dk_ref[:, span(h)]
            - dot(x, w, NT, 3)
            + to_col(e) * dot(r, end, NT, 3)
            + dot(d_gram + d_gram.T, k, NN, 3)
        )
        pull = to_row(jnp.sum(r * dot(k, end, NN, 3), axis=1, keepdims=True))
        de = de_ref[h : h + 1, :] + jnp.sum(d_low * gram_ref[h], axis=0, keepdims=True) + pull
        draw = ninv_ref[h] * (dk - k * jnp.sum(k * dk, -1, keepdims=True))
        all_ref[n : 2 * n, span(h)] = draw.astype(BF).astype(F32)
        d_boost = de / ((1.0 + boost) * (1.0 + boost))
        gates_ref[0, h : h + 1, :] = d_boost * base_ref[h]
        all_ref[3 * n + HS : 3 * n + HS + 1, span(h)] = dgain_ref[h : h + 1, :]
        all_ref[3 * n + HS + 1 : 3 * n + HS + 2, span(h)] = jnp.broadcast_to(
            jnp.sum(d_boost * gate_ref[0, h : h + 1, :], axis=1, keepdims=True), (1, HS)
        )


def turn_kernel(other_ref, out_ref):
    out_ref[...] = other_ref[...].T.astype(BF)


def product_kernel(pos_ref, tokt_ref, other_tokt_ref, own_ref, other_ref, *out_refs):
    n = tokt_ref.shape[1]
    for turn, out_ref in zip(TURNS, out_refs):
        at = (pos_ref[1] + turn) & (RING - 1)
        rows = pl.ds(pl.multiple_of(at * CHUNK, CHUNK), CHUNK)
        for m in range(3):
            out_ref[m * CHUNK : (m + 1) * CHUNK, :] = jnp.dot(
                tokt_ref[rows, :], own_ref[m * n : (m + 1) * n, :].astype(BF), preferred_element_type=F32
            ) + jnp.dot(
                other_tokt_ref[rows, :], other_ref[m * n : (m + 1) * n, :].astype(BF), preferred_element_type=F32
            )
        extra = pl.ds(pl.multiple_of(3 * n + (pos_ref[0] * RING + at) * PIECE, 8), PIECE)
        out_ref[3 * CHUNK : 3 * CHUNK + PIECE, :] = own_ref[extra, :] + other_ref[extra, :]


def token_kernel(pos_ref, w_ref, all_ref, *out_refs):
    n = out_refs[0].shape[0]
    ds = [all_ref[m * n : (m + 1) * n, :].astype(BF) for m in range(3)]
    quarter = w_ref.shape[1] // RING
    for turn, out_ref in zip(TURNS, out_refs):
        at = (pos_ref[3] + turn) & (RING - 1)
        rows = pl.ds(pl.multiple_of(at * quarter, quarter), quarter)
        total = lax.dot_general(ds[0], w_ref[0, rows, :], NT, preferred_element_type=F32)
        total = total + lax.dot_general(ds[1], w_ref[1, rows, :], NT, preferred_element_type=F32)
        out_ref[...] = total + lax.dot_general(ds[2], w_ref[2, rows, :], NT, preferred_element_type=F32)


def slice_rows(pos_ref, turn):
    at = (pos_ref[2] + turn) & (RING - 1)
    taken = [
        (pl.ds(pl.multiple_of(m * CHUNK + at * SLICE, SLICE), SLICE), slice(m * SLICE, (m + 1) * SLICE))
        for m in range(3)
    ]
    few = PIECE // RING
    extra = pl.ds(pl.multiple_of(3 * CHUNK + at * few, few), few)
    return taken + [(extra, slice(3 * SLICE, 3 * SLICE + few))]


def split_kernel(pos_ref, own_ref, back_ref, ahead_ref, far_ref, *refs):
    for turn, out_ref in zip(TURNS, refs[-RING:]):
        for rows, to in slice_rows(pos_ref, turn):
            out_ref[to, :] = (own_ref[rows, :] + far_ref[rows, :]) + (back_ref[rows, :] + ahead_ref[rows, :])


def sum_kernel(own_ref, back_ref, ahead_ref, far_ref, out_ref):
    out_ref[...] = (own_ref[...] + far_ref[...]) + (back_ref[...] + ahead_ref[...])


def join_kernel(pos_ref, own_ref, ahead_ref, back_ref, far_ref, *refs):
    for turn, part_ref in zip(TURNS, (own_ref, ahead_ref, back_ref, far_ref)):
        for rows, to in slice_rows(pos_ref, turn):
            refs[-1][rows, :] = part_ref[to, :]


def place_kernel(pos_ref, *refs, which):
    pieces = refs[: len(which)]
    out_ref, sem = refs[len(refs) - 3 if len(refs) == len(which) + 4 else -2], refs[-1]
    copies = []
    for g, ((half, m), piece) in enumerate(zip(which, pieces)):
        core = pos_ref[0] if half == 0 else 1 - pos_ref[0]
        at = core * RING + ((pos_ref[1 + half] + TURNS[m]) & (RING - 1))
        rows = pl.ds(pl.multiple_of(at * CHUNK, CHUNK), CHUNK)
        for s in range(3):
            copies.append(
                pltpu.make_async_copy(piece.at[pl.ds(s * CHUNK, CHUNK), :], out_ref.at[s, rows, :], sem.at[s, g])
            )
    for copy in copies:
        copy.start()
    for copy in copies:
        copy.wait()


def last_kernel(pos_ref, *refs, which):
    pieces = refs[: 2 * RING]
    out_ref, init_ref, gain_ref, rates_ref, extra_ref, sem = refs[-6:]
    copies = []
    for g, (half, m) in enumerate(which):
        core = pos_ref[0] if half == 0 else 1 - pos_ref[0]
        at = core * RING + ((pos_ref[1 + half] + TURNS[m]) & (RING - 1))
        rows = pl.ds(pl.multiple_of(at * CHUNK, CHUNK), CHUNK)
        for s in range(3):
            copies.append(
                pltpu.make_async_copy(
                    pieces[half * RING + m].at[pl.ds(s * CHUNK, CHUNK), :], out_ref.at[s, rows, :], sem.at[s, g]
                )
            )
    for copy in copies:
        copy.start()
    for p, piece in enumerate(pieces):
        core = pos_ref[0] if p < RING else 1 - pos_ref[0]
        at = core * RING + ((pos_ref[1 + p // RING] + TURNS[p % RING]) & (RING - 1))
        extra_ref[pl.ds(pl.multiple_of(at * PIECE, 8), PIECE), :] = piece[3 * CHUNK : 3 * CHUNK + PIECE, :]
    for h in range(init_ref.shape[0]):
        init_ref[h] = extra_ref[0:HS, span(h)]
        gain_ref[h : h + 1, :] = extra_ref[HS : HS + 1, span(h)]
        rates_ref[h] = extra_ref[HS + 1, h * HS]
    for copy in copies:
        copy.wait()


def moves(first, by):
    pairs = []
    for x in range(RING):
        for core in range(2):
            for y in range(RING):
                along_x = (core == 0) == first
                to_x = (x + by) % RING if along_x else x
                to_y = y if along_x else (y + by) % RING
                pairs.append(((x * 2 + core) * RING + y, (to_x * 2 + core) * RING + to_y))
    return pairs


def round_turn(chunks, first):
    return [
        lax.ppermute(chunk, ("dp", "ctx"), moves(first, turn)) for chunk, turn in zip(chunks, TURNS[1:])
    ]


def swap(value):
    return lax.ppermute(value, "dp", [(i, i ^ 1) for i in range(2 * RING)])


VM = pl.BlockSpec(memory_space=pltpu.VMEM)
SM = pl.BlockSpec(memory_space=pltpu.SMEM)
PARAMS = pltpu.CompilerParams(vmem_limit_bytes=20 * 1024 * 1024)


def shape(*dims, dtype=F32):
    return jax.ShapeDtypeStruct(dims, dtype)


def vmem(*dims, dtype=F32):
    return pltpu.VMEM(dims, dtype)


def hbm(value):
    return pltpu.with_memory_space_constraint(value, pltpu.HBM)


def whole(kernel, outs, specs):
    return pl.pallas_call(
        kernel,
        out_shape=outs,
        in_specs=specs,
        out_specs=tuple(VM for _ in outs) if isinstance(outs, tuple) else VM,
        compiler_params=PARAMS,
    )


def part(which, dims):
    return pl.BlockSpec((1,) + dims, lambda i: (which, 0, 0))


def full(*dims):
    return pl.BlockSpec(dims, lambda i: (0,) * len(dims))


def body(tokens, proj_weights, init_weight, base_rates, gate_values, out_gain, cotangent):
    n = tokens.shape[1]
    model = tokens.shape[2]
    heads = init_weight.shape[0]
    wide = heads * HS
    ctx = lax.axis_index("ctx")
    dp = lax.axis_index("dp")
    core, x_at = dp % 2, dp // 2
    pos = jnp.stack(
        [core, jnp.where(core == 0, x_at, ctx), jnp.where(core == 0, ctx, x_at), lax.axis_index("head"), ctx]
    ).astype(jnp.int32)
    half = model // 2

    wide_f32 = vmem(n, wide)
    square = vmem(heads, n, n)
    small = vmem(heads, HS, HS)
    wspec = functools.partial(part, dims=(model, wide))
    tokens = hbm(tokens)
    raw_weights = proj_weights
    proj_weights = hbm(proj_weights)
    anywhere = pl.BlockSpec(memory_space=pl.ANY)

    k, v, ninv, gram, inv, bt, decay, send, offset, other_half = pl.pallas_call(
        maps_kernel,
        grid=(1,),
        out_shape=(
            wide_f32, wide_f32, vmem(heads, n, HS), square, square, vmem(heads, HS, n), small, small, small,
            vmem(n, half),
        ),
        in_specs=[SM, SM, full(1, n, model), wspec(1), wspec(2), full(1, heads, n), full(heads, HS, HS)],
        out_specs=(VM,) * 10,
        compiler_params=PARAMS,
    )(pos, hbm(base_rates), tokens, proj_weights, proj_weights, hbm(gate_values), hbm(init_weight))

    near = lax.ppermute(send, "ctx", [(0, 1), (2, 3)])
    moved = lax.ppermute(decay, "ctx", [(2, 3), (1, 0)])
    got_half = swap(other_half)

    q, score, rv, y, qt, zv, tokt = pl.pallas_call(
        reach_kernel,
        grid=(1,),
        out_shape=(wide_f32, square, wide_f32, wide_f32, wide_f32, wide_f32, vmem(half, n, dtype=BF)),
        in_specs=[SM, SM, full(1, n, model), wspec(0), full(1, heads, n), VM, VM, VM],
        out_specs=(VM,) * 7,
        compiler_params=PARAMS,
    )(pos, base_rates, tokens, proj_weights, gate_values, k, v, inv)

    second = whole(functools.partial(step_kernel, transposed=False), small, [VM] * 3 + [anywhere])(
        decay, near, offset, qt
    )
    mid = lax.ppermute(second, "ctx", [(1, 2)])
    far = lax.ppermute(second, "ctx", [(1, 3)])
    other_tokt = whole(turn_kernel, vmem(half, n, dtype=BF), [VM])(got_half)

    w, back, pulled, dgain = whole(
        norm_kernel, (small, wide_f32, small, vmem(heads, HS)), [SM] + [VM] * 9 + [anywhere]
    )(pos, init_weight, near, mid, far, moved, qt, zv, cotangent, out_gain, other_tokt)

    back_near = lax.ppermute(pulled, "ctx", [(3, 2), (1, 0)])

    dq, r, x, dk, de = whole(
        query_kernel, (wide_f32, wide_f32, wide_f32, wide_f32, vmem(heads, n)), [SM] + [VM] * 10
    )(base_rates, gate_values, w, back, cotangent, q, score, rv, y, k, inv)

    back_second = whole(functools.partial(step_kernel, transposed=True), small, [VM] * 3 + [anywhere])(
        decay, back_near, pulled, de
    )
    back_mid = lax.ppermute(back_second, "ctx", [(2, 1)])
    back_far = lax.ppermute(back_second, "ctx", [(2, 0)])

    grads, grad_gates = whole(
        keys_kernel, (vmem(3 * n + EXTRA, wide), shape(1, heads, n)), [SM, SM] + [VM] * 18
    )(pos, base_rates, gate_values, back_near, back_mid, back_far, moved, pulled, decay, w, k, ninv, gram, bt, r, x,
      dk, de, dgain, dq)

    chunk = vmem(3 * CHUNK + PIECE, wide)
    own, *away = whole(product_kernel, (chunk,) * RING, [SM] + [VM] * 4)(
        pos, tokt, other_tokt, grads, swap(grads)
    )
    away = round_turn(away, True)
    quarters = whole(token_kernel, (vmem(n, model // RING),) * RING, [SM, VM, VM])(pos, raw_weights, grads)
    from_back, from_ahead, from_far = [
        lax.ppermute(terms, "head", [(i, (i + turn) % RING) for i in range(RING)])
        for terms, turn in zip(quarters[1:], TURNS[1:])
    ]
    grad_tokens = ((quarters[0] + from_far) + (from_back + from_ahead)).astype(BF).reshape(1, n, -1)

    piece = vmem(3 * SLICE + PIECE // RING, wide)
    own, *away = whole(split_kernel, (piece,) * RING, [SM] + [VM] * 4 + [anywhere] * 2)(
        pos, own, *away, from_back, from_ahead
    )
    part_sum = whole(sum_kernel, piece, [VM] * 4)(own, *round_turn(away, False))
    from_back, from_ahead, from_far = round_turn([part_sum] * 3, False)
    total = whole(join_kernel, chunk, [SM] + [VM] * 4 + [anywhere])(
        pos, part_sum, from_ahead, from_back, from_far, grad_tokens
    )
    from_back, from_ahead, from_far = round_turn([total] * 3, True)
    out = shape(3, model, wide)

    def place(which, extra, extra_out, extra_spec, aliases):
        given = [(mine, others)[half][m] for half, m in which]
        return pl.pallas_call(
            functools.partial(place_kernel, which=which),
            out_shape=(out,) + extra_out,
            in_specs=[SM] + [VM] * len(given) + [extra_spec],
            out_specs=(anywhere,) + (VM,) * len(extra_out),
            scratch_shapes=[pltpu.SemaphoreType.DMA((3, len(which)))],
            input_output_aliases={len(given) + 1: aliases},
            compiler_params=PARAMS,
        )(pos, *given, extra)

    mine = [total, from_ahead, from_back, from_far]
    others = [swap(total)]
    placed, mine[3] = place(((0, 0), (1, 0)), from_far, (chunk,), VM, 1)
    others += [swap(given) for given in mine[1:]]
    (placed,) = place(((0, 1), (0, 2), (0, 3), (1, 3)), placed, (), anywhere, 0)
    which = ((1, 1), (1, 2))
    grad_proj, grad_init, grad_gain, grad_rates = pl.pallas_call(
        functools.partial(last_kernel, which=which),
        out_shape=(out, shape(heads, HS, HS), shape(heads, HS), shape(heads)),
        in_specs=[SM] + [VM] * 8 + [anywhere],
        out_specs=(anywhere, VM, VM, SM),
        scratch_shapes=[pltpu.VMEM((EXTRA, wide), F32), pltpu.SemaphoreType.DMA((3, len(which)))],
        input_output_aliases={9: 0},
        compiler_params=PARAMS,
    )(pos, *mine, *others, placed)
    return (grad_tokens, grad_proj, grad_init, grad_gain, grad_rates, grad_gates)


def solution(mesh):
    in_specs = (
        P("dp", "ctx", None),
        P(None, None, "head"),
        P("head", None, None),
        P("head"),
        P("dp", "head", "ctx"),
        P("head", None),
        P("dp", "ctx", "head"),
    )
    out_specs = (
        P("dp", "ctx", "head"),
        P(None, None, "head"),
        P("head", None, None),
        P("head", None),
        P("head"),
        P("dp", "head", "ctx"),
    )
    return jax.shard_map(body, mesh=mesh, in_specs=in_specs, out_specs=out_specs, check_vma=False)
```

```python
import functools

import jax
import jax.numpy as jnp
from jax import lax
from jax.experimental import pallas as pl
from jax.experimental.pallas import tpu as pltpu
from jax.sharding import PartitionSpec as P

MB = 16
HS = 128
RING = 4
TURNS = (0, 1, 3, 2)
CHUNK = 256
SLICE = CHUNK // RING
PIECE = 32
EXTRA = 2 * RING * PIECE
F32 = jnp.float32
BF = jnp.bfloat16
NN = (((1,), (0,)), ((), ()))
NT = (((1,), (1,)), ((), ()))
TN = (((0,), (0,)), ((), ()))


def dot(a, b, dims, passes):
    ah = a.astype(BF)
    bh = b.astype(BF)
    result = lax.dot_general(ah, bh, dims, preferred_element_type=F32)
    if passes == 3:
        al = (a - ah.astype(F32)).astype(BF)
        bl = (b - bh.astype(F32)).astype(BF)
        result = result + (
            lax.dot_general(ah, bl, dims, preferred_element_type=F32)
            + lax.dot_general(al, bh, dims, preferred_element_type=F32)
        )
    return result


def places(n):
    return (
        lax.broadcasted_iota(jnp.int32, (n, n), 0),
        lax.broadcasted_iota(jnp.int32, (n, n), 1),
    )


def to_col(row):
    i, j = places(row.shape[1])
    return jnp.sum(jnp.where(i == j, row, 0.0), axis=1, keepdims=True)


def to_row(col):
    i, j = places(col.shape[0])
    return jnp.sum(jnp.where(i == j, col, 0.0), axis=0, keepdims=True)


def unit_lower_inverses(lowers):
    n = lowers[0].shape[0]
    i, j = places(n)
    size = 2 * MB
    same = (i // size) == (j // size)
    inverses = [jnp.where(i == j, 1.0, 0.0) - jnp.where(same, low, 0.0) for low in lowers]
    while size < n:
        pair = ((i // (2 * size)) == (j // (2 * size))) & ((i // size) != (j // size))
        corners = [jnp.where(pair, low, 0.0) for low in lowers]
        halves = [dot(inv, corner, NN, 3) for inv, corner in zip(inverses, corners)]
        inverses = [inv - dot(half, inv, NN, 3) for inv, half in zip(inverses, halves)]
        size *= 2
    return inverses


def span(h):
    return slice(h * HS, (h + 1) * HS)


def rates_of(base_ref, gate_ref, h):
    boost = base_ref[h] * gate_ref[0, h : h + 1, :]
    return boost, boost / (1.0 + boost)


def maps_kernel(
    pos_ref, base_ref, tok_ref, wk_ref, wv_ref, gate_ref, init_ref,
    k_ref, v_ref, ninv_ref, gram_ref, inv_ref, bt_ref, d_ref, send_ref, o_ref, half_ref,
):
    half = tok_ref.shape[2] // 2
    columns = pl.ds(pl.multiple_of((1 - pos_ref[0]) * half, half), half)
    half_ref[...] = tok_ref[0, :, columns].astype(F32)
    tok = tok_ref[0]
    kraw_all = jnp.dot(tok, wk_ref[0], preferred_element_type=F32).astype(BF).astype(F32)
    v_all = jnp.dot(tok, wv_ref[0], preferred_element_type=F32).astype(BF).astype(F32)
    n = kraw_all.shape[0]
    i, j = places(n)
    strict = (i // MB) > (j // MB)
    heads = range(init_ref.shape[0])
    ks, kts, es, lows = [], [], [], []
    for h in heads:
        kraw = kraw_all[:, span(h)]
        ninv = lax.rsqrt(jnp.sum(kraw * kraw, -1, keepdims=True) + 1e-06)
        k = kraw * ninv
        kt = k.T
        _, e = rates_of(base_ref, gate_ref, h)
        gram = dot(k, kt, NN, 3)
        ninv_ref[h] = jnp.broadcast_to(ninv, (n, HS))
        k_ref[:, span(h)] = k
        gram_ref[h] = gram
        ks.append(k)
        kts.append(kt)
        es.append(e)
        lows.append(jnp.where(strict, gram * e, 0.0))
    v_ref[...] = v_all
    inverses = unit_lower_inverses(lows)
    a, b = places(HS)
    for h in heads:
        bt = dot(kts[h] * es[h], inverses[h], NN, 3)
        inv_ref[h] = inverses[h]
        bt_ref[h] = bt
        decay = jnp.where(a == b, 1.0, 0.0) - dot(bt, ks[h], NN, 3)
        offset = dot(bt, v_all[:, span(h)], NN, 3)
        d_ref[h] = decay
        o_ref[h] = offset
        first = dot(decay, init_ref[h], NN, 3) + offset
        send_ref[h] = jnp.where(pos_ref[4] == 0, first, offset)


def reach_kernel(
    pos_ref, base_ref, tok_ref, wq_ref, gate_ref, k_ref, v_ref, inv_ref,
    q_ref, score_ref, rv_ref, y_ref, qt_ref, zv_ref, tokt_ref,
):
    half = tok_ref.shape[2] // 2
    columns = pl.ds(pl.multiple_of(pos_ref[0] * half, half), half)
    tokt_ref[...] = tok_ref[0, :, columns].astype(F32).T.astype(BF)
    q_all = jnp.dot(tok_ref[0], wq_ref[0], preferred_element_type=F32).astype(BF).astype(F32)
    n = q_all.shape[0]
    i, j = places(n)
    q_ref[...] = q_all
    for h in range(inv_ref.shape[0]):
        q = q_all[:, span(h)]
        k = k_ref[:, span(h)]
        _, e = rates_of(base_ref, gate_ref, h)
        score = dot(q, k, NT, 3)
        mix = jnp.where(i >= j, score * e, 0.0)
        inv = inv_ref[h]
        rv = dot(inv, v_ref[:, span(h)], NN, 3)
        y = dot(inv, k, NN, 3)
        score_ref[h] = score
        rv_ref[:, span(h)] = rv
        y_ref[:, span(h)] = y
        qt_ref[:, span(h)] = q - dot(mix, y, NN, 3)
        zv_ref[:, span(h)] = dot(mix, rv, NN, 3)


def step_kernel(d_ref, w_ref, o_ref, after_ref, out_ref):
    del after_ref
    for h in range(d_ref.shape[0]):
        out_ref[h] = o_ref[h] + dot(d_ref[h], w_ref[h], NN, 3)


def norm_kernel(
    pos_ref, init_ref, near_ref, mid_ref, far_ref, rd_ref, qt_ref, zv_ref, up_ref, gain_ref, after_ref,
    w_ref, h_ref, p_ref, dgain_ref,
):
    del after_ref
    ctx = pos_ref[4]
    for h in range(init_ref.shape[0]):
        last = dot(rd_ref[h], far_ref[h], NN, 3) + near_ref[h]
        start = jnp.where(
            ctx == 0, init_ref[h], jnp.where(ctx == 1, near_ref[h], jnp.where(ctx == 2, mid_ref[h], last))
        )
        w_ref[h] = start
        qt = qt_ref[:, span(h)]
        z = dot(qt, start, NN, 3) + zv_ref[:, span(h)]
        up = up_ref[0, :, span(h)].astype(F32)
        centred = z - jnp.mean(z, -1, keepdims=True)
        inv_std = lax.rsqrt(jnp.mean(centred * centred, -1, keepdims=True) + 1e-05)
        normed = centred * inv_std
        weighted = up * gain_ref[h : h + 1, :]
        back = inv_std * (
            weighted
            - jnp.mean(weighted, -1, keepdims=True)
            - normed * jnp.mean(weighted * normed, -1, keepdims=True)
        )
        h_ref[:, span(h)] = back
        p_ref[h] = dot(qt, back, TN, 3)
        dgain_ref[h : h + 1, :] = jnp.sum(up * normed, axis=0, keepdims=True)


def query_kernel(
    base_ref, gate_ref, w_ref, h_ref, up_ref, q_ref, score_ref, rv_ref, y_ref, k_ref, inv_ref,
    dq_ref, r_ref, x_ref, dk_ref, de_ref,
):
    n = h_ref.shape[0]
    i, j = places(n)
    for h in range(w_ref.shape[0]):
        w = w_ref[h]
        back = h_ref[:, span(h)]
        k = k_ref[:, span(h)]
        q = q_ref[:, span(h)]
        score = score_ref[h]
        _, e = rates_of(base_ref, gate_ref, h)
        mix = jnp.where(i >= j, score * e, 0.0)
        r = rv_ref[:, span(h)] - dot(y_ref[:, span(h)], w, NN, 3)
        r_ref[:, span(h)] = r
        d_mix = jnp.where(i >= j, dot(back, r, NT, 3), 0.0)
        d_score = d_mix * e
        dq = up_ref[0, :, span(h)].astype(F32) + dot(back, w, NT, 3) + dot(d_score, k, NN, 3)
        dq_ref[:, span(h)] = dq.astype(BF).astype(F32)
        x_ref[:, span(h)] = dot(inv_ref[h], dot(mix, back, TN, 3), TN, 3)
        dk_ref[:, span(h)] = dot(d_score, q, TN, 3)
        de_ref[h : h + 1, :] = jnp.sum(d_mix * score, axis=0, keepdims=True)


def keys_kernel(
    pos_ref, base_ref, gate_ref, one_ref, two_ref, three_ref, rd_ref, rd_one_ref, rd_two_ref, p_ref, d_ref, w_ref, k_ref, ninv_ref,
    gram_ref, bt_ref, r_ref, x_ref, dk_ref, de_ref, dgain_ref, dq_ref,
    all_ref, gates_ref,
):
    ctx = pos_ref[4]
    n = k_ref.shape[0]
    i, j = places(n)
    strict = (i // MB) > (j // MB)
    all_ref[0:n, :] = dq_ref[...]
    all_ref[3 * n + HS : 3 * n + EXTRA, :] = jnp.zeros((EXTRA - HS, all_ref.shape[1]), F32)
    for h in range(w_ref.shape[0]):
        step = jnp.where(ctx == 0, rd_ref[h], rd_one_ref[h])
        end = one_ref[h] + dot(step, two_ref[h] + dot(rd_two_ref[h], three_ref[h], TN, 3), TN, 3)
        all_ref[3 * n : 3 * n + HS, span(h)] = jnp.where(ctx == 0, p_ref[h] + dot(d_ref[h], end, TN, 3), 0.0)
        w = w_ref[h]
        k = k_ref[:, span(h)]
        r = r_ref[:, span(h)]
        boost, e = rates_of(base_ref, gate_ref, h)
        x = x_ref[:, span(h)] + dot(bt_ref[h], end, TN, 3)
        all_ref[2 * n : 3 * n, span(h)] = x.astype(BF).astype(F32)
        d_low = jnp.where(strict, -dot(x, r, NT, 3), 0.0)
        d_gram = d_low * e
        dk = (
            dk_ref[:, span(h)]
            - dot(x, w, NT, 3)
            + to_col(e) * dot(r, end, NT, 3)
            + dot(d_gram + d_gram.T, k, NN, 3)
        )
        pull = to_row(jnp.sum(r * dot(k, end, NN, 3), axis=1, keepdims=True))
        de = de_ref[h : h + 1, :] + jnp.sum(d_low * gram_ref[h], axis=0, keepdims=True) + pull
        draw = ninv_ref[h] * (dk - k * jnp.sum(k * dk, -1, keepdims=True))
        all_ref[n : 2 * n, span(h)] = draw.astype(BF).astype(F32)
        d_boost = de / ((1.0 + boost) * (1.0 + boost))
        gates_ref[0, h : h + 1, :] = d_boost * base_ref[h]
        all_ref[3 * n + HS : 3 * n + HS + 1, span(h)] = dgain_ref[h : h + 1, :]
        all_ref[3 * n + HS + 1 : 3 * n + HS + 2, span(h)] = jnp.broadcast_to(
            jnp.sum(d_boost * gate_ref[0, h : h + 1, :], axis=1, keepdims=True), (1, HS)
        )


def turn_kernel(other_ref, out_ref):
    out_ref[...] = other_ref[...].T.astype(BF)


def product_kernel(pos_ref, tokt_ref, other_tokt_ref, own_ref, other_ref, *refs):
    out_refs = refs[2 : 2 + RING]
    n = tokt_ref.shape[1]
    for turn, out_ref in zip(TURNS, out_refs):
        at = (pos_ref[1] + turn) & (RING - 1)
        rows = pl.ds(pl.multiple_of(at * CHUNK, CHUNK), CHUNK)
        for m in range(3):
            out_ref[m * CHUNK : (m + 1) * CHUNK, :] = jnp.dot(
                tokt_ref[rows, :], own_ref[m * n : (m + 1) * n, :].astype(BF), preferred_element_type=F32
            ) + jnp.dot(
                other_tokt_ref[rows, :], other_ref[m * n : (m + 1) * n, :].astype(BF), preferred_element_type=F32
            )
        extra = pl.ds(pl.multiple_of(3 * n + (pos_ref[0] * RING + at) * PIECE, 8), PIECE)
        out_ref[3 * CHUNK : 3 * CHUNK + PIECE, :] = own_ref[extra, :] + other_ref[extra, :]


def token_kernel(pos_ref, w_ref, all_ref, *out_refs):
    n = out_refs[0].shape[0]
    ds = [all_ref[m * n : (m + 1) * n, :].astype(BF) for m in range(3)]
    quarter = w_ref.shape[1] // RING
    for turn, out_ref in zip(TURNS, out_refs):
        at = (pos_ref[3] + turn) & (RING - 1)
        rows = pl.ds(pl.multiple_of(at * quarter, quarter), quarter)
        total = lax.dot_general(ds[0], w_ref[0, rows, :], NT, preferred_element_type=F32)
        total = total + lax.dot_general(ds[1], w_ref[1, rows, :], NT, preferred_element_type=F32)
        out_ref[...] = total + lax.dot_general(ds[2], w_ref[2, rows, :], NT, preferred_element_type=F32)


def slice_rows(pos_ref, turn):
    at = (pos_ref[2] + turn) & (RING - 1)
    taken = [
        (pl.ds(pl.multiple_of(m * CHUNK + at * SLICE, SLICE), SLICE), slice(m * SLICE, (m + 1) * SLICE))
        for m in range(3)
    ]
    few = PIECE // RING
    extra = pl.ds(pl.multiple_of(3 * CHUNK + at * few, few), few)
    return taken + [(extra, slice(3 * SLICE, 3 * SLICE + few))]


def split_kernel(pos_ref, own_ref, back_ref, ahead_ref, far_ref, *refs):
    for turn, out_ref in zip(TURNS, refs[3 : 3 + RING]):
        for rows, to in slice_rows(pos_ref, turn):
            out_ref[to, :] = (own_ref[rows, :] + far_ref[rows, :]) + (back_ref[rows, :] + ahead_ref[rows, :])


def sum_kernel(own_ref, back_ref, ahead_ref, far_ref, out_ref):
    out_ref[...] = (own_ref[...] + far_ref[...]) + (back_ref[...] + ahead_ref[...])


def join_kernel(pos_ref, own_ref, ahead_ref, back_ref, far_ref, *refs):
    for turn, part_ref in zip(TURNS, (own_ref, ahead_ref, back_ref, far_ref)):
        for rows, to in slice_rows(pos_ref, turn):
            refs[-1][rows, :] = part_ref[to, :]


def place_kernel(pos_ref, *refs, which):
    pieces = refs[: len(which)]
    out_ref, sem = refs[len(refs) - 3 if len(refs) == len(which) + 4 else -2], refs[-1]
    copies = []
    for g, ((half, m), piece) in enumerate(zip(which, pieces)):
        core = pos_ref[0] if half == 0 else 1 - pos_ref[0]
        at = core * RING + ((pos_ref[1 + half] + TURNS[m]) & (RING - 1))
        rows = pl.ds(pl.multiple_of(at * CHUNK, CHUNK), CHUNK)
        for s in range(3):
            copies.append(
                pltpu.make_async_copy(piece.at[pl.ds(s * CHUNK, CHUNK), :], out_ref.at[s, rows, :], sem.at[s, g])
            )
    for copy in copies:
        copy.start()
    for copy in copies:
        copy.wait()


def last_kernel(pos_ref, *refs, which):
    pieces = refs[: 2 * RING]
    out_ref, init_ref, gain_ref, rates_ref, extra_ref, sem = refs[-6:]
    copies = []
    for g, (half, m) in enumerate(which):
        core = pos_ref[0] if half == 0 else 1 - pos_ref[0]
        at = core * RING + ((pos_ref[1 + half] + TURNS[m]) & (RING - 1))
        rows = pl.ds(pl.multiple_of(at * CHUNK, CHUNK), CHUNK)
        for s in range(3):
            copies.append(
                pltpu.make_async_copy(
                    pieces[half * RING + m].at[pl.ds(s * CHUNK, CHUNK), :], out_ref.at[s, rows, :], sem.at[s, g]
                )
            )
    for copy in copies:
        copy.start()
    for p, piece in enumerate(pieces):
        core = pos_ref[0] if p < RING else 1 - pos_ref[0]
        at = core * RING + ((pos_ref[1 + p // RING] + TURNS[p % RING]) & (RING - 1))
        extra_ref[pl.ds(pl.multiple_of(at * PIECE, 8), PIECE), :] = piece[3 * CHUNK : 3 * CHUNK + PIECE, :]
    for h in range(init_ref.shape[0]):
        init_ref[h] = extra_ref[0:HS, span(h)]
        gain_ref[h : h + 1, :] = extra_ref[HS : HS + 1, span(h)]
        rates_ref[h] = extra_ref[HS + 1, h * HS]
    for copy in copies:
        copy.wait()


def moves(first, by):
    pairs = []
    for x in range(RING):
        for core in range(2):
            for y in range(RING):
                along_x = (core == 0) == first
                to_x = (x + by) % RING if along_x else x
                to_y = y if along_x else (y + by) % RING
                pairs.append(((x * 2 + core) * RING + y, (to_x * 2 + core) * RING + to_y))
    return pairs


def round_turn(chunks, first):
    return [
        lax.ppermute(chunk, ("dp", "ctx"), moves(first, turn)) for chunk, turn in zip(chunks, TURNS[1:])
    ]


def swap(value):
    return lax.ppermute(value, "dp", [(i, i ^ 1) for i in range(2 * RING)])


VM = pl.BlockSpec(memory_space=pltpu.VMEM)
SM = pl.BlockSpec(memory_space=pltpu.SMEM)
PARAMS = pltpu.CompilerParams(vmem_limit_bytes=20 * 1024 * 1024)


def shape(*dims, dtype=F32):
    return jax.ShapeDtypeStruct(dims, dtype)


def vmem(*dims, dtype=F32):
    return pltpu.VMEM(dims, dtype)


def hbm(value):
    return pltpu.with_memory_space_constraint(value, pltpu.HBM)


def whole(kernel, outs, specs, aliases=None):
    return pl.pallas_call(
        kernel,
        out_shape=outs,
        in_specs=specs,
        out_specs=tuple(VM for _ in outs) if isinstance(outs, tuple) else VM,
        input_output_aliases=aliases or {},
        compiler_params=PARAMS,
    )


def part(which, dims):
    return pl.BlockSpec((1,) + dims, lambda i: (which, 0, 0))


def full(*dims):
    return pl.BlockSpec(dims, lambda i: (0,) * len(dims))


def body(tokens, proj_weights, init_weight, base_rates, gate_values, out_gain, cotangent):
    n = tokens.shape[1]
    model = tokens.shape[2]
    heads = init_weight.shape[0]
    wide = heads * HS
    ctx = lax.axis_index("ctx")
    dp = lax.axis_index("dp")
    core, x_at = dp % 2, dp // 2
    pos = jnp.stack(
        [core, jnp.where(core == 0, x_at, ctx), jnp.where(core == 0, ctx, x_at), lax.axis_index("head"), ctx]
    ).astype(jnp.int32)
    half = model // 2

    wide_f32 = vmem(n, wide)
    square = vmem(heads, n, n)
    small = vmem(heads, HS, HS)
    wspec = functools.partial(part, dims=(model, wide))
    tokens = hbm(tokens)
    raw_weights = proj_weights
    proj_weights = hbm(proj_weights)
    anywhere = pl.BlockSpec(memory_space=pl.ANY)

    k, v, ninv, gram, inv, bt, decay, send, offset, other_half = pl.pallas_call(
        maps_kernel,
        grid=(1,),
        out_shape=(
            wide_f32, wide_f32, vmem(heads, n, HS), square, square, vmem(heads, HS, n), small, small, small,
            vmem(n, half),
        ),
        in_specs=[SM, SM, full(1, n, model), wspec(1), wspec(2), full(1, heads, n), full(heads, HS, HS)],
        out_specs=(VM,) * 10,
        compiler_params=PARAMS,
    )(pos, hbm(base_rates), tokens, proj_weights, proj_weights, hbm(gate_values), hbm(init_weight))

    near = lax.ppermute(send, "ctx", [(0, 1), (2, 3)])
    moved = lax.ppermute(decay, "ctx", [(2, 3), (1, 0)])
    moved_one = lax.ppermute(decay, "ctx", [(2, 1)])
    moved_two = lax.ppermute(decay, "ctx", [(2, 0)])
    got_half = swap(other_half)

    q, score, rv, y, qt, zv, tokt = pl.pallas_call(
        reach_kernel,
        grid=(1,),
        out_shape=(wide_f32, square, wide_f32, wide_f32, wide_f32, wide_f32, vmem(half, n, dtype=BF)),
        in_specs=[SM, SM, full(1, n, model), wspec(0), full(1, heads, n), VM, VM, VM],
        out_specs=(VM,) * 7,
        compiler_params=PARAMS,
    )(pos, base_rates, tokens, proj_weights, gate_values, k, v, inv)

    second = whole(step_kernel, small, [VM] * 3 + [anywhere])(
        decay, near, offset, qt
    )
    mid = lax.ppermute(second, "ctx", [(1, 2)])
    far = lax.ppermute(second, "ctx", [(1, 3)])
    other_tokt = whole(turn_kernel, vmem(half, n, dtype=BF), [VM])(got_half)

    w, back, pulled, dgain = whole(
        norm_kernel, (small, wide_f32, small, vmem(heads, HS)), [SM] + [VM] * 9 + [anywhere]
    )(pos, init_weight, near, mid, far, moved, qt, zv, cotangent, out_gain, other_tokt)

    back_one = lax.ppermute(pulled, "ctx", [(3, 2), (2, 1), (1, 0)])
    back_two = lax.ppermute(pulled, "ctx", [(3, 1), (2, 0)])
    back_three = lax.ppermute(pulled, "ctx", [(3, 0)])

    dq, r, x, dk, de = whole(
        query_kernel, (wide_f32, wide_f32, wide_f32, wide_f32, vmem(heads, n)), [SM] + [VM] * 10
    )(base_rates, gate_values, w, back, cotangent, q, score, rv, y, k, inv)

    grads, grad_gates = whole(
        keys_kernel, (vmem(3 * n + EXTRA, wide), shape(1, heads, n)), [SM, SM] + [VM] * 20
    )(pos, base_rates, gate_values, back_one, back_two, back_three, moved, moved_one, moved_two, pulled, decay, w, k, ninv, gram, bt, r, x,
      dk, de, dgain, dq)

    chunk = vmem(3 * CHUNK + PIECE, wide)
    quarter = vmem(n, model // RING)
    quarters = whole(token_kernel, (quarter,) * RING, [SM, VM, VM])(pos, raw_weights, grads)

    def along_head(terms, turn):
        return lax.ppermute(terms, "head", [(i, (i + turn) % RING) for i in range(RING)])

    *chunks, near_one, near_two = whole(
        product_kernel, (chunk,) * RING + (quarter,) * 2, [SM] + [VM] * 6, {5: RING, 6: RING + 1}
    )(pos, tokt, other_tokt, grads, swap(grads), quarters[1], quarters[2])
    own, away = chunks[0], round_turn(chunks[1:], True)
    from_back, from_ahead = along_head(near_one, 1), along_head(near_two, 3)

    piece = vmem(3 * SLICE + PIECE // RING, wide)
    *pieces, far_quarter = whole(
        split_kernel, (piece,) * RING + (quarter,), [SM] + [VM] * 5 + [anywhere] * 2, {5: RING}
    )(pos, own, *away, quarters[3], from_back, from_ahead)
    from_far = along_head(far_quarter, 2)
    grad_tokens = ((quarters[0] + from_far) + (from_back + from_ahead)).astype(BF).reshape(1, n, -1)
    own, away = pieces[0], pieces[1:]
    part_sum = whole(sum_kernel, piece, [VM] * 4)(own, *round_turn(away, False))
    from_back, from_ahead, from_far = round_turn([part_sum] * 3, False)
    total = whole(join_kernel, chunk, [SM] + [VM] * 4 + [anywhere])(
        pos, part_sum, from_ahead, from_back, from_far, grad_tokens
    )
    from_back, from_ahead, from_far = round_turn([total] * 3, True)
    out = shape(3, model, wide)

    def place(which, extra, extra_out, extra_spec, aliases):
        given = [(mine, others)[half][m] for half, m in which]
        return pl.pallas_call(
            functools.partial(place_kernel, which=which),
            out_shape=(out,) + extra_out,
            in_specs=[SM] + [VM] * len(given) + [extra_spec],
            out_specs=(anywhere,) + (VM,) * len(extra_out),
            scratch_shapes=[pltpu.SemaphoreType.DMA((3, len(which)))],
            input_output_aliases={len(given) + 1: aliases},
            compiler_params=PARAMS,
        )(pos, *given, extra)

    mine = [total, from_ahead, from_back, from_far]
    others = [swap(total)]
    placed, mine[3] = place(((0, 0), (1, 0)), from_far, (chunk,), VM, 1)
    others += [swap(given) for given in mine[1:]]
    (placed,) = place(((0, 1), (0, 2), (0, 3), (1, 3)), placed, (), anywhere, 0)
    which = ((1, 1), (1, 2))
    grad_proj, grad_init, grad_gain, grad_rates = pl.pallas_call(
        functools.partial(last_kernel, which=which),
        out_shape=(out, shape(heads, HS, HS), shape(heads, HS), shape(heads)),
        in_specs=[SM] + [VM] * 8 + [anywhere],
        out_specs=(anywhere, VM, VM, SM),
        scratch_shapes=[pltpu.VMEM((EXTRA, wide), F32), pltpu.SemaphoreType.DMA((3, len(which)))],
        input_output_aliases={9: 0},
        compiler_params=PARAMS,
    )(pos, *mine, *others, placed)
    return (grad_tokens, grad_proj, grad_init, grad_gain, grad_rates, grad_gates)


def solution(mesh):
    in_specs = (
        P("dp", "ctx", None),
        P(None, None, "head"),
        P("head", None, None),
        P("head"),
        P("dp", "head", "ctx"),
        P("head", None),
        P("dp", "ctx", "head"),
    )
    out_specs = (
        P("dp", "ctx", "head"),
        P(None, None, "head"),
        P("head", None, None),
        P("head", None),
        P("head"),
        P("dp", "head", "ctx"),
    )
    return jax.shard_map(body, mesh=mesh, in_specs=in_specs, out_specs=out_specs, check_vma=False)
```

```python
import functools

import jax
import jax.numpy as jnp
from jax import lax
from jax.experimental import pallas as pl
from jax.experimental.pallas import tpu as pltpu
from jax.sharding import PartitionSpec as P

MB = 16
HS = 128
RING = 4
TURNS = (0, 1, 3, 2)
CHUNK = 256
SLICE = CHUNK // RING
PIECE = 32
EXTRA = 2 * RING * PIECE
F32 = jnp.float32
BF = jnp.bfloat16
NN = (((1,), (0,)), ((), ()))
NT = (((1,), (1,)), ((), ()))
TN = (((0,), (0,)), ((), ()))


def dot(a, b, dims, passes):
    ah = a.astype(BF)
    bh = b.astype(BF)
    result = lax.dot_general(ah, bh, dims, preferred_element_type=F32)
    if passes == 3:
        al = (a - ah.astype(F32)).astype(BF)
        bl = (b - bh.astype(F32)).astype(BF)
        result = result + (
            lax.dot_general(ah, bl, dims, preferred_element_type=F32)
            + lax.dot_general(al, bh, dims, preferred_element_type=F32)
        )
    return result


def places(n):
    return (
        lax.broadcasted_iota(jnp.int32, (n, n), 0),
        lax.broadcasted_iota(jnp.int32, (n, n), 1),
    )


def to_col(row):
    i, j = places(row.shape[1])
    return jnp.sum(jnp.where(i == j, row, 0.0), axis=1, keepdims=True)


def to_row(col):
    i, j = places(col.shape[0])
    return jnp.sum(jnp.where(i == j, col, 0.0), axis=0, keepdims=True)


def unit_lower_inverses(lowers):
    n = lowers[0].shape[0]
    i, j = places(n)
    size = 2 * MB
    same = (i // size) == (j // size)
    inverses = [jnp.where(i == j, 1.0, 0.0) - jnp.where(same, low, 0.0) for low in lowers]
    while size < n:
        pair = ((i // (2 * size)) == (j // (2 * size))) & ((i // size) != (j // size))
        corners = [jnp.where(pair, low, 0.0) for low in lowers]
        halves = [dot(inv, corner, NN, 3) for inv, corner in zip(inverses, corners)]
        inverses = [inv - dot(half, inv, NN, 3) for inv, half in zip(inverses, halves)]
        size *= 2
    return inverses


def span(h):
    return slice(h * HS, (h + 1) * HS)


def rates_of(base_ref, gate_ref, h):
    boost = base_ref[h] * gate_ref[0, h : h + 1, :]
    return boost, boost / (1.0 + boost)


def maps_kernel(
    pos_ref, base_ref, tok_ref, wk_ref, wv_ref, gate_ref, init_ref,
    k_ref, v_ref, ninv_ref, gram_ref, inv_ref, bt_ref, d_ref, send_ref, o_ref, half_ref,
):
    half = tok_ref.shape[2] // 2
    columns = pl.ds(pl.multiple_of((1 - pos_ref[0]) * half, half), half)
    half_ref[...] = tok_ref[0, :, columns].astype(F32)
    tok = tok_ref[0]
    kraw_all = jnp.dot(tok, wk_ref[0], preferred_element_type=F32).astype(BF).astype(F32)
    v_all = jnp.dot(tok, wv_ref[0], preferred_element_type=F32).astype(BF).astype(F32)
    n = kraw_all.shape[0]
    i, j = places(n)
    strict = (i // MB) > (j // MB)
    heads = range(init_ref.shape[0])
    ks, kts, es, lows = [], [], [], []
    for h in heads:
        kraw = kraw_all[:, span(h)]
        ninv = lax.rsqrt(jnp.sum(kraw * kraw, -1, keepdims=True) + 1e-06)
        k = kraw * ninv
        kt = k.T
        _, e = rates_of(base_ref, gate_ref, h)
        gram = dot(k, kt, NN, 3)
        ninv_ref[h] = jnp.broadcast_to(ninv, (n, HS))
        k_ref[:, span(h)] = k
        gram_ref[h] = gram
        ks.append(k)
        kts.append(kt)
        es.append(e)
        lows.append(jnp.where(strict, gram * e, 0.0))
    v_ref[...] = v_all
    inverses = unit_lower_inverses(lows)
    a, b = places(HS)
    for h in heads:
        bt = dot(kts[h] * es[h], inverses[h], NN, 3)
        inv_ref[h] = inverses[h]
        bt_ref[h] = bt
        decay = jnp.where(a == b, 1.0, 0.0) - dot(bt, ks[h], NN, 3)
        offset = dot(bt, v_all[:, span(h)], NN, 3)
        d_ref[h] = decay
        o_ref[h] = offset
        first = dot(decay, init_ref[h], NN, 3) + offset
        send_ref[h] = jnp.where(pos_ref[4] == 0, first, offset)


def reach_kernel(
    pos_ref, base_ref, tok_ref, wq_ref, gate_ref, k_ref, v_ref, inv_ref,
    q_ref, score_ref, rv_ref, y_ref, qt_ref, zv_ref, tokt_ref,
):
    half = tok_ref.shape[2] // 2
    columns = pl.ds(pl.multiple_of(pos_ref[0] * half, half), half)
    tokt_ref[...] = tok_ref[0, :, columns].astype(F32).T.astype(BF)
    q_all = jnp.dot(tok_ref[0], wq_ref[0], preferred_element_type=F32).astype(BF).astype(F32)
    n = q_all.shape[0]
    i, j = places(n)
    q_ref[...] = q_all
    for h in range(inv_ref.shape[0]):
        q = q_all[:, span(h)]
        k = k_ref[:, span(h)]
        _, e = rates_of(base_ref, gate_ref, h)
        score = dot(q, k, NT, 3)
        mix = jnp.where(i >= j, score * e, 0.0)
        inv = inv_ref[h]
        rv = dot(inv, v_ref[:, span(h)], NN, 3)
        y = dot(inv, k, NN, 3)
        score_ref[h] = score
        rv_ref[:, span(h)] = rv
        y_ref[:, span(h)] = y
        qt_ref[:, span(h)] = q - dot(mix, y, NN, 3)
        zv_ref[:, span(h)] = dot(mix, rv, NN, 3)


def step_kernel(d_ref, w_ref, o_ref, after_ref, out_ref):
    del after_ref
    for h in range(d_ref.shape[0]):
        out_ref[h] = o_ref[h] + dot(d_ref[h], w_ref[h], NN, 3)


def norm_kernel(
    pos_ref, init_ref, near_ref, mid_ref, far_ref, rd_ref, qt_ref, zv_ref, up_ref, gain_ref, after_ref,
    w_ref, h_ref, p_ref, dgain_ref,
):
    del after_ref
    ctx = pos_ref[4]
    heads = range(init_ref.shape[0])
    lasts = [dot(rd_ref[h], far_ref[h], NN, 3) + near_ref[h] for h in heads]
    starts = [
        jnp.where(
            ctx == 0, init_ref[h], jnp.where(ctx == 1, near_ref[h], jnp.where(ctx == 2, mid_ref[h], lasts[h]))
        )
        for h in heads
    ]
    qts = [qt_ref[:, span(h)] for h in heads]
    zs = [dot(qts[h], starts[h], NN, 3) + zv_ref[:, span(h)] for h in heads]
    ups = [up_ref[0, :, span(h)].astype(F32) for h in heads]
    centred = [z - jnp.mean(z, -1, keepdims=True) for z in zs]
    inv_stds = [lax.rsqrt(jnp.mean(c * c, -1, keepdims=True) + 1e-05) for c in centred]
    normed = [c * inv_std for c, inv_std in zip(centred, inv_stds)]
    weighted = [ups[h] * gain_ref[h : h + 1, :] for h in heads]
    backs = [
        inv_stds[h]
        * (
            weighted[h]
            - jnp.mean(weighted[h], -1, keepdims=True)
            - normed[h] * jnp.mean(weighted[h] * normed[h], -1, keepdims=True)
        )
        for h in heads
    ]
    pulled = [dot(qts[h], backs[h], TN, 3) for h in heads]
    for h in heads:
        w_ref[h] = starts[h]
        h_ref[:, span(h)] = backs[h]
        p_ref[h] = pulled[h]
        dgain_ref[h : h + 1, :] = jnp.sum(ups[h] * normed[h], axis=0, keepdims=True)


def query_kernel(
    base_ref, gate_ref, w_ref, h_ref, up_ref, q_ref, score_ref, rv_ref, y_ref, k_ref, inv_ref,
    dq_ref, r_ref, x_ref, dk_ref, de_ref,
):
    n = h_ref.shape[0]
    i, j = places(n)
    for h in range(w_ref.shape[0]):
        w = w_ref[h]
        back = h_ref[:, span(h)]
        k = k_ref[:, span(h)]
        q = q_ref[:, span(h)]
        score = score_ref[h]
        _, e = rates_of(base_ref, gate_ref, h)
        mix = jnp.where(i >= j, score * e, 0.0)
        r = rv_ref[:, span(h)] - dot(y_ref[:, span(h)], w, NN, 3)
        r_ref[:, span(h)] = r
        d_mix = jnp.where(i >= j, dot(back, r, NT, 3), 0.0)
        d_score = d_mix * e
        dq = up_ref[0, :, span(h)].astype(F32) + dot(back, w, NT, 3) + dot(d_score, k, NN, 3)
        dq_ref[:, span(h)] = dq.astype(BF).astype(F32)
        x_ref[:, span(h)] = dot(inv_ref[h], dot(mix, back, TN, 3), TN, 3)
        dk_ref[:, span(h)] = dot(d_score, q, TN, 3)
        de_ref[h : h + 1, :] = jnp.sum(d_mix * score, axis=0, keepdims=True)


def keys_kernel(
    pos_ref, base_ref, gate_ref, one_ref, two_ref, three_ref, rd_ref, rd_one_ref, rd_two_ref, p_ref, d_ref, w_ref, k_ref, ninv_ref,
    gram_ref, bt_ref, r_ref, x_ref, dk_ref, de_ref, dgain_ref, dq_ref,
    all_ref, gates_ref,
):
    ctx = pos_ref[4]
    n = k_ref.shape[0]
    i, j = places(n)
    strict = (i // MB) > (j // MB)
    heads = range(w_ref.shape[0])
    steps = [jnp.where(ctx == 0, rd_ref[h], rd_one_ref[h]) for h in heads]
    inner = [two_ref[h] + dot(rd_two_ref[h], three_ref[h], TN, 3) for h in heads]
    ends = [one_ref[h] + dot(steps[h], inner[h], TN, 3) for h in heads]
    ks = [k_ref[:, span(h)] for h in heads]
    rs = [r_ref[:, span(h)] for h in heads]
    rates = [rates_of(base_ref, gate_ref, h) for h in heads]
    xs = [x_ref[:, span(h)] + dot(bt_ref[h], ends[h], TN, 3) for h in heads]
    d_lows = [jnp.where(strict, -dot(xs[h], rs[h], NT, 3), 0.0) for h in heads]
    begins = [jnp.where(ctx == 0, p_ref[h] + dot(d_ref[h], ends[h], TN, 3), 0.0) for h in heads]
    pulls = [to_row(jnp.sum(rs[h] * dot(ks[h], ends[h], NN, 3), axis=1, keepdims=True)) for h in heads]
    dks = [
        dk_ref[:, span(h)] - dot(xs[h], w_ref[h], NT, 3) + to_col(rates[h][1]) * dot(rs[h], ends[h], NT, 3)
        for h in heads
    ]
    d_grams = [d_lows[h] * rates[h][1] for h in heads]
    dks = [dks[h] + dot(d_grams[h] + d_grams[h].T, ks[h], NN, 3) for h in heads]
    draws = [ninv_ref[h] * (dks[h] - ks[h] * jnp.sum(ks[h] * dks[h], -1, keepdims=True)) for h in heads]
    des = [
        de_ref[h : h + 1, :] + jnp.sum(d_lows[h] * gram_ref[h], axis=0, keepdims=True) + pulls[h] for h in heads
    ]
    all_ref[0:n, :] = dq_ref[...]
    all_ref[3 * n + HS : 3 * n + EXTRA, :] = jnp.zeros((EXTRA - HS, all_ref.shape[1]), F32)
    for h in heads:
        boost = rates[h][0]
        all_ref[n : 2 * n, span(h)] = draws[h].astype(BF).astype(F32)
        all_ref[2 * n : 3 * n, span(h)] = xs[h].astype(BF).astype(F32)
        all_ref[3 * n : 3 * n + HS, span(h)] = begins[h]
        d_boost = des[h] / ((1.0 + boost) * (1.0 + boost))
        gates_ref[0, h : h + 1, :] = d_boost * base_ref[h]
        all_ref[3 * n + HS : 3 * n + HS + 1, span(h)] = dgain_ref[h : h + 1, :]
        all_ref[3 * n + HS + 1 : 3 * n + HS + 2, span(h)] = jnp.broadcast_to(
            jnp.sum(d_boost * gate_ref[0, h : h + 1, :], axis=1, keepdims=True), (1, HS)
        )


def turn_kernel(other_ref, out_ref):
    out_ref[...] = other_ref[...].T.astype(BF)


def product_kernel(pos_ref, tokt_ref, other_tokt_ref, own_ref, other_ref, *refs):
    out_refs = refs[2 : 2 + RING]
    n = tokt_ref.shape[1]
    for turn, out_ref in zip(TURNS, out_refs):
        at = (pos_ref[1] + turn) & (RING - 1)
        rows = pl.ds(pl.multiple_of(at * CHUNK, CHUNK), CHUNK)
        for m in range(3):
            out_ref[m * CHUNK : (m + 1) * CHUNK, :] = jnp.dot(
                tokt_ref[rows, :], own_ref[m * n : (m + 1) * n, :].astype(BF), preferred_element_type=F32
            ) + jnp.dot(
                other_tokt_ref[rows, :], other_ref[m * n : (m + 1) * n, :].astype(BF), preferred_element_type=F32
            )
        extra = pl.ds(pl.multiple_of(3 * n + (pos_ref[0] * RING + at) * PIECE, 8), PIECE)
        out_ref[3 * CHUNK : 3 * CHUNK + PIECE, :] = own_ref[extra, :] + other_ref[extra, :]


def token_kernel(pos_ref, w_ref, all_ref, *out_refs):
    n = out_refs[0].shape[0]
    ds = [all_ref[m * n : (m + 1) * n, :].astype(BF) for m in range(3)]
    quarter = w_ref.shape[1] // RING
    for turn, out_ref in zip(TURNS, out_refs):
        at = (pos_ref[3] + turn) & (RING - 1)
        rows = pl.ds(pl.multiple_of(at * quarter, quarter), quarter)
        total = lax.dot_general(ds[0], w_ref[0, rows, :], NT, preferred_element_type=F32)
        total = total + lax.dot_general(ds[1], w_ref[1, rows, :], NT, preferred_element_type=F32)
        out_ref[...] = total + lax.dot_general(ds[2], w_ref[2, rows, :], NT, preferred_element_type=F32)


def slice_rows(pos_ref, turn):
    at = (pos_ref[2] + turn) & (RING - 1)
    taken = [
        (pl.ds(pl.multiple_of(m * CHUNK + at * SLICE, SLICE), SLICE), slice(m * SLICE, (m + 1) * SLICE))
        for m in range(3)
    ]
    few = PIECE // RING
    extra = pl.ds(pl.multiple_of(3 * CHUNK + at * few, few), few)
    return taken + [(extra, slice(3 * SLICE, 3 * SLICE + few))]


def split_kernel(pos_ref, own_ref, back_ref, ahead_ref, far_ref, *refs):
    for turn, out_ref in zip(TURNS, refs[-RING:]):
        for rows, to in slice_rows(pos_ref, turn):
            out_ref[to, :] = (own_ref[rows, :] + far_ref[rows, :]) + (back_ref[rows, :] + ahead_ref[rows, :])


def sum_kernel(own_ref, back_ref, ahead_ref, far_ref, out_ref):
    out_ref[...] = (own_ref[...] + far_ref[...]) + (back_ref[...] + ahead_ref[...])


def join_kernel(pos_ref, own_ref, ahead_ref, back_ref, far_ref, *refs):
    for turn, part_ref in zip(TURNS, (own_ref, ahead_ref, back_ref, far_ref)):
        for rows, to in slice_rows(pos_ref, turn):
            refs[-1][rows, :] = part_ref[to, :]


def place_kernel(pos_ref, *refs, which):
    pieces = refs[: len(which)]
    out_ref, sem = refs[len(refs) - 3 if len(refs) == len(which) + 4 else -2], refs[-1]
    copies = []
    for g, ((half, m), piece) in enumerate(zip(which, pieces)):
        core = pos_ref[0] if half == 0 else 1 - pos_ref[0]
        at = core * RING + ((pos_ref[1 + half] + TURNS[m]) & (RING - 1))
        rows = pl.ds(pl.multiple_of(at * CHUNK, CHUNK), CHUNK)
        for s in range(3):
            copies.append(
                pltpu.make_async_copy(piece.at[pl.ds(s * CHUNK, CHUNK), :], out_ref.at[s, rows, :], sem.at[s, g])
            )
    for copy in copies:
        copy.start()
    for copy in copies:
        copy.wait()


def last_kernel(pos_ref, *refs, which):
    pieces = refs[: 2 * RING]
    out_ref, init_ref, gain_ref, rates_ref, extra_ref, sem = refs[-6:]
    copies = []
    for g, (half, m) in enumerate(which):
        core = pos_ref[0] if half == 0 else 1 - pos_ref[0]
        at = core * RING + ((pos_ref[1 + half] + TURNS[m]) & (RING - 1))
        rows = pl.ds(pl.multiple_of(at * CHUNK, CHUNK), CHUNK)
        for s in range(3):
            copies.append(
                pltpu.make_async_copy(
                    pieces[half * RING + m].at[pl.ds(s * CHUNK, CHUNK), :], out_ref.at[s, rows, :], sem.at[s, g]
                )
            )
    for copy in copies:
        copy.start()
    for p, piece in enumerate(pieces):
        core = pos_ref[0] if p < RING else 1 - pos_ref[0]
        at = core * RING + ((pos_ref[1 + p // RING] + TURNS[p % RING]) & (RING - 1))
        extra_ref[pl.ds(pl.multiple_of(at * PIECE, 8), PIECE), :] = piece[3 * CHUNK : 3 * CHUNK + PIECE, :]
    for h in range(init_ref.shape[0]):
        init_ref[h] = extra_ref[0:HS, span(h)]
        gain_ref[h : h + 1, :] = extra_ref[HS : HS + 1, span(h)]
        rates_ref[h] = extra_ref[HS + 1, h * HS]
    for copy in copies:
        copy.wait()


def moves(first, by):
    pairs = []
    for x in range(RING):
        for core in range(2):
            for y in range(RING):
                along_x = (core == 0) == first
                to_x = (x + by) % RING if along_x else x
                to_y = y if along_x else (y + by) % RING
                pairs.append(((x * 2 + core) * RING + y, (to_x * 2 + core) * RING + to_y))
    return pairs


def round_turn(chunks, first):
    return [
        lax.ppermute(chunk, ("dp", "ctx"), moves(first, turn)) for chunk, turn in zip(chunks, TURNS[1:])
    ]


def swap(value):
    return lax.ppermute(value, "dp", [(i, i ^ 1) for i in range(2 * RING)])


VM = pl.BlockSpec(memory_space=pltpu.VMEM)
SM = pl.BlockSpec(memory_space=pltpu.SMEM)
PARAMS = pltpu.CompilerParams(vmem_limit_bytes=20 * 1024 * 1024)


def shape(*dims, dtype=F32):
    return jax.ShapeDtypeStruct(dims, dtype)


def vmem(*dims, dtype=F32):
    return pltpu.VMEM(dims, dtype)


def hbm(value):
    return pltpu.with_memory_space_constraint(value, pltpu.HBM)


def whole(kernel, outs, specs, aliases=None):
    return pl.pallas_call(
        kernel,
        out_shape=outs,
        in_specs=specs,
        out_specs=tuple(VM for _ in outs) if isinstance(outs, tuple) else VM,
        input_output_aliases=aliases or {},
        compiler_params=PARAMS,
    )


def part(which, dims):
    return pl.BlockSpec((1,) + dims, lambda i: (which, 0, 0))


def full(*dims):
    return pl.BlockSpec(dims, lambda i: (0,) * len(dims))


def body(tokens, proj_weights, init_weight, base_rates, gate_values, out_gain, cotangent):
    n = tokens.shape[1]
    model = tokens.shape[2]
    heads = init_weight.shape[0]
    wide = heads * HS
    ctx = lax.axis_index("ctx")
    dp = lax.axis_index("dp")
    core, x_at = dp % 2, dp // 2
    pos = jnp.stack(
        [core, jnp.where(core == 0, x_at, ctx), jnp.where(core == 0, ctx, x_at), lax.axis_index("head"), ctx]
    ).astype(jnp.int32)
    half = model // 2

    wide_f32 = vmem(n, wide)
    square = vmem(heads, n, n)
    small = vmem(heads, HS, HS)
    wspec = functools.partial(part, dims=(model, wide))
    tokens = hbm(tokens)
    raw_weights = proj_weights
    proj_weights = hbm(proj_weights)
    anywhere = pl.BlockSpec(memory_space=pl.ANY)

    k, v, ninv, gram, inv, bt, decay, send, offset, other_half = pl.pallas_call(
        maps_kernel,
        grid=(1,),
        out_shape=(
            wide_f32, wide_f32, vmem(heads, n, HS), square, square, vmem(heads, HS, n), small, small, small,
            vmem(n, half),
        ),
        in_specs=[SM, SM, full(1, n, model), wspec(1), wspec(2), full(1, heads, n), full(heads, HS, HS)],
        out_specs=(VM,) * 10,
        compiler_params=PARAMS,
    )(pos, hbm(base_rates), tokens, proj_weights, proj_weights, hbm(gate_values), hbm(init_weight))

    near = lax.ppermute(send, "ctx", [(0, 1), (2, 3)])
    moved = lax.ppermute(decay, "ctx", [(2, 3), (1, 0)])
    moved_one = lax.ppermute(decay, "ctx", [(2, 1)])
    moved_two = lax.ppermute(decay, "ctx", [(2, 0)])
    got_half = swap(other_half)

    q, score, rv, y, qt, zv, tokt = pl.pallas_call(
        reach_kernel,
        grid=(1,),
        out_shape=(wide_f32, square, wide_f32, wide_f32, wide_f32, wide_f32, vmem(half, n, dtype=BF)),
        in_specs=[SM, SM, full(1, n, model), wspec(0), full(1, heads, n), VM, VM, VM],
        out_specs=(VM,) * 7,
        compiler_params=PARAMS,
    )(pos, base_rates, tokens, proj_weights, gate_values, k, v, inv)

    second = whole(step_kernel, small, [VM] * 3 + [anywhere])(
        decay, near, offset, qt
    )
    mid = lax.ppermute(second, "ctx", [(1, 2)])
    far = lax.ppermute(second, "ctx", [(1, 3)])
    other_tokt = whole(turn_kernel, vmem(half, n, dtype=BF), [VM])(got_half)

    w, back, pulled, dgain = whole(
        norm_kernel, (small, wide_f32, small, vmem(heads, HS)), [SM] + [VM] * 9 + [anywhere]
    )(pos, init_weight, near, mid, far, moved, qt, zv, cotangent, out_gain, other_tokt)

    back_one = lax.ppermute(pulled, "ctx", [(3, 2), (2, 1), (1, 0)])
    back_two = lax.ppermute(pulled, "ctx", [(3, 1), (2, 0)])
    back_three = lax.ppermute(pulled, "ctx", [(3, 0)])

    dq, r, x, dk, de = whole(
        query_kernel, (wide_f32, wide_f32, wide_f32, wide_f32, vmem(heads, n)), [SM] + [VM] * 10
    )(base_rates, gate_values, w, back, cotangent, q, score, rv, y, k, inv)

    grads, grad_gates = whole(
        keys_kernel, (vmem(3 * n + EXTRA, wide), shape(1, heads, n)), [SM, SM] + [VM] * 20
    )(pos, base_rates, gate_values, back_one, back_two, back_three, moved, moved_one, moved_two, pulled, decay, w, k, ninv, gram, bt, r, x,
      dk, de, dgain, dq)

    chunk = vmem(3 * CHUNK + PIECE, wide)
    quarter = vmem(n, model // RING)
    quarters = whole(token_kernel, (quarter,) * RING, [SM, VM, VM])(pos, raw_weights, grads)

    def along_head(terms, turn):
        return lax.ppermute(terms, "head", [(i, (i + turn) % RING) for i in range(RING)])

    *chunks, near_two, far_quarter = whole(
        product_kernel, (chunk,) * RING + (quarter,) * 2, [SM] + [VM] * 6, {5: RING, 6: RING + 1}
    )(pos, tokt, other_tokt, grads, swap(grads), *quarters[2:])
    own, away = chunks[0], round_turn(chunks[1:], True)
    from_back, from_ahead, from_far = along_head(quarters[1], 1), along_head(near_two, 3), along_head(far_quarter, 2)

    piece = vmem(3 * SLICE + PIECE // RING, wide)
    pieces = whole(split_kernel, (piece,) * RING, [SM] + [VM] * 4 + [anywhere] * 2)(pos, own, *away, from_back, from_ahead)
    grad_tokens = ((quarters[0] + from_far) + (from_back + from_ahead)).astype(BF).reshape(1, n, -1)
    own, away = pieces[0], pieces[1:]
    part_sum = whole(sum_kernel, piece, [VM] * 4)(own, *round_turn(away, False))
    from_back, from_ahead, from_far = round_turn([part_sum] * 3, False)
    total = whole(join_kernel, chunk, [SM] + [VM] * 4 + [anywhere])(
        pos, part_sum, from_ahead, from_back, from_far, grad_tokens
    )
    from_back, from_ahead, from_far = round_turn([total] * 3, True)
    out = shape(3, model, wide)

    def place(which, extra, extra_out, extra_spec, aliases):
        given = [(mine, others)[half][m] for half, m in which]
        return pl.pallas_call(
            functools.partial(place_kernel, which=which),
            out_shape=(out,) + extra_out,
            in_specs=[SM] + [VM] * len(given) + [extra_spec],
            out_specs=(anywhere,) + (VM,) * len(extra_out),
            scratch_shapes=[pltpu.SemaphoreType.DMA((3, len(which)))],
            input_output_aliases={len(given) + 1: aliases},
            compiler_params=PARAMS,
        )(pos, *given, extra)

    mine = [total, from_ahead, from_back, from_far]
    others = [swap(total)]
    placed, mine[3] = place(((0, 0), (1, 0)), from_far, (chunk,), VM, 1)
    others += [swap(given) for given in mine[1:]]
    (placed,) = place(((0, 1), (0, 2), (0, 3), (1, 3)), placed, (), anywhere, 0)
    which = ((1, 1), (1, 2))
    grad_proj, grad_init, grad_gain, grad_rates = pl.pallas_call(
        functools.partial(last_kernel, which=which),
        out_shape=(out, shape(heads, HS, HS), shape(heads, HS), shape(heads)),
        in_specs=[SM] + [VM] * 8 + [anywhere],
        out_specs=(anywhere, VM, VM, SM),
        scratch_shapes=[pltpu.VMEM((EXTRA, wide), F32), pltpu.SemaphoreType.DMA((3, len(which)))],
        input_output_aliases={9: 0},
        compiler_params=PARAMS,
    )(pos, *mine, *others, placed)
    return (grad_tokens, grad_proj, grad_init, grad_gain, grad_rates, grad_gates)


def solution(mesh):
    in_specs = (
        P("dp", "ctx", None),
        P(None, None, "head"),
        P("head", None, None),
        P("head"),
        P("dp", "head", "ctx"),
        P("head", None),
        P("dp", "ctx", "head"),
    )
    out_specs = (
        P("dp", "ctx", "head"),
        P(None, None, "head"),
        P("head", None, None),
        P("head", None),
        P("head"),
        P("dp", "head", "ctx"),
    )
    return jax.shard_map(body, mesh=mesh, in_specs=in_specs, out_specs=out_specs, check_vma=False)
```

```python
import functools

import jax
import jax.numpy as jnp
from jax import lax
from jax.experimental import pallas as pl
from jax.experimental.pallas import tpu as pltpu
from jax.sharding import PartitionSpec as P

MB = 16
HS = 128
RING = 4
TURNS = (0, 1, 3, 2)
CHUNK = 256
SLICE = CHUNK // RING
PIECE = 32
EXTRA = 2 * RING * PIECE
F32 = jnp.float32
BF = jnp.bfloat16
NN = (((1,), (0,)), ((), ()))
NT = (((1,), (1,)), ((), ()))
TN = (((0,), (0,)), ((), ()))


def dot(a, b, dims, passes):
    ah = a.astype(BF)
    bh = b.astype(BF)
    result = lax.dot_general(ah, bh, dims, preferred_element_type=F32)
    if passes == 3:
        al = (a - ah.astype(F32)).astype(BF)
        bl = (b - bh.astype(F32)).astype(BF)
        result = result + (
            lax.dot_general(ah, bl, dims, preferred_element_type=F32)
            + lax.dot_general(al, bh, dims, preferred_element_type=F32)
        )
    return result


def places(n):
    return (
        lax.broadcasted_iota(jnp.int32, (n, n), 0),
        lax.broadcasted_iota(jnp.int32, (n, n), 1),
    )


def to_col(row):
    i, j = places(row.shape[1])
    return jnp.sum(jnp.where(i == j, row, 0.0), axis=1, keepdims=True)


def to_row(col):
    i, j = places(col.shape[0])
    return jnp.sum(jnp.where(i == j, col, 0.0), axis=0, keepdims=True)


def unit_lower_inverses(lowers):
    n = lowers[0].shape[0]
    i, j = places(n)
    size = 2 * MB
    same = (i // size) == (j // size)
    inverses = [jnp.where(i == j, 1.0, 0.0) - jnp.where(same, low, 0.0) for low in lowers]
    while size < n:
        pair = ((i // (2 * size)) == (j // (2 * size))) & ((i // size) != (j // size))
        corners = [jnp.where(pair, low, 0.0) for low in lowers]
        halves = [dot(inv, corner, NN, 3) for inv, corner in zip(inverses, corners)]
        inverses = [inv - dot(half, inv, NN, 3) for inv, half in zip(inverses, halves)]
        size *= 2
    return inverses


def span(h):
    return slice(h * HS, (h + 1) * HS)


def rates_of(base_ref, gate_ref, h):
    boost = base_ref[h] * gate_ref[0, h : h + 1, :]
    return boost, boost / (1.0 + boost)


def maps_kernel(
    pos_ref, base_ref, tok_ref, wk_ref, wv_ref, gate_ref, init_ref,
    k_ref, v_ref, ninv_ref, gram_ref, inv_ref, bt_ref, d_ref, send_ref, o_ref, half_ref,
):
    half = tok_ref.shape[2] // 2
    columns = pl.ds(pl.multiple_of((1 - pos_ref[0]) * half, half), half)
    half_ref[...] = tok_ref[0, :, columns].astype(F32)
    tok = tok_ref[0]
    kraw_all = jnp.dot(tok, wk_ref[0], preferred_element_type=F32).astype(BF).astype(F32)
    v_all = jnp.dot(tok, wv_ref[0], preferred_element_type=F32).astype(BF).astype(F32)
    n = kraw_all.shape[0]
    i, j = places(n)
    strict = (i // MB) > (j // MB)
    heads = range(init_ref.shape[0])
    kraws = [kraw_all[:, span(h)] for h in heads]
    ninvs = [lax.rsqrt(jnp.sum(kraw * kraw, -1, keepdims=True) + 1e-06) for kraw in kraws]
    ks = [kraw * ninv for kraw, ninv in zip(kraws, ninvs)]
    kts = [k.T for k in ks]
    es = [rates_of(base_ref, gate_ref, h)[1] for h in heads]
    grams = [dot(k, kt, NN, 3) for k, kt in zip(ks, kts)]
    inverses = unit_lower_inverses([jnp.where(strict, gram * e, 0.0) for gram, e in zip(grams, es)])
    a, b = places(HS)
    bts = [dot(kts[h] * es[h], inverses[h], NN, 3) for h in heads]
    decays = [jnp.where(a == b, 1.0, 0.0) - dot(bts[h], ks[h], NN, 3) for h in heads]
    offsets = [dot(bts[h], v_all[:, span(h)], NN, 3) for h in heads]
    firsts = [dot(decays[h], init_ref[h], NN, 3) + offsets[h] for h in heads]
    v_ref[...] = v_all
    for h in heads:
        send_ref[h] = jnp.where(pos_ref[4] == 0, firsts[h], offsets[h])
        d_ref[h] = decays[h]
        o_ref[h] = offsets[h]
        k_ref[:, span(h)] = ks[h]
        ninv_ref[h] = jnp.broadcast_to(ninvs[h], (n, HS))
        gram_ref[h] = grams[h]
        inv_ref[h] = inverses[h]
        bt_ref[h] = bts[h]


def reach_kernel(
    pos_ref, base_ref, tok_ref, wq_ref, gate_ref, k_ref, v_ref, inv_ref,
    q_ref, score_ref, rv_ref, y_ref, qt_ref, zv_ref, tokt_ref,
):
    half = tok_ref.shape[2] // 2
    columns = pl.ds(pl.multiple_of(pos_ref[0] * half, half), half)
    tokt_ref[...] = tok_ref[0, :, columns].astype(F32).T.astype(BF)
    q_all = jnp.dot(tok_ref[0], wq_ref[0], preferred_element_type=F32).astype(BF).astype(F32)
    n = q_all.shape[0]
    i, j = places(n)
    q_ref[...] = q_all
    for h in range(inv_ref.shape[0]):
        q = q_all[:, span(h)]
        k = k_ref[:, span(h)]
        _, e = rates_of(base_ref, gate_ref, h)
        score = dot(q, k, NT, 3)
        mix = jnp.where(i >= j, score * e, 0.0)
        inv = inv_ref[h]
        rv = dot(inv, v_ref[:, span(h)], NN, 3)
        y = dot(inv, k, NN, 3)
        score_ref[h] = score
        rv_ref[:, span(h)] = rv
        y_ref[:, span(h)] = y
        qt_ref[:, span(h)] = q - dot(mix, y, NN, 3)
        zv_ref[:, span(h)] = dot(mix, rv, NN, 3)


def step_kernel(d_ref, w_ref, o_ref, after_ref, out_ref):
    del after_ref
    for h in range(d_ref.shape[0]):
        out_ref[h] = o_ref[h] + dot(d_ref[h], w_ref[h], NN, 3)


def norm_kernel(
    pos_ref, init_ref, near_ref, mid_ref, far_ref, rd_ref, qt_ref, zv_ref, up_ref, gain_ref, after_ref,
    w_ref, h_ref, p_ref, dgain_ref,
):
    del after_ref
    ctx = pos_ref[4]
    heads = range(init_ref.shape[0])
    lasts = [dot(rd_ref[h], far_ref[h], NN, 3) + near_ref[h] for h in heads]
    starts = [
        jnp.where(
            ctx == 0, init_ref[h], jnp.where(ctx == 1, near_ref[h], jnp.where(ctx == 2, mid_ref[h], lasts[h]))
        )
        for h in heads
    ]
    qts = [qt_ref[:, span(h)] for h in heads]
    zs = [dot(qts[h], starts[h], NN, 3) + zv_ref[:, span(h)] for h in heads]
    ups = [up_ref[0, :, span(h)].astype(F32) for h in heads]
    centred = [z - jnp.mean(z, -1, keepdims=True) for z in zs]
    inv_stds = [lax.rsqrt(jnp.mean(c * c, -1, keepdims=True) + 1e-05) for c in centred]
    normed = [c * inv_std for c, inv_std in zip(centred, inv_stds)]
    weighted = [ups[h] * gain_ref[h : h + 1, :] for h in heads]
    backs = [
        inv_stds[h]
        * (
            weighted[h]
            - jnp.mean(weighted[h], -1, keepdims=True)
            - normed[h] * jnp.mean(weighted[h] * normed[h], -1, keepdims=True)
        )
        for h in heads
    ]
    pulled = [dot(qts[h], backs[h], TN, 3) for h in heads]
    for h in heads:
        w_ref[h] = starts[h]
        h_ref[:, span(h)] = backs[h]
        p_ref[h] = pulled[h]
        dgain_ref[h : h + 1, :] = jnp.sum(ups[h] * normed[h], axis=0, keepdims=True)


def query_kernel(
    base_ref, gate_ref, w_ref, h_ref, up_ref, q_ref, score_ref, rv_ref, y_ref, k_ref, inv_ref,
    dq_ref, r_ref, x_ref, dk_ref, de_ref,
):
    n = h_ref.shape[0]
    i, j = places(n)
    for h in range(w_ref.shape[0]):
        w = w_ref[h]
        back = h_ref[:, span(h)]
        k = k_ref[:, span(h)]
        q = q_ref[:, span(h)]
        score = score_ref[h]
        _, e = rates_of(base_ref, gate_ref, h)
        mix = jnp.where(i >= j, score * e, 0.0)
        r = rv_ref[:, span(h)] - dot(y_ref[:, span(h)], w, NN, 3)
        r_ref[:, span(h)] = r
        d_mix = jnp.where(i >= j, dot(back, r, NT, 3), 0.0)
        d_score = d_mix * e
        dq = up_ref[0, :, span(h)].astype(F32) + dot(back, w, NT, 3) + dot(d_score, k, NN, 3)
        dq_ref[:, span(h)] = dq.astype(BF).astype(F32)
        x_ref[:, span(h)] = dot(inv_ref[h], dot(mix, back, TN, 3), TN, 3)
        dk_ref[:, span(h)] = dot(d_score, q, TN, 3)
        de_ref[h : h + 1, :] = jnp.sum(d_mix * score, axis=0, keepdims=True)


def keys_kernel(
    pos_ref, base_ref, gate_ref, one_ref, two_ref, three_ref, rd_ref, rd_one_ref, rd_two_ref, p_ref, d_ref, w_ref, k_ref, ninv_ref,
    gram_ref, bt_ref, r_ref, x_ref, dk_ref, de_ref, dgain_ref, dq_ref,
    all_ref, gates_ref,
):
    ctx = pos_ref[4]
    n = k_ref.shape[0]
    i, j = places(n)
    strict = (i // MB) > (j // MB)
    heads = range(w_ref.shape[0])
    steps = [jnp.where(ctx == 0, rd_ref[h], rd_one_ref[h]) for h in heads]
    inner = [two_ref[h] + dot(rd_two_ref[h], three_ref[h], TN, 3) for h in heads]
    ends = [one_ref[h] + dot(steps[h], inner[h], TN, 3) for h in heads]
    ks = [k_ref[:, span(h)] for h in heads]
    rs = [r_ref[:, span(h)] for h in heads]
    rates = [rates_of(base_ref, gate_ref, h) for h in heads]
    xs = [x_ref[:, span(h)] + dot(bt_ref[h], ends[h], TN, 3) for h in heads]
    d_lows = [jnp.where(strict, -dot(xs[h], rs[h], NT, 3), 0.0) for h in heads]
    begins = [jnp.where(ctx == 0, p_ref[h] + dot(d_ref[h], ends[h], TN, 3), 0.0) for h in heads]
    pulls = [to_row(jnp.sum(rs[h] * dot(ks[h], ends[h], NN, 3), axis=1, keepdims=True)) for h in heads]
    dks = [
        dk_ref[:, span(h)] - dot(xs[h], w_ref[h], NT, 3) + to_col(rates[h][1]) * dot(rs[h], ends[h], NT, 3)
        for h in heads
    ]
    d_grams = [d_lows[h] * rates[h][1] for h in heads]
    dks = [dks[h] + dot(d_grams[h] + d_grams[h].T, ks[h], NN, 3) for h in heads]
    draws = [ninv_ref[h] * (dks[h] - ks[h] * jnp.sum(ks[h] * dks[h], -1, keepdims=True)) for h in heads]
    des = [
        de_ref[h : h + 1, :] + jnp.sum(d_lows[h] * gram_ref[h], axis=0, keepdims=True) + pulls[h] for h in heads
    ]
    all_ref[0:n, :] = dq_ref[...]
    all_ref[3 * n + HS : 3 * n + EXTRA, :] = jnp.zeros((EXTRA - HS, all_ref.shape[1]), F32)
    for h in heads:
        boost = rates[h][0]
        all_ref[n : 2 * n, span(h)] = draws[h].astype(BF).astype(F32)
        all_ref[2 * n : 3 * n, span(h)] = xs[h].astype(BF).astype(F32)
        all_ref[3 * n : 3 * n + HS, span(h)] = begins[h]
        d_boost = des[h] / ((1.0 + boost) * (1.0 + boost))
        gates_ref[0, h : h + 1, :] = d_boost * base_ref[h]
        all_ref[3 * n + HS : 3 * n + HS + 1, span(h)] = dgain_ref[h : h + 1, :]
        all_ref[3 * n + HS + 1 : 3 * n + HS + 2, span(h)] = jnp.broadcast_to(
            jnp.sum(d_boost * gate_ref[0, h : h + 1, :], axis=1, keepdims=True), (1, HS)
        )


def turn_kernel(other_ref, out_ref):
    out_ref[...] = other_ref[...].T.astype(BF)


def product_kernel(pos_ref, tokt_ref, other_tokt_ref, own_ref, other_ref, *refs):
    out_refs = refs[2 : 2 + RING]
    n = tokt_ref.shape[1]
    for turn, out_ref in zip(TURNS, out_refs):
        at = (pos_ref[1] + turn) & (RING - 1)
        rows = pl.ds(pl.multiple_of(at * CHUNK, CHUNK), CHUNK)
        for m in range(3):
            out_ref[m * CHUNK : (m + 1) * CHUNK, :] = jnp.dot(
                tokt_ref[rows, :], own_ref[m * n : (m + 1) * n, :].astype(BF), preferred_element_type=F32
            ) + jnp.dot(
                other_tokt_ref[rows, :], other_ref[m * n : (m + 1) * n, :].astype(BF), preferred_element_type=F32
            )
        extra = pl.ds(pl.multiple_of(3 * n + (pos_ref[0] * RING + at) * PIECE, 8), PIECE)
        out_ref[3 * CHUNK : 3 * CHUNK + PIECE, :] = own_ref[extra, :] + other_ref[extra, :]


def token_kernel(pos_ref, w_ref, all_ref, *out_refs):
    n = out_refs[0].shape[0]
    ds = [all_ref[m * n : (m + 1) * n, :].astype(BF) for m in range(3)]
    quarter = w_ref.shape[1] // RING
    for turn, out_ref in zip(TURNS, out_refs):
        at = (pos_ref[3] + turn) & (RING - 1)
        rows = pl.ds(pl.multiple_of(at * quarter, quarter), quarter)
        total = lax.dot_general(ds[0], w_ref[0, rows, :], NT, preferred_element_type=F32)
        total = total + lax.dot_general(ds[1], w_ref[1, rows, :], NT, preferred_element_type=F32)
        out_ref[...] = total + lax.dot_general(ds[2], w_ref[2, rows, :], NT, preferred_element_type=F32)


def slice_rows(pos_ref, turn):
    at = (pos_ref[2] + turn) & (RING - 1)
    taken = [
        (pl.ds(pl.multiple_of(m * CHUNK + at * SLICE, SLICE), SLICE), slice(m * SLICE, (m + 1) * SLICE))
        for m in range(3)
    ]
    few = PIECE // RING
    extra = pl.ds(pl.multiple_of(3 * CHUNK + at * few, few), few)
    return taken + [(extra, slice(3 * SLICE, 3 * SLICE + few))]


def split_kernel(pos_ref, own_ref, back_ref, ahead_ref, far_ref, *refs):
    for turn, out_ref in zip(TURNS, refs[-RING:]):
        for rows, to in slice_rows(pos_ref, turn):
            out_ref[to, :] = (own_ref[rows, :] + far_ref[rows, :]) + (back_ref[rows, :] + ahead_ref[rows, :])


def sum_kernel(own_ref, back_ref, ahead_ref, far_ref, out_ref):
    out_ref[...] = (own_ref[...] + far_ref[...]) + (back_ref[...] + ahead_ref[...])


def join_kernel(pos_ref, own_ref, ahead_ref, back_ref, far_ref, *refs):
    for turn, part_ref in zip(TURNS, (own_ref, ahead_ref, back_ref, far_ref)):
        for rows, to in slice_rows(pos_ref, turn):
            refs[-1][rows, :] = part_ref[to, :]


def place_kernel(pos_ref, *refs, which):
    pieces = refs[: len(which)]
    out_ref, sem = refs[len(refs) - 3 if len(refs) == len(which) + 4 else -2], refs[-1]
    copies = []
    for g, ((half, m), piece) in enumerate(zip(which, pieces)):
        core = pos_ref[0] if half == 0 else 1 - pos_ref[0]
        at = core * RING + ((pos_ref[1 + half] + TURNS[m]) & (RING - 1))
        rows = pl.ds(pl.multiple_of(at * CHUNK, CHUNK), CHUNK)
        for s in range(3):
            copies.append(
                pltpu.make_async_copy(piece.at[pl.ds(s * CHUNK, CHUNK), :], out_ref.at[s, rows, :], sem.at[s, g])
            )
    for copy in copies:
        copy.start()
    for copy in copies:
        copy.wait()


def last_kernel(pos_ref, *refs, which):
    pieces = refs[: 2 * RING]
    out_ref, init_ref, gain_ref, rates_ref, extra_ref, sem = refs[-6:]
    copies = []
    for g, (half, m) in enumerate(which):
        core = pos_ref[0] if half == 0 else 1 - pos_ref[0]
        at = core * RING + ((pos_ref[1 + half] + TURNS[m]) & (RING - 1))
        rows = pl.ds(pl.multiple_of(at * CHUNK, CHUNK), CHUNK)
        for s in range(3):
            copies.append(
                pltpu.make_async_copy(
                    pieces[half * RING + m].at[pl.ds(s * CHUNK, CHUNK), :], out_ref.at[s, rows, :], sem.at[s, g]
                )
            )
    for copy in copies:
        copy.start()
    for p, piece in enumerate(pieces):
        core = pos_ref[0] if p < RING else 1 - pos_ref[0]
        at = core * RING + ((pos_ref[1 + p // RING] + TURNS[p % RING]) & (RING - 1))
        extra_ref[pl.ds(pl.multiple_of(at * PIECE, 8), PIECE), :] = piece[3 * CHUNK : 3 * CHUNK + PIECE, :]
    for h in range(init_ref.shape[0]):
        init_ref[h] = extra_ref[0:HS, span(h)]
        gain_ref[h : h + 1, :] = extra_ref[HS : HS + 1, span(h)]
        rates_ref[h] = extra_ref[HS + 1, h * HS]
    for copy in copies:
        copy.wait()


def moves(first, by):
    pairs = []
    for x in range(RING):
        for core in range(2):
            for y in range(RING):
                along_x = (core == 0) == first
                to_x = (x + by) % RING if along_x else x
                to_y = y if along_x else (y + by) % RING
                pairs.append(((x * 2 + core) * RING + y, (to_x * 2 + core) * RING + to_y))
    return pairs


def round_turn(chunks, first):
    return [
        lax.ppermute(chunk, ("dp", "ctx"), moves(first, turn)) for chunk, turn in zip(chunks, TURNS[1:])
    ]


def swap(value):
    return lax.ppermute(value, "dp", [(i, i ^ 1) for i in range(2 * RING)])


VM = pl.BlockSpec(memory_space=pltpu.VMEM)
SM = pl.BlockSpec(memory_space=pltpu.SMEM)
PARAMS = pltpu.CompilerParams(vmem_limit_bytes=20 * 1024 * 1024)


def shape(*dims, dtype=F32):
    return jax.ShapeDtypeStruct(dims, dtype)


def vmem(*dims, dtype=F32):
    return pltpu.VMEM(dims, dtype)


def hbm(value):
    return pltpu.with_memory_space_constraint(value, pltpu.HBM)


def whole(kernel, outs, specs, aliases=None):
    return pl.pallas_call(
        kernel,
        out_shape=outs,
        in_specs=specs,
        out_specs=tuple(VM for _ in outs) if isinstance(outs, tuple) else VM,
        input_output_aliases=aliases or {},
        compiler_params=PARAMS,
    )


def part(which, dims):
    return pl.BlockSpec((1,) + dims, lambda i: (which, 0, 0))


def full(*dims):
    return pl.BlockSpec(dims, lambda i: (0,) * len(dims))


def body(tokens, proj_weights, init_weight, base_rates, gate_values, out_gain, cotangent):
    n = tokens.shape[1]
    model = tokens.shape[2]
    heads = init_weight.shape[0]
    wide = heads * HS
    ctx = lax.axis_index("ctx")
    dp = lax.axis_index("dp")
    core, x_at = dp % 2, dp // 2
    pos = jnp.stack(
        [core, jnp.where(core == 0, x_at, ctx), jnp.where(core == 0, ctx, x_at), lax.axis_index("head"), ctx]
    ).astype(jnp.int32)
    half = model // 2

    wide_f32 = vmem(n, wide)
    square = vmem(heads, n, n)
    small = vmem(heads, HS, HS)
    wspec = functools.partial(part, dims=(model, wide))
    tokens = hbm(tokens)
    raw_weights = proj_weights
    proj_weights = hbm(proj_weights)
    anywhere = pl.BlockSpec(memory_space=pl.ANY)

    k, v, ninv, gram, inv, bt, decay, send, offset, other_half = pl.pallas_call(
        maps_kernel,
        grid=(1,),
        out_shape=(
            wide_f32, wide_f32, vmem(heads, n, HS), square, square, vmem(heads, HS, n), small, small, small,
            vmem(n, half),
        ),
        in_specs=[SM, SM, full(1, n, model), wspec(1), wspec(2), full(1, heads, n), full(heads, HS, HS)],
        out_specs=(VM,) * 10,
        compiler_params=PARAMS,
    )(pos, hbm(base_rates), tokens, proj_weights, proj_weights, hbm(gate_values), hbm(init_weight))

    near = lax.ppermute(send, "ctx", [(0, 1), (2, 3)])
    moved = lax.ppermute(decay, "ctx", [(2, 3), (1, 0)])
    moved_one = lax.ppermute(decay, "ctx", [(2, 1)])
    moved_two = lax.ppermute(decay, "ctx", [(2, 0)])
    got_half = swap(other_half)

    q, score, rv, y, qt, zv, tokt = pl.pallas_call(
        reach_kernel,
        grid=(1,),
        out_shape=(wide_f32, square, wide_f32, wide_f32, wide_f32, wide_f32, vmem(half, n, dtype=BF)),
        in_specs=[SM, SM, full(1, n, model), wspec(0), full(1, heads, n), VM, VM, VM],
        out_specs=(VM,) * 7,
        compiler_params=PARAMS,
    )(pos, base_rates, tokens, proj_weights, gate_values, k, v, inv)

    second = whole(step_kernel, small, [VM] * 3 + [anywhere])(
        decay, near, offset, qt
    )
    mid = lax.ppermute(second, "ctx", [(1, 2)])
    far = lax.ppermute(second, "ctx", [(1, 3)])
    other_tokt = whole(turn_kernel, vmem(half, n, dtype=BF), [VM])(got_half)

    w, back, pulled, dgain = whole(
        norm_kernel, (small, wide_f32, small, vmem(heads, HS)), [SM] + [VM] * 9 + [anywhere]
    )(pos, init_weight, near, mid, far, moved, qt, zv, cotangent, out_gain, other_tokt)

    back_one = lax.ppermute(pulled, "ctx", [(3, 2), (2, 1), (1, 0)])
    back_two = lax.ppermute(pulled, "ctx", [(3, 1), (2, 0)])
    back_three = lax.ppermute(pulled, "ctx", [(3, 0)])

    dq, r, x, dk, de = whole(
        query_kernel, (wide_f32, wide_f32, wide_f32, wide_f32, vmem(heads, n)), [SM] + [VM] * 10
    )(base_rates, gate_values, w, back, cotangent, q, score, rv, y, k, inv)

    grads, grad_gates = whole(
        keys_kernel, (vmem(3 * n + EXTRA, wide), shape(1, heads, n)), [SM, SM] + [VM] * 20
    )(pos, base_rates, gate_values, back_one, back_two, back_three, moved, moved_one, moved_two, pulled, decay, w, k, ninv, gram, bt, r, x,
      dk, de, dgain, dq)

    chunk = vmem(3 * CHUNK + PIECE, wide)
    quarter = vmem(n, model // RING)
    quarters = whole(token_kernel, (quarter,) * RING, [SM, VM, VM])(pos, raw_weights, grads)

    def along_head(terms, turn):
        return lax.ppermute(terms, "head", [(i, (i + turn) % RING) for i in range(RING)])

    *chunks, near_two, far_quarter = whole(
        product_kernel, (chunk,) * RING + (quarter,) * 2, [SM] + [VM] * 6, {5: RING, 6: RING + 1}
    )(pos, tokt, other_tokt, grads, swap(grads), *quarters[2:])
    own, away = chunks[0], round_turn(chunks[1:], True)
    from_back, from_ahead, from_far = along_head(quarters[1], 1), along_head(near_two, 3), along_head(far_quarter, 2)

    piece = vmem(3 * SLICE + PIECE // RING, wide)
    pieces = whole(split_kernel, (piece,) * RING, [SM] + [VM] * 4 + [anywhere])(pos, own, *away, from_back)
    grad_tokens = ((quarters[0] + from_far) + (from_back + from_ahead)).astype(BF).reshape(1, n, -1)
    own, away = pieces[0], pieces[1:]
    part_sum = whole(sum_kernel, piece, [VM] * 4)(own, *round_turn(away, False))
    from_back, from_ahead, from_far = round_turn([part_sum] * 3, False)
    total = whole(join_kernel, chunk, [SM] + [VM] * 4 + [anywhere])(
        pos, part_sum, from_ahead, from_back, from_far, grad_tokens
    )
    from_back, from_ahead, from_far = round_turn([total] * 3, True)
    out = shape(3, model, wide)

    def place(which, extra, extra_out, extra_spec, aliases):
        given = [(mine, others)[half][m] for half, m in which]
        return pl.pallas_call(
            functools.partial(place_kernel, which=which),
            out_shape=(out,) + extra_out,
            in_specs=[SM] + [VM] * len(given) + [extra_spec],
            out_specs=(anywhere,) + (VM,) * len(extra_out),
            scratch_shapes=[pltpu.SemaphoreType.DMA((3, len(which)))],
            input_output_aliases={len(given) + 1: aliases},
            compiler_params=PARAMS,
        )(pos, *given, extra)

    mine = [total, from_ahead, from_back, from_far]
    others = [swap(total)]
    placed, mine[3] = place(((0, 0), (1, 0)), from_far, (chunk,), VM, 1)
    others += [swap(given) for given in mine[1:]]
    (placed,) = place(((0, 1), (0, 2), (0, 3), (1, 3)), placed, (), anywhere, 0)
    which = ((1, 1), (1, 2))
    grad_proj, grad_init, grad_gain, grad_rates = pl.pallas_call(
        functools.partial(last_kernel, which=which),
        out_shape=(out, shape(heads, HS, HS), shape(heads, HS), shape(heads)),
        in_specs=[SM] + [VM] * 8 + [anywhere],
        out_specs=(anywhere, VM, VM, SM),
        scratch_shapes=[pltpu.VMEM((EXTRA, wide), F32), pltpu.SemaphoreType.DMA((3, len(which)))],
        input_output_aliases={9: 0},
        compiler_params=PARAMS,
    )(pos, *mine, *others, placed)
    return (grad_tokens, grad_proj, grad_init, grad_gain, grad_rates, grad_gates)


def solution(mesh):
    in_specs = (
        P("dp", "ctx", None),
        P(None, None, "head"),
        P("head", None, None),
        P("head"),
        P("dp", "head", "ctx"),
        P("head", None),
        P("dp", "ctx", "head"),
    )
    out_specs = (
        P("dp", "ctx", "head"),
        P(None, None, "head"),
        P("head", None, None),
        P("head", None),
        P("head"),
        P("dp", "head", "ctx"),
    )
    return jax.shard_map(body, mesh=mesh, in_specs=in_specs, out_specs=out_specs, check_vma=False)
```

```python
import functools

import jax
import jax.numpy as jnp
from jax import lax
from jax.experimental import pallas as pl
from jax.experimental.pallas import tpu as pltpu
from jax.sharding import PartitionSpec as P

MB = 16
HS = 128
RING = 4
TURNS = (0, 1, 3, 2)
CHUNK = 256
SLICE = CHUNK // RING
PIECE = 32
EXTRA = 2 * RING * PIECE
F32 = jnp.float32
BF = jnp.bfloat16
NN = (((1,), (0,)), ((), ()))
NT = (((1,), (1,)), ((), ()))
TN = (((0,), (0,)), ((), ()))


def dot(a, b, dims, passes):
    ah = a.astype(BF)
    bh = b.astype(BF)
    result = lax.dot_general(ah, bh, dims, preferred_element_type=F32)
    if passes == 3:
        al = (a - ah.astype(F32)).astype(BF)
        bl = (b - bh.astype(F32)).astype(BF)
        result = result + (
            lax.dot_general(ah, bl, dims, preferred_element_type=F32)
            + lax.dot_general(al, bh, dims, preferred_element_type=F32)
        )
    return result


def places(n):
    return (
        lax.broadcasted_iota(jnp.int32, (n, n), 0),
        lax.broadcasted_iota(jnp.int32, (n, n), 1),
    )


def to_col(row):
    i, j = places(row.shape[1])
    return jnp.sum(jnp.where(i == j, row, 0.0), axis=1, keepdims=True)


def to_row(col):
    i, j = places(col.shape[0])
    return jnp.sum(jnp.where(i == j, col, 0.0), axis=0, keepdims=True)


def unit_lower_inverses(lowers):
    n = lowers[0].shape[0]
    i, j = places(n)
    size = 2 * MB
    same = (i // size) == (j // size)
    inverses = [jnp.where(i == j, 1.0, 0.0) - jnp.where(same, low, 0.0) for low in lowers]
    while size < n:
        pair = ((i // (2 * size)) == (j // (2 * size))) & ((i // size) != (j // size))
        corners = [jnp.where(pair, low, 0.0) for low in lowers]
        halves = [dot(inv, corner, NN, 3) for inv, corner in zip(inverses, corners)]
        inverses = [inv - dot(half, inv, NN, 3) for inv, half in zip(inverses, halves)]
        size *= 2
    return inverses


def span(h):
    return slice(h * HS, (h + 1) * HS)


def rates_of(base_ref, gate_ref, h):
    boost = base_ref[h] * gate_ref[0, h : h + 1, :]
    return boost, boost / (1.0 + boost)


def maps_kernel(
    pos_ref, base_ref, tok_ref, wk_ref, wv_ref, gate_ref, init_ref,
    k_ref, v_ref, ninv_ref, gram_ref, inv_ref, bt_ref, d_ref, send_ref, o_ref, half_ref,
):
    half = tok_ref.shape[2] // 2
    columns = pl.ds(pl.multiple_of((1 - pos_ref[0]) * half, half), half)
    half_ref[...] = tok_ref[0, :, columns].astype(F32)
    tok = tok_ref[0]
    kraw_all = jnp.dot(tok, wk_ref[0], preferred_element_type=F32).astype(BF).astype(F32)
    v_all = jnp.dot(tok, wv_ref[0], preferred_element_type=F32).astype(BF).astype(F32)
    n = kraw_all.shape[0]
    i, j = places(n)
    strict = (i // MB) > (j // MB)
    heads = range(init_ref.shape[0])
    kraws = [kraw_all[:, span(h)] for h in heads]
    ninvs = [lax.rsqrt(jnp.sum(kraw * kraw, -1, keepdims=True) + 1e-06) for kraw in kraws]
    ks = [kraw * ninv for kraw, ninv in zip(kraws, ninvs)]
    kts = [k.T for k in ks]
    es = [rates_of(base_ref, gate_ref, h)[1] for h in heads]
    grams = [dot(k, kt, NN, 3) for k, kt in zip(ks, kts)]
    inverses = unit_lower_inverses([jnp.where(strict, gram * e, 0.0) for gram, e in zip(grams, es)])
    a, b = places(HS)
    bts = [dot(kts[h] * es[h], inverses[h], NN, 3) for h in heads]
    decays = [jnp.where(a == b, 1.0, 0.0) - dot(bts[h], ks[h], NN, 3) for h in heads]
    offsets = [dot(bts[h], v_all[:, span(h)], NN, 3) for h in heads]
    firsts = [dot(decays[h], init_ref[h], NN, 3) + offsets[h] for h in heads]
    v_ref[...] = v_all
    for h in heads:
        send_ref[h] = jnp.where(pos_ref[4] == 0, firsts[h], offsets[h])
        d_ref[h] = decays[h]
        o_ref[h] = offsets[h]
        k_ref[:, span(h)] = ks[h]
        ninv_ref[h] = jnp.broadcast_to(ninvs[h], (n, HS))
        gram_ref[h] = grams[h]
        inv_ref[h] = inverses[h]
        bt_ref[h] = bts[h]


def reach_kernel(
    pos_ref, base_ref, tok_ref, wq_ref, gate_ref, k_ref, v_ref, inv_ref,
    q_ref, score_ref, rv_ref, y_ref, qt_ref, zv_ref, tokt_ref,
):
    half = tok_ref.shape[2] // 2
    columns = pl.ds(pl.multiple_of(pos_ref[0] * half, half), half)
    tokt_ref[...] = tok_ref[0, :, columns].astype(F32).T.astype(BF)
    q_all = jnp.dot(tok_ref[0], wq_ref[0], preferred_element_type=F32).astype(BF).astype(F32)
    n = q_all.shape[0]
    i, j = places(n)
    q_ref[...] = q_all
    for h in range(inv_ref.shape[0]):
        q = q_all[:, span(h)]
        k = k_ref[:, span(h)]
        _, e = rates_of(base_ref, gate_ref, h)
        score = dot(q, k, NT, 3)
        mix = jnp.where(i >= j, score * e, 0.0)
        inv = inv_ref[h]
        rv = dot(inv, v_ref[:, span(h)], NN, 3)
        y = dot(inv, k, NN, 3)
        score_ref[h] = score
        rv_ref[:, span(h)] = rv
        y_ref[:, span(h)] = y
        qt_ref[:, span(h)] = q - dot(mix, y, NN, 3)
        zv_ref[:, span(h)] = dot(mix, rv, NN, 3)


def step_kernel(d_ref, w_ref, o_ref, after_ref, out_ref):
    del after_ref
    for h in range(d_ref.shape[0]):
        out_ref[h] = o_ref[h] + dot(d_ref[h], w_ref[h], NN, 3)


def norm_kernel(
    pos_ref, init_ref, near_ref, mid_ref, far_ref, rd_ref, qt_ref, zv_ref, up_ref, gain_ref, after_ref,
    w_ref, h_ref, p_ref, dgain_ref,
):
    del after_ref
    ctx = pos_ref[4]
    heads = range(init_ref.shape[0])
    lasts = [dot(rd_ref[h], far_ref[h], NN, 3) + near_ref[h] for h in heads]
    starts = [
        jnp.where(
            ctx == 0, init_ref[h], jnp.where(ctx == 1, near_ref[h], jnp.where(ctx == 2, mid_ref[h], lasts[h]))
        )
        for h in heads
    ]
    qts = [qt_ref[:, span(h)] for h in heads]
    zs = [dot(qts[h], starts[h], NN, 3) + zv_ref[:, span(h)] for h in heads]
    ups = [up_ref[0, :, span(h)].astype(F32) for h in heads]
    centred = [z - jnp.mean(z, -1, keepdims=True) for z in zs]
    inv_stds = [lax.rsqrt(jnp.mean(c * c, -1, keepdims=True) + 1e-05) for c in centred]
    normed = [c * inv_std for c, inv_std in zip(centred, inv_stds)]
    weighted = [ups[h] * gain_ref[h : h + 1, :] for h in heads]
    backs = [
        inv_stds[h]
        * (
            weighted[h]
            - jnp.mean(weighted[h], -1, keepdims=True)
            - normed[h] * jnp.mean(weighted[h] * normed[h], -1, keepdims=True)
        )
        for h in heads
    ]
    pulled = [dot(qts[h], backs[h], TN, 3) for h in heads]
    for h in heads:
        w_ref[h] = starts[h]
        h_ref[:, span(h)] = backs[h]
        p_ref[h] = pulled[h]
        dgain_ref[h : h + 1, :] = jnp.sum(ups[h] * normed[h], axis=0, keepdims=True)


def query_kernel(
    base_ref, gate_ref, w_ref, h_ref, up_ref, q_ref, score_ref, rv_ref, y_ref, k_ref, inv_ref,
    dq_ref, r_ref, x_ref, dk_ref, de_ref,
):
    n = h_ref.shape[0]
    i, j = places(n)
    for h in range(w_ref.shape[0]):
        w = w_ref[h]
        back = h_ref[:, span(h)]
        k = k_ref[:, span(h)]
        q = q_ref[:, span(h)]
        score = score_ref[h]
        _, e = rates_of(base_ref, gate_ref, h)
        mix = jnp.where(i >= j, score * e, 0.0)
        r = rv_ref[:, span(h)] - dot(y_ref[:, span(h)], w, NN, 3)
        r_ref[:, span(h)] = r
        d_mix = jnp.where(i >= j, dot(back, r, NT, 3), 0.0)
        d_score = d_mix * e
        dq = up_ref[0, :, span(h)].astype(F32) + dot(back, w, NT, 3) + dot(d_score, k, NN, 3)
        dq_ref[:, span(h)] = dq.astype(BF).astype(F32)
        x_ref[:, span(h)] = dot(inv_ref[h], dot(mix, back, TN, 3), TN, 3)
        dk_ref[:, span(h)] = dot(d_score, q, TN, 3)
        de_ref[h : h + 1, :] = jnp.sum(d_mix * score, axis=0, keepdims=True)


def keys_kernel(
    pos_ref, base_ref, gate_ref, one_ref, two_ref, three_ref, rd_ref, rd_one_ref, rd_two_ref, p_ref, d_ref, w_ref, k_ref, ninv_ref,
    gram_ref, bt_ref, r_ref, x_ref, dk_ref, de_ref, dgain_ref, dq_ref,
    all_ref, gates_ref,
):
    ctx = pos_ref[4]
    n = k_ref.shape[0]
    i, j = places(n)
    strict = (i // MB) > (j // MB)
    heads = range(w_ref.shape[0])
    steps = [jnp.where(ctx == 0, rd_ref[h], rd_one_ref[h]) for h in heads]
    inner = [two_ref[h] + dot(rd_two_ref[h], three_ref[h], TN, 3) for h in heads]
    ends = [one_ref[h] + dot(steps[h], inner[h], TN, 3) for h in heads]
    ks = [k_ref[:, span(h)] for h in heads]
    rs = [r_ref[:, span(h)] for h in heads]
    rates = [rates_of(base_ref, gate_ref, h) for h in heads]
    xs = [x_ref[:, span(h)] + dot(bt_ref[h], ends[h], TN, 3) for h in heads]
    d_lows = [jnp.where(strict, -dot(xs[h], rs[h], NT, 3), 0.0) for h in heads]
    begins = [jnp.where(ctx == 0, p_ref[h] + dot(d_ref[h], ends[h], TN, 3), 0.0) for h in heads]
    pulls = [to_row(jnp.sum(rs[h] * dot(ks[h], ends[h], NN, 3), axis=1, keepdims=True)) for h in heads]
    dks = [
        dk_ref[:, span(h)] - dot(xs[h], w_ref[h], NT, 3) + to_col(rates[h][1]) * dot(rs[h], ends[h], NT, 3)
        for h in heads
    ]
    d_grams = [d_lows[h] * rates[h][1] for h in heads]
    dks = [dks[h] + dot(d_grams[h] + d_grams[h].T, ks[h], NN, 3) for h in heads]
    draws = [ninv_ref[h] * (dks[h] - ks[h] * jnp.sum(ks[h] * dks[h], -1, keepdims=True)) for h in heads]
    des = [
        de_ref[h : h + 1, :] + jnp.sum(d_lows[h] * gram_ref[h], axis=0, keepdims=True) + pulls[h] for h in heads
    ]
    all_ref[0:n, :] = dq_ref[...]
    all_ref[3 * n + HS : 3 * n + EXTRA, :] = jnp.zeros((EXTRA - HS, all_ref.shape[1]), F32)
    for h in heads:
        boost = rates[h][0]
        all_ref[n : 2 * n, span(h)] = draws[h].astype(BF).astype(F32)
        all_ref[2 * n : 3 * n, span(h)] = xs[h].astype(BF).astype(F32)
        all_ref[3 * n : 3 * n + HS, span(h)] = begins[h]
        d_boost = des[h] / ((1.0 + boost) * (1.0 + boost))
        gates_ref[0, h : h + 1, :] = d_boost * base_ref[h]
        all_ref[3 * n + HS : 3 * n + HS + 1, span(h)] = dgain_ref[h : h + 1, :]
        all_ref[3 * n + HS + 1 : 3 * n + HS + 2, span(h)] = jnp.broadcast_to(
            jnp.sum(d_boost * gate_ref[0, h : h + 1, :], axis=1, keepdims=True), (1, HS)
        )


def turn_kernel(other_ref, out_ref):
    out_ref[...] = other_ref[...].T.astype(BF)


def product_kernel(pos_ref, tokt_ref, other_tokt_ref, own_ref, other_ref, *refs):
    out_refs = refs[2 : 2 + RING]
    n = tokt_ref.shape[1]
    for turn, out_ref in zip(TURNS, out_refs):
        at = (pos_ref[1] + turn) & (RING - 1)
        rows = pl.ds(pl.multiple_of(at * CHUNK, CHUNK), CHUNK)
        for m in range(3):
            out_ref[m * CHUNK : (m + 1) * CHUNK, :] = jnp.dot(
                tokt_ref[rows, :], own_ref[m * n : (m + 1) * n, :].astype(BF), preferred_element_type=F32
            ) + jnp.dot(
                other_tokt_ref[rows, :], other_ref[m * n : (m + 1) * n, :].astype(BF), preferred_element_type=F32
            )
        extra = pl.ds(pl.multiple_of(3 * n + (pos_ref[0] * RING + at) * PIECE, 8), PIECE)
        out_ref[3 * CHUNK : 3 * CHUNK + PIECE, :] = own_ref[extra, :] + other_ref[extra, :]


def token_kernel(pos_ref, w_ref, all_ref, *out_refs):
    n = out_refs[0].shape[0]
    ds = [all_ref[m * n : (m + 1) * n, :].astype(BF) for m in range(3)]
    quarter = w_ref.shape[1] // RING
    for turn, out_ref in zip(TURNS, out_refs):
        at = (pos_ref[3] + turn) & (RING - 1)
        rows = pl.ds(pl.multiple_of(at * quarter, quarter), quarter)
        total = lax.dot_general(ds[0], w_ref[0, rows, :], NT, preferred_element_type=F32)
        total = total + lax.dot_general(ds[1], w_ref[1, rows, :], NT, preferred_element_type=F32)
        out_ref[...] = total + lax.dot_general(ds[2], w_ref[2, rows, :], NT, preferred_element_type=F32)


def slice_rows(pos_ref, turn):
    at = (pos_ref[2] + turn) & (RING - 1)
    taken = [
        (pl.ds(pl.multiple_of(m * CHUNK + at * SLICE, SLICE), SLICE), slice(m * SLICE, (m + 1) * SLICE))
        for m in range(3)
    ]
    few = PIECE // RING
    extra = pl.ds(pl.multiple_of(3 * CHUNK + at * few, few), few)
    return taken + [(extra, slice(3 * SLICE, 3 * SLICE + few))]


def split_kernel(pos_ref, own_ref, back_ref, ahead_ref, far_ref, *refs):
    for turn, out_ref in zip(TURNS, refs[-RING:]):
        for rows, to in slice_rows(pos_ref, turn):
            out_ref[to, :] = (own_ref[rows, :] + far_ref[rows, :]) + (back_ref[rows, :] + ahead_ref[rows, :])


def sum_kernel(own_ref, back_ref, ahead_ref, far_ref, out_ref):
    out_ref[...] = (own_ref[...] + far_ref[...]) + (back_ref[...] + ahead_ref[...])


def join_kernel(pos_ref, own_ref, ahead_ref, back_ref, far_ref, *refs):
    for turn, part_ref in zip(TURNS, (own_ref, ahead_ref, back_ref, far_ref)):
        for rows, to in slice_rows(pos_ref, turn):
            refs[-1][rows, :] = part_ref[to, :]


def place_kernel(pos_ref, *refs, which, passed):
    pieces = refs[: len(which)]
    out_ref, sem = refs[-3 if passed else -2], refs[-1]
    copies = []
    for g, ((half, m), piece) in enumerate(zip(which, pieces)):
        core = pos_ref[0] if half == 0 else 1 - pos_ref[0]
        at = core * RING + ((pos_ref[1 + half] + TURNS[m]) & (RING - 1))
        rows = pl.ds(pl.multiple_of(at * CHUNK, CHUNK), CHUNK)
        for s in range(3):
            copies.append(
                pltpu.make_async_copy(piece.at[pl.ds(s * CHUNK, CHUNK), :], out_ref.at[s, rows, :], sem.at[s, g])
            )
    for copy in copies:
        copy.start()
    if passed:
        refs[-2][...] = pieces[0][...]
    for copy in copies:
        copy.wait()


def last_kernel(pos_ref, *refs, which):
    pieces = refs[: 2 * RING]
    out_ref, init_ref, gain_ref, rates_ref, extra_ref, sem = refs[-6:]
    copies = []
    for g, (half, m) in enumerate(which):
        core = pos_ref[0] if half == 0 else 1 - pos_ref[0]
        at = core * RING + ((pos_ref[1 + half] + TURNS[m]) & (RING - 1))
        rows = pl.ds(pl.multiple_of(at * CHUNK, CHUNK), CHUNK)
        for s in range(3):
            copies.append(
                pltpu.make_async_copy(
                    pieces[half * RING + m].at[pl.ds(s * CHUNK, CHUNK), :], out_ref.at[s, rows, :], sem.at[s, g]
                )
            )
    for copy in copies:
        copy.start()
    for p, piece in enumerate(pieces):
        core = pos_ref[0] if p < RING else 1 - pos_ref[0]
        at = core * RING + ((pos_ref[1 + p // RING] + TURNS[p % RING]) & (RING - 1))
        extra_ref[pl.ds(pl.multiple_of(at * PIECE, 8), PIECE), :] = piece[3 * CHUNK : 3 * CHUNK + PIECE, :]
    for h in range(init_ref.shape[0]):
        init_ref[h] = extra_ref[0:HS, span(h)]
        gain_ref[h : h + 1, :] = extra_ref[HS : HS + 1, span(h)]
        rates_ref[h] = extra_ref[HS + 1, h * HS]
    for copy in copies:
        copy.wait()


def moves(first, by):
    pairs = []
    for x in range(RING):
        for core in range(2):
            for y in range(RING):
                along_x = (core == 0) == first
                to_x = (x + by) % RING if along_x else x
                to_y = y if along_x else (y + by) % RING
                pairs.append(((x * 2 + core) * RING + y, (to_x * 2 + core) * RING + to_y))
    return pairs


def round_turn(chunks, first):
    return [
        lax.ppermute(chunk, ("dp", "ctx"), moves(first, turn)) for chunk, turn in zip(chunks, TURNS[1:])
    ]


def swap(value):
    return lax.ppermute(value, "dp", [(i, i ^ 1) for i in range(2 * RING)])


VM = pl.BlockSpec(memory_space=pltpu.VMEM)
SM = pl.BlockSpec(memory_space=pltpu.SMEM)
PARAMS = pltpu.CompilerParams(vmem_limit_bytes=20 * 1024 * 1024)


def shape(*dims, dtype=F32):
    return jax.ShapeDtypeStruct(dims, dtype)


def vmem(*dims, dtype=F32):
    return pltpu.VMEM(dims, dtype)


def hbm(value):
    return pltpu.with_memory_space_constraint(value, pltpu.HBM)


def whole(kernel, outs, specs, aliases=None):
    return pl.pallas_call(
        kernel,
        out_shape=outs,
        in_specs=specs,
        out_specs=tuple(VM for _ in outs) if isinstance(outs, tuple) else VM,
        input_output_aliases=aliases or {},
        compiler_params=PARAMS,
    )


def part(which, dims):
    return pl.BlockSpec((1,) + dims, lambda i: (which, 0, 0))


def full(*dims):
    return pl.BlockSpec(dims, lambda i: (0,) * len(dims))


def body(tokens, proj_weights, init_weight, base_rates, gate_values, out_gain, cotangent):
    n = tokens.shape[1]
    model = tokens.shape[2]
    heads = init_weight.shape[0]
    wide = heads * HS
    ctx = lax.axis_index("ctx")
    dp = lax.axis_index("dp")
    core, x_at = dp % 2, dp // 2
    pos = jnp.stack(
        [core, jnp.where(core == 0, x_at, ctx), jnp.where(core == 0, ctx, x_at), lax.axis_index("head"), ctx]
    ).astype(jnp.int32)
    half = model // 2

    wide_f32 = vmem(n, wide)
    square = vmem(heads, n, n)
    small = vmem(heads, HS, HS)
    wspec = functools.partial(part, dims=(model, wide))
    tokens = hbm(tokens)
    raw_weights = proj_weights
    proj_weights = hbm(proj_weights)
    anywhere = pl.BlockSpec(memory_space=pl.ANY)

    k, v, ninv, gram, inv, bt, decay, send, offset, other_half = pl.pallas_call(
        maps_kernel,
        grid=(1,),
        out_shape=(
            wide_f32, wide_f32, vmem(heads, n, HS), square, square, vmem(heads, HS, n), small, small, small,
            vmem(n, half),
        ),
        in_specs=[SM, SM, full(1, n, model), wspec(1), wspec(2), full(1, heads, n), full(heads, HS, HS)],
        out_specs=(VM,) * 10,
        compiler_params=PARAMS,
    )(pos, hbm(base_rates), tokens, proj_weights, proj_weights, hbm(gate_values), hbm(init_weight))

    near = lax.ppermute(send, "ctx", [(0, 1), (2, 3)])
    moved = lax.ppermute(decay, "ctx", [(2, 3), (1, 0)])
    moved_one = lax.ppermute(decay, "ctx", [(2, 1)])
    moved_two = lax.ppermute(decay, "ctx", [(2, 0)])
    got_half = swap(other_half)

    q, score, rv, y, qt, zv, tokt = pl.pallas_call(
        reach_kernel,
        grid=(1,),
        out_shape=(wide_f32, square, wide_f32, wide_f32, wide_f32, wide_f32, vmem(half, n, dtype=BF)),
        in_specs=[SM, SM, full(1, n, model), wspec(0), full(1, heads, n), VM, VM, VM],
        out_specs=(VM,) * 7,
        compiler_params=PARAMS,
    )(pos, base_rates, tokens, proj_weights, gate_values, k, v, inv)

    second = whole(step_kernel, small, [VM] * 3 + [anywhere])(
        decay, near, offset, qt
    )
    mid = lax.ppermute(second, "ctx", [(1, 2)])
    far = lax.ppermute(second, "ctx", [(1, 3)])
    other_tokt = whole(turn_kernel, vmem(half, n, dtype=BF), [VM])(got_half)

    w, back, pulled, dgain = whole(
        norm_kernel, (small, wide_f32, small, vmem(heads, HS)), [SM] + [VM] * 9 + [anywhere]
    )(pos, init_weight, near, mid, far, moved, qt, zv, cotangent, out_gain, other_tokt)

    back_one = lax.ppermute(pulled, "ctx", [(3, 2), (2, 1), (1, 0)])
    back_two = lax.ppermute(pulled, "ctx", [(3, 1), (2, 0)])
    back_three = lax.ppermute(pulled, "ctx", [(3, 0)])

    dq, r, x, dk, de = whole(
        query_kernel, (wide_f32, wide_f32, wide_f32, wide_f32, vmem(heads, n)), [SM] + [VM] * 10
    )(base_rates, gate_values, w, back, cotangent, q, score, rv, y, k, inv)

    grads, grad_gates = whole(
        keys_kernel, (vmem(3 * n + EXTRA, wide), shape(1, heads, n)), [SM, SM] + [VM] * 20
    )(pos, base_rates, gate_values, back_one, back_two, back_three, moved, moved_one, moved_two, pulled, decay, w, k, ninv, gram, bt, r, x,
      dk, de, dgain, dq)

    chunk = vmem(3 * CHUNK + PIECE, wide)
    quarter = vmem(n, model // RING)
    quarters = whole(token_kernel, (quarter,) * RING, [SM, VM, VM])(pos, raw_weights, grads)

    def along_head(terms, turn):
        return lax.ppermute(terms, "head", [(i, (i + turn) % RING) for i in range(RING)])

    *chunks, near_two, far_quarter = whole(
        product_kernel, (chunk,) * RING + (quarter,) * 2, [SM] + [VM] * 6, {5: RING, 6: RING + 1}
    )(pos, tokt, other_tokt, grads, swap(grads), *quarters[2:])
    own, away = chunks[0], round_turn(chunks[1:], True)
    from_back, from_ahead, from_far = along_head(quarters[1], 1), along_head(near_two, 3), along_head(far_quarter, 2)

    piece = vmem(3 * SLICE + PIECE // RING, wide)
    pieces = whole(split_kernel, (piece,) * RING, [SM] + [VM] * 4 + [anywhere])(pos, own, *away, from_back)
    grad_tokens = ((quarters[0] + from_far) + (from_back + from_ahead)).astype(BF).reshape(1, n, -1)
    own, away = pieces[0], pieces[1:]
    part_sum = whole(sum_kernel, piece, [VM] * 4)(own, *round_turn(away, False))
    from_back, from_ahead, from_far = round_turn([part_sum] * 3, False)
    total = whole(join_kernel, chunk, [SM] + [VM] * 4 + [anywhere])(
        pos, part_sum, from_ahead, from_back, from_far, grad_tokens
    )
    from_back, from_ahead, from_far = round_turn([total] * 3, True)
    out = shape(3, model, wide)

    def place(which, passed, *placed):
        given = [sides[half][m] for half, m in which]
        return pl.pallas_call(
            functools.partial(place_kernel, which=which, passed=passed),
            out_shape=(out, chunk) if passed else (out,),
            in_specs=[SM] + [VM] * len(given) + [anywhere] * len(placed),
            out_specs=(anywhere, VM) if passed else (anywhere,),
            scratch_shapes=[pltpu.SemaphoreType.DMA((3, len(which)))],
            input_output_aliases={len(given) + 1: 0} if placed else {},
            compiler_params=PARAMS,
        )(pos, *given, *placed)

    mine, others = [total, from_ahead, from_back, from_far], []
    sides = (mine, others)
    placed, own_piece = place(((0, 0), (0, 3)), True)
    others += [swap(given) for given in [own_piece] + mine[1:]]
    (placed,) = place(((0, 1), (0, 2), (1, 0), (1, 3)), False, placed)
    which = ((1, 1), (1, 2))
    grad_proj, grad_init, grad_gain, grad_rates = pl.pallas_call(
        functools.partial(last_kernel, which=which),
        out_shape=(out, shape(heads, HS, HS), shape(heads, HS), shape(heads)),
        in_specs=[SM] + [VM] * 8 + [anywhere],
        out_specs=(anywhere, VM, VM, SM),
        scratch_shapes=[pltpu.VMEM((EXTRA, wide), F32), pltpu.SemaphoreType.DMA((3, len(which)))],
        input_output_aliases={9: 0},
        compiler_params=PARAMS,
    )(pos, *mine, *others, placed)
    return (grad_tokens, grad_proj, grad_init, grad_gain, grad_rates, grad_gates)


def solution(mesh):
    in_specs = (
        P("dp", "ctx", None),
        P(None, None, "head"),
        P("head", None, None),
        P("head"),
        P("dp", "head", "ctx"),
        P("head", None),
        P("dp", "ctx", "head"),
    )
    out_specs = (
        P("dp", "ctx", "head"),
        P(None, None, "head"),
        P("head", None, None),
        P("head", None),
        P("head"),
        P("dp", "head", "ctx"),
    )
    return jax.shard_map(body, mesh=mesh, in_specs=in_specs, out_specs=out_specs, check_vma=False)
```

```python
import functools

import jax
import jax.numpy as jnp
from jax import lax
from jax.experimental import pallas as pl
from jax.experimental.pallas import tpu as pltpu
from jax.sharding import PartitionSpec as P

MB = 16
HS = 128
RING = 4
TURNS = (0, 1, 3, 2)
CHUNK = 256
PIECE = 24
EXTRA = 2 * RING * PIECE
F32 = jnp.float32
BF = jnp.bfloat16
NN = (((1,), (0,)), ((), ()))
NT = (((1,), (1,)), ((), ()))
TN = (((0,), (0,)), ((), ()))


def dot(a, b, dims, passes):
    ah = a.astype(BF)
    bh = b.astype(BF)
    result = lax.dot_general(ah, bh, dims, preferred_element_type=F32)
    if passes == 3:
        al = (a - ah.astype(F32)).astype(BF)
        bl = (b - bh.astype(F32)).astype(BF)
        result = result + (
            lax.dot_general(ah, bl, dims, preferred_element_type=F32)
            + lax.dot_general(al, bh, dims, preferred_element_type=F32)
        )
    return result


def places(n):
    return (
        lax.broadcasted_iota(jnp.int32, (n, n), 0),
        lax.broadcasted_iota(jnp.int32, (n, n), 1),
    )


def to_col(row):
    i, j = places(row.shape[1])
    return jnp.sum(jnp.where(i == j, row, 0.0), axis=1, keepdims=True)


def to_row(col):
    i, j = places(col.shape[0])
    return jnp.sum(jnp.where(i == j, col, 0.0), axis=0, keepdims=True)


def unit_lower_inverses(lowers):
    n = lowers[0].shape[0]
    i, j = places(n)
    size = 2 * MB
    same = (i // size) == (j // size)
    inverses = [jnp.where(i == j, 1.0, 0.0) - jnp.where(same, low, 0.0) for low in lowers]
    while size < n:
        pair = ((i // (2 * size)) == (j // (2 * size))) & ((i // size) != (j // size))
        corners = [jnp.where(pair, low, 0.0) for low in lowers]
        halves = [dot(inv, corner, NN, 3) for inv, corner in zip(inverses, corners)]
        inverses = [inv - dot(half, inv, NN, 3) for inv, half in zip(inverses, halves)]
        size *= 2
    return inverses


def span(h):
    return slice(h * HS, (h + 1) * HS)


def rates_of(base_ref, gate_ref, h):
    boost = base_ref[h] * gate_ref[0, h : h + 1, :]
    return boost, boost / (1.0 + boost)


def maps_kernel(
    pos_ref, base_ref, tok_ref, wk_ref, wv_ref, gate_ref, init_ref,
    k_ref, v_ref, ninv_ref, gram_ref, inv_ref, bt_ref, d_ref, send_ref, o_ref, half_ref,
):
    half = tok_ref.shape[2] // 2
    columns = pl.ds(pl.multiple_of((1 - pos_ref[0]) * half, half), half)
    half_ref[...] = tok_ref[0, :, columns].astype(F32)
    tok = tok_ref[0]
    kraw_all = jnp.dot(tok, wk_ref[0], preferred_element_type=F32).astype(BF).astype(F32)
    v_all = jnp.dot(tok, wv_ref[0], preferred_element_type=F32).astype(BF).astype(F32)
    n = kraw_all.shape[0]
    i, j = places(n)
    strict = (i // MB) > (j // MB)
    heads = range(init_ref.shape[0])
    kraws = [kraw_all[:, span(h)] for h in heads]
    ninvs = [lax.rsqrt(jnp.sum(kraw * kraw, -1, keepdims=True) + 1e-06) for kraw in kraws]
    ks = [kraw * ninv for kraw, ninv in zip(kraws, ninvs)]
    kts = [k.T for k in ks]
    es = [rates_of(base_ref, gate_ref, h)[1] for h in heads]
    grams = [dot(k, kt, NN, 3) for k, kt in zip(ks, kts)]
    inverses = unit_lower_inverses([jnp.where(strict, gram * e, 0.0) for gram, e in zip(grams, es)])
    a, b = places(HS)
    bts = [dot(kts[h] * es[h], inverses[h], NN, 3) for h in heads]
    decays = [jnp.where(a == b, 1.0, 0.0) - dot(bts[h], ks[h], NN, 3) for h in heads]
    offsets = [dot(bts[h], v_all[:, span(h)], NN, 3) for h in heads]
    firsts = [dot(decays[h], init_ref[h], NN, 3) + offsets[h] for h in heads]
    v_ref[...] = v_all
    for h in heads:
        send_ref[h] = jnp.where(pos_ref[4] == 0, firsts[h], offsets[h])
        d_ref[h] = decays[h]
        o_ref[h] = offsets[h]
        k_ref[:, span(h)] = ks[h]
        ninv_ref[h] = jnp.broadcast_to(ninvs[h], (n, HS))
        gram_ref[h] = grams[h]
        inv_ref[h] = inverses[h]
        bt_ref[h] = bts[h]


def reach_kernel(
    pos_ref, base_ref, tok_ref, wq_ref, gate_ref, k_ref, v_ref, inv_ref,
    q_ref, score_ref, rv_ref, y_ref, qt_ref, zv_ref, tokt_ref,
):
    half = tok_ref.shape[2] // 2
    columns = pl.ds(pl.multiple_of(pos_ref[0] * half, half), half)
    tokt_ref[...] = tok_ref[0, :, columns].astype(F32).T.astype(BF)
    q_all = jnp.dot(tok_ref[0], wq_ref[0], preferred_element_type=F32).astype(BF).astype(F32)
    n = q_all.shape[0]
    i, j = places(n)
    q_ref[...] = q_all
    for h in range(inv_ref.shape[0]):
        q = q_all[:, span(h)]
        k = k_ref[:, span(h)]
        _, e = rates_of(base_ref, gate_ref, h)
        score = dot(q, k, NT, 3)
        mix = jnp.where(i >= j, score * e, 0.0)
        inv = inv_ref[h]
        rv = dot(inv, v_ref[:, span(h)], NN, 3)
        y = dot(inv, k, NN, 3)
        score_ref[h] = score
        rv_ref[:, span(h)] = rv
        y_ref[:, span(h)] = y
        qt_ref[:, span(h)] = q - dot(mix, y, NN, 3)
        zv_ref[:, span(h)] = dot(mix, rv, NN, 3)


def step_kernel(d_ref, w_ref, o_ref, after_ref, out_ref):
    del after_ref
    for h in range(d_ref.shape[0]):
        out_ref[h] = o_ref[h] + dot(d_ref[h], w_ref[h], NN, 3)


def norm_kernel(
    pos_ref, init_ref, near_ref, mid_ref, far_ref, rd_ref, qt_ref, zv_ref, up_ref, gain_ref, after_ref,
    w_ref, h_ref, p_ref, dgain_ref,
):
    del after_ref
    ctx = pos_ref[4]
    heads = range(init_ref.shape[0])
    lasts = [dot(rd_ref[h], far_ref[h], NN, 3) + near_ref[h] for h in heads]
    starts = [
        jnp.where(
            ctx == 0, init_ref[h], jnp.where(ctx == 1, near_ref[h], jnp.where(ctx == 2, mid_ref[h], lasts[h]))
        )
        for h in heads
    ]
    qts = [qt_ref[:, span(h)] for h in heads]
    zs = [dot(qts[h], starts[h], NN, 3) + zv_ref[:, span(h)] for h in heads]
    ups = [up_ref[0, :, span(h)].astype(F32) for h in heads]
    centred = [z - jnp.mean(z, -1, keepdims=True) for z in zs]
    inv_stds = [lax.rsqrt(jnp.mean(c * c, -1, keepdims=True) + 1e-05) for c in centred]
    normed = [c * inv_std for c, inv_std in zip(centred, inv_stds)]
    weighted = [ups[h] * gain_ref[h : h + 1, :] for h in heads]
    backs = [
        inv_stds[h]
        * (
            weighted[h]
            - jnp.mean(weighted[h], -1, keepdims=True)
            - normed[h] * jnp.mean(weighted[h] * normed[h], -1, keepdims=True)
        )
        for h in heads
    ]
    pulled = [dot(qts[h], backs[h], TN, 3) for h in heads]
    for h in heads:
        w_ref[h] = starts[h]
        h_ref[:, span(h)] = backs[h]
        p_ref[h] = pulled[h]
        dgain_ref[h : h + 1, :] = jnp.sum(ups[h] * normed[h], axis=0, keepdims=True)


def query_kernel(
    base_ref, gate_ref, w_ref, h_ref, up_ref, q_ref, score_ref, rv_ref, y_ref, k_ref, inv_ref,
    dq_ref, r_ref, x_ref, dk_ref, de_ref,
):
    n = h_ref.shape[0]
    i, j = places(n)
    for h in range(w_ref.shape[0]):
        w = w_ref[h]
        back = h_ref[:, span(h)]
        k = k_ref[:, span(h)]
        q = q_ref[:, span(h)]
        score = score_ref[h]
        _, e = rates_of(base_ref, gate_ref, h)
        mix = jnp.where(i >= j, score * e, 0.0)
        r = rv_ref[:, span(h)] - dot(y_ref[:, span(h)], w, NN, 3)
        r_ref[:, span(h)] = r
        d_mix = jnp.where(i >= j, dot(back, r, NT, 3), 0.0)
        d_score = d_mix * e
        dq = up_ref[0, :, span(h)].astype(F32) + dot(back, w, NT, 3) + dot(d_score, k, NN, 3)
        dq_ref[:, span(h)] = dq.astype(BF).astype(F32)
        x_ref[:, span(h)] = dot(inv_ref[h], dot(mix, back, TN, 3), TN, 3)
        dk_ref[:, span(h)] = dot(d_score, q, TN, 3)
        de_ref[h : h + 1, :] = jnp.sum(d_mix * score, axis=0, keepdims=True)


def keys_kernel(
    pos_ref, base_ref, gate_ref, one_ref, two_ref, three_ref, rd_ref, rd_one_ref, rd_two_ref, p_ref, d_ref, w_ref, k_ref, ninv_ref,
    gram_ref, bt_ref, r_ref, x_ref, dk_ref, de_ref, dgain_ref, dq_ref,
    all_ref, gates_ref,
):
    ctx = pos_ref[4]
    n = k_ref.shape[0]
    i, j = places(n)
    strict = (i // MB) > (j // MB)
    heads = range(w_ref.shape[0])
    steps = [jnp.where(ctx == 0, rd_ref[h], rd_one_ref[h]) for h in heads]
    inner = [two_ref[h] + dot(rd_two_ref[h], three_ref[h], TN, 3) for h in heads]
    ends = [one_ref[h] + dot(steps[h], inner[h], TN, 3) for h in heads]
    ks = [k_ref[:, span(h)] for h in heads]
    rs = [r_ref[:, span(h)] for h in heads]
    rates = [rates_of(base_ref, gate_ref, h) for h in heads]
    xs = [x_ref[:, span(h)] + dot(bt_ref[h], ends[h], TN, 3) for h in heads]
    d_lows = [jnp.where(strict, -dot(xs[h], rs[h], NT, 3), 0.0) for h in heads]
    begins = [jnp.where(ctx == 0, p_ref[h] + dot(d_ref[h], ends[h], TN, 3), 0.0) for h in heads]
    pulls = [to_row(jnp.sum(rs[h] * dot(ks[h], ends[h], NN, 3), axis=1, keepdims=True)) for h in heads]
    dks = [
        dk_ref[:, span(h)] - dot(xs[h], w_ref[h], NT, 3) + to_col(rates[h][1]) * dot(rs[h], ends[h], NT, 3)
        for h in heads
    ]
    d_grams = [d_lows[h] * rates[h][1] for h in heads]
    dks = [dks[h] + dot(d_grams[h] + d_grams[h].T, ks[h], NN, 3) for h in heads]
    draws = [ninv_ref[h] * (dks[h] - ks[h] * jnp.sum(ks[h] * dks[h], -1, keepdims=True)) for h in heads]
    des = [
        de_ref[h : h + 1, :] + jnp.sum(d_lows[h] * gram_ref[h], axis=0, keepdims=True) + pulls[h] for h in heads
    ]
    all_ref[0:n, :] = dq_ref[...]
    all_ref[3 * n + HS : 3 * n + EXTRA, :] = jnp.zeros((EXTRA - HS, all_ref.shape[1]), F32)
    for h in heads:
        boost = rates[h][0]
        all_ref[n : 2 * n, span(h)] = draws[h].astype(BF).astype(F32)
        all_ref[2 * n : 3 * n, span(h)] = xs[h].astype(BF).astype(F32)
        all_ref[3 * n : 3 * n + HS, span(h)] = begins[h]
        d_boost = des[h] / ((1.0 + boost) * (1.0 + boost))
        gates_ref[0, h : h + 1, :] = d_boost * base_ref[h]
        all_ref[3 * n + HS : 3 * n + HS + 1, span(h)] = dgain_ref[h : h + 1, :]
        all_ref[3 * n + HS + 1 : 3 * n + HS + 2, span(h)] = jnp.broadcast_to(
            jnp.sum(d_boost * gate_ref[0, h : h + 1, :], axis=1, keepdims=True), (1, HS)
        )


def turn_kernel(other_ref, out_ref):
    out_ref[...] = other_ref[...].T.astype(BF)


def product_kernel(pos_ref, tokt_ref, other_tokt_ref, own_ref, other_ref, *refs):
    out_refs = refs[2 : 2 + RING]
    n = tokt_ref.shape[1]
    for turn, out_ref in zip(TURNS, out_refs):
        at = (pos_ref[1] + turn) & (RING - 1)
        rows = pl.ds(pl.multiple_of(at * CHUNK, CHUNK), CHUNK)
        for m in range(3):
            out_ref[m * CHUNK : (m + 1) * CHUNK, :] = jnp.dot(
                tokt_ref[rows, :], own_ref[m * n : (m + 1) * n, :].astype(BF), preferred_element_type=F32
            ) + jnp.dot(
                other_tokt_ref[rows, :], other_ref[m * n : (m + 1) * n, :].astype(BF), preferred_element_type=F32
            )
        extra = pl.ds(pl.multiple_of(3 * n + (pos_ref[0] * RING + at) * PIECE, 8), PIECE)
        out_ref[3 * CHUNK : 3 * CHUNK + PIECE, :] = own_ref[extra, :] + other_ref[extra, :]


def token_kernel(pos_ref, w_ref, all_ref, *out_refs):
    n = out_refs[0].shape[0]
    ds = [all_ref[m * n : (m + 1) * n, :].astype(BF) for m in range(3)]
    quarter = w_ref.shape[1] // RING
    for turn, out_ref in zip(TURNS, out_refs):
        at = (pos_ref[3] + turn) & (RING - 1)
        rows = pl.ds(pl.multiple_of(at * quarter, quarter), quarter)
        total = lax.dot_general(ds[0], w_ref[0, rows, :], NT, preferred_element_type=F32)
        total = total + lax.dot_general(ds[1], w_ref[1, rows, :], NT, preferred_element_type=F32)
        out_ref[...] = total + lax.dot_general(ds[2], w_ref[2, rows, :], NT, preferred_element_type=F32)


def sum_kernel(own_ref, back_ref, ahead_ref, far_ref, *refs):
    refs[-1][...] = (own_ref[...] + far_ref[...]) + (back_ref[...] + ahead_ref[...])


def place_kernel(pos_ref, *refs, which, passed):
    pieces = refs[: len(which)]
    out_ref, sem = refs[-3 if passed else -2], refs[-1]
    copies = []
    for g, ((half, m), piece) in enumerate(zip(which, pieces)):
        core = pos_ref[0] if half == 0 else 1 - pos_ref[0]
        at = core * RING + ((pos_ref[1 + half] + TURNS[m]) & (RING - 1))
        rows = pl.ds(pl.multiple_of(at * CHUNK, CHUNK), CHUNK)
        for s in range(3):
            copies.append(
                pltpu.make_async_copy(piece.at[pl.ds(s * CHUNK, CHUNK), :], out_ref.at[s, rows, :], sem.at[s, g])
            )
    for copy in copies:
        copy.start()
    if passed:
        refs[-2][...] = pieces[0][...]
    for copy in copies:
        copy.wait()


def last_kernel(pos_ref, *refs, which):
    pieces = refs[: 2 * RING]
    out_ref, init_ref, gain_ref, rates_ref, extra_ref, sem = refs[-6:]
    copies = []
    for g, (half, m) in enumerate(which):
        core = pos_ref[0] if half == 0 else 1 - pos_ref[0]
        at = core * RING + ((pos_ref[1 + half] + TURNS[m]) & (RING - 1))
        rows = pl.ds(pl.multiple_of(at * CHUNK, CHUNK), CHUNK)
        for s in range(3):
            copies.append(
                pltpu.make_async_copy(
                    pieces[half * RING + m].at[pl.ds(s * CHUNK, CHUNK), :], out_ref.at[s, rows, :], sem.at[s, g]
                )
            )
    for copy in copies:
        copy.start()
    for p, piece in enumerate(pieces):
        core = pos_ref[0] if p < RING else 1 - pos_ref[0]
        at = core * RING + ((pos_ref[1 + p // RING] + TURNS[p % RING]) & (RING - 1))
        extra_ref[pl.ds(pl.multiple_of(at * PIECE, 8), PIECE), :] = piece[3 * CHUNK : 3 * CHUNK + PIECE, :]
    for h in range(init_ref.shape[0]):
        init_ref[h] = extra_ref[0:HS, span(h)]
        gain_ref[h : h + 1, :] = extra_ref[HS : HS + 1, span(h)]
        rates_ref[h] = extra_ref[HS + 1, h * HS]
    for copy in copies:
        copy.wait()


def moves(first, by):
    pairs = []
    for x in range(RING):
        for core in range(2):
            for y in range(RING):
                along_x = (core == 0) == first
                to_x = (x + by) % RING if along_x else x
                to_y = y if along_x else (y + by) % RING
                pairs.append(((x * 2 + core) * RING + y, (to_x * 2 + core) * RING + to_y))
    return pairs


def round_turn(chunks, first):
    return [
        lax.ppermute(chunk, ("dp", "ctx"), moves(first, turn)) for chunk, turn in zip(chunks, TURNS[1:])
    ]


def swap(value):
    return lax.ppermute(value, "dp", [(i, i ^ 1) for i in range(2 * RING)])


VM = pl.BlockSpec(memory_space=pltpu.VMEM)
SM = pl.BlockSpec(memory_space=pltpu.SMEM)
PARAMS = pltpu.CompilerParams(vmem_limit_bytes=20 * 1024 * 1024)


def shape(*dims, dtype=F32):
    return jax.ShapeDtypeStruct(dims, dtype)


def vmem(*dims, dtype=F32):
    return pltpu.VMEM(dims, dtype)


def hbm(value):
    return pltpu.with_memory_space_constraint(value, pltpu.HBM)


def whole(kernel, outs, specs, aliases=None):
    return pl.pallas_call(
        kernel,
        out_shape=outs,
        in_specs=specs,
        out_specs=tuple(VM for _ in outs) if isinstance(outs, tuple) else VM,
        input_output_aliases=aliases or {},
        compiler_params=PARAMS,
    )


def part(which, dims):
    return pl.BlockSpec((1,) + dims, lambda i: (which, 0, 0))


def full(*dims):
    return pl.BlockSpec(dims, lambda i: (0,) * len(dims))


def body(tokens, proj_weights, init_weight, base_rates, gate_values, out_gain, cotangent):
    n = tokens.shape[1]
    model = tokens.shape[2]
    heads = init_weight.shape[0]
    wide = heads * HS
    ctx = lax.axis_index("ctx")
    dp = lax.axis_index("dp")
    core, x_at = dp % 2, dp // 2
    pos = jnp.stack(
        [core, jnp.where(core == 0, x_at, ctx), jnp.where(core == 0, ctx, x_at), lax.axis_index("head"), ctx]
    ).astype(jnp.int32)
    half = model // 2

    wide_f32 = vmem(n, wide)
    square = vmem(heads, n, n)
    small = vmem(heads, HS, HS)
    wspec = functools.partial(part, dims=(model, wide))
    tokens = hbm(tokens)
    raw_weights = proj_weights
    proj_weights = hbm(proj_weights)
    anywhere = pl.BlockSpec(memory_space=pl.ANY)

    k, v, ninv, gram, inv, bt, decay, send, offset, other_half = pl.pallas_call(
        maps_kernel,
        grid=(1,),
        out_shape=(
            wide_f32, wide_f32, vmem(heads, n, HS), square, square, vmem(heads, HS, n), small, small, small,
            vmem(n, half),
        ),
        in_specs=[SM, SM, full(1, n, model), wspec(1), wspec(2), full(1, heads, n), full(heads, HS, HS)],
        out_specs=(VM,) * 10,
        compiler_params=PARAMS,
    )(pos, hbm(base_rates), tokens, proj_weights, proj_weights, hbm(gate_values), hbm(init_weight))

    near = lax.ppermute(send, "ctx", [(0, 1), (2, 3)])
    moved = lax.ppermute(decay, "ctx", [(2, 3), (1, 0)])
    moved_one = lax.ppermute(decay, "ctx", [(2, 1)])
    moved_two = lax.ppermute(decay, "ctx", [(2, 0)])
    got_half = swap(other_half)

    q, score, rv, y, qt, zv, tokt = pl.pallas_call(
        reach_kernel,
        grid=(1,),
        out_shape=(wide_f32, square, wide_f32, wide_f32, wide_f32, wide_f32, vmem(half, n, dtype=BF)),
        in_specs=[SM, SM, full(1, n, model), wspec(0), full(1, heads, n), VM, VM, VM],
        out_specs=(VM,) * 7,
        compiler_params=PARAMS,
    )(pos, base_rates, tokens, proj_weights, gate_values, k, v, inv)

    second = whole(step_kernel, small, [VM] * 3 + [anywhere])(
        decay, near, offset, qt
    )
    mid = lax.ppermute(second, "ctx", [(1, 2)])
    far = lax.ppermute(second, "ctx", [(1, 3)])
    other_tokt = whole(turn_kernel, vmem(half, n, dtype=BF), [VM])(got_half)

    w, back, pulled, dgain = whole(
        norm_kernel, (small, wide_f32, small, vmem(heads, HS)), [SM] + [VM] * 9 + [anywhere]
    )(pos, init_weight, near, mid, far, moved, qt, zv, cotangent, out_gain, other_tokt)

    back_one = lax.ppermute(pulled, "ctx", [(3, 2), (2, 1), (1, 0)])
    back_two = lax.ppermute(pulled, "ctx", [(3, 1), (2, 0)])
    back_three = lax.ppermute(pulled, "ctx", [(3, 0)])

    dq, r, x, dk, de = whole(
        query_kernel, (wide_f32, wide_f32, wide_f32, wide_f32, vmem(heads, n)), [SM] + [VM] * 10
    )(base_rates, gate_values, w, back, cotangent, q, score, rv, y, k, inv)

    grads, grad_gates = whole(
        keys_kernel, (vmem(3 * n + EXTRA, wide), shape(1, heads, n)), [SM, SM] + [VM] * 20
    )(pos, base_rates, gate_values, back_one, back_two, back_three, moved, moved_one, moved_two, pulled, decay, w, k, ninv, gram, bt, r, x,
      dk, de, dgain, dq)

    chunk = vmem(3 * CHUNK + PIECE, wide)
    quarter = vmem(n, model // RING)
    quarters = whole(token_kernel, (quarter,) * RING, [SM, VM, VM])(pos, raw_weights, grads)

    def along_head(terms, turn):
        return lax.ppermute(terms, "head", [(i, (i + turn) % RING) for i in range(RING)])

    *chunks, near_one, near_two = whole(
        product_kernel, (chunk,) * RING + (quarter,) * 2, [SM] + [VM] * 6, {5: RING, 6: RING + 1}
    )(pos, tokt, other_tokt, grads, swap(grads), *quarters[1:3])
    own, away = chunks[0], round_turn(chunks[1:], True)
    from_back, from_ahead, from_far = along_head(near_one, 1), along_head(near_two, 3), along_head(quarters[3], 2)

    part_sum = whole(sum_kernel, chunk, [VM] * 4 + [anywhere] * 2)(own, *away, from_back, from_ahead)
    grad_tokens = ((quarters[0] + from_far) + (from_back + from_ahead)).astype(BF).reshape(1, n, -1)
    total = whole(sum_kernel, chunk, [VM] * 4 + [anywhere])(
        part_sum, *round_turn([part_sum] * 3, False), grad_tokens
    )
    from_back, from_ahead, from_far = round_turn([total] * 3, True)
    out = shape(3, model, wide)

    def place(which, passed, *placed):
        given = [sides[half][m] for half, m in which]
        return pl.pallas_call(
            functools.partial(place_kernel, which=which, passed=passed),
            out_shape=(out, chunk) if passed else (out,),
            in_specs=[SM] + [VM] * len(given) + [anywhere] * len(placed),
            out_specs=(anywhere, VM) if passed else (anywhere,),
            scratch_shapes=[pltpu.SemaphoreType.DMA((3, len(which)))],
            input_output_aliases={len(given) + 1: 0} if placed else {},
            compiler_params=PARAMS,
        )(pos, *given, *placed)

    mine, others = [total, from_ahead, from_back, from_far], []
    sides = (mine, others)
    placed, own_piece = place(((0, 0), (0, 3)), True)
    others += [swap(given) for given in [own_piece] + mine[1:]]
    (placed,) = place(((0, 1), (0, 2), (1, 0), (1, 3)), False, placed)
    which = ((1, 1), (1, 2))
    grad_proj, grad_init, grad_gain, grad_rates = pl.pallas_call(
        functools.partial(last_kernel, which=which),
        out_shape=(out, shape(heads, HS, HS), shape(heads, HS), shape(heads)),
        in_specs=[SM] + [VM] * 8 + [anywhere],
        out_specs=(anywhere, VM, VM, SM),
        scratch_shapes=[pltpu.VMEM((EXTRA, wide), F32), pltpu.SemaphoreType.DMA((3, len(which)))],
        input_output_aliases={9: 0},
        compiler_params=PARAMS,
    )(pos, *mine, *others, placed)
    return (grad_tokens, grad_proj, grad_init, grad_gain, grad_rates, grad_gates)


def solution(mesh):
    in_specs = (
        P("dp", "ctx", None),
        P(None, None, "head"),
        P("head", None, None),
        P("head"),
        P("dp", "head", "ctx"),
        P("head", None),
        P("dp", "ctx", "head"),
    )
    out_specs = (
        P("dp", "ctx", "head"),
        P(None, None, "head"),
        P("head", None, None),
        P("head", None),
        P("head"),
        P("dp", "head", "ctx"),
    )
    return jax.shard_map(body, mesh=mesh, in_specs=in_specs, out_specs=out_specs, check_vma=False)
```

```python
import functools

import jax
import jax.numpy as jnp
from jax import lax
from jax.experimental import pallas as pl
from jax.experimental.pallas import tpu as pltpu
from jax.sharding import PartitionSpec as P

MB = 16
HS = 128
RING = 4
TURNS = (0, 1, 3, 2)
CHUNK = 256
PIECE = 24
STEPS = 4
EXTRA = 2 * RING * PIECE
F32 = jnp.float32
BF = jnp.bfloat16
NN = (((1,), (0,)), ((), ()))
NT = (((1,), (1,)), ((), ()))
TN = (((0,), (0,)), ((), ()))


def dot(a, b, dims, passes):
    ah = a.astype(BF)
    bh = b.astype(BF)
    result = lax.dot_general(ah, bh, dims, preferred_element_type=F32)
    if passes == 3:
        al = (a - ah.astype(F32)).astype(BF)
        bl = (b - bh.astype(F32)).astype(BF)
        result = result + (
            lax.dot_general(ah, bl, dims, preferred_element_type=F32)
            + lax.dot_general(al, bh, dims, preferred_element_type=F32)
        )
    return result


def places(n):
    return (
        lax.broadcasted_iota(jnp.int32, (n, n), 0),
        lax.broadcasted_iota(jnp.int32, (n, n), 1),
    )


def to_col(row):
    i, j = places(row.shape[1])
    return jnp.sum(jnp.where(i == j, row, 0.0), axis=1, keepdims=True)


def to_row(col):
    i, j = places(col.shape[0])
    return jnp.sum(jnp.where(i == j, col, 0.0), axis=0, keepdims=True)


def unit_lower_inverses(lowers):
    n = lowers[0].shape[0]
    i, j = places(n)
    size = 2 * MB
    same = (i // size) == (j // size)
    inverses = [jnp.where(i == j, 1.0, 0.0) - jnp.where(same, low, 0.0) for low in lowers]
    while size < n:
        pair = ((i // (2 * size)) == (j // (2 * size))) & ((i // size) != (j // size))
        corners = [jnp.where(pair, low, 0.0) for low in lowers]
        halves = [dot(inv, corner, NN, 3) for inv, corner in zip(inverses, corners)]
        inverses = [inv - dot(half, inv, NN, 3) for inv, half in zip(inverses, halves)]
        size *= 2
    return inverses


def span(h):
    return slice(h * HS, (h + 1) * HS)


def rates_of(base_ref, gate_ref, h):
    boost = base_ref[h] * gate_ref[0, h : h + 1, :]
    return boost, boost / (1.0 + boost)


def maps_kernel(
    pos_ref, base_ref, tok_ref, wk_ref, wv_ref, gate_ref, init_ref,
    k_ref, v_ref, ninv_ref, gram_ref, inv_ref, bt_ref, d_ref, send_ref, o_ref, half_ref, kacc_ref, vacc_ref,
):
    at = pl.program_id(0)
    steps = pl.num_programs(0)
    tok = tok_ref[0]
    width = tok.shape[1]
    for acc_ref, weight_ref in ((kacc_ref, wk_ref), (vacc_ref, wv_ref)):
        term = jnp.dot(tok, weight_ref[0], preferred_element_type=F32)
        acc_ref[...] = jnp.where(at == 0, term, acc_ref[...] + term)

    @pl.when((at // (steps // 2)) != pos_ref[0])
    def _():
        columns = pl.ds(pl.multiple_of((at % (steps // 2)) * width, width), width)
        half_ref[:, columns] = tok.astype(F32)

    @pl.when(at == steps - 1)
    def _():
        kraw_all = kacc_ref[...].astype(BF).astype(F32)
        v_all = vacc_ref[...].astype(BF).astype(F32)
        n = kraw_all.shape[0]
        i, j = places(n)
        strict = (i // MB) > (j // MB)
        heads = range(init_ref.shape[0])
        kraws = [kraw_all[:, span(h)] for h in heads]
        ninvs = [lax.rsqrt(jnp.sum(kraw * kraw, -1, keepdims=True) + 1e-06) for kraw in kraws]
        ks = [kraw * ninv for kraw, ninv in zip(kraws, ninvs)]
        kts = [k.T for k in ks]
        es = [rates_of(base_ref, gate_ref, h)[1] for h in heads]
        grams = [dot(k, kt, NN, 3) for k, kt in zip(ks, kts)]
        inverses = unit_lower_inverses([jnp.where(strict, gram * e, 0.0) for gram, e in zip(grams, es)])
        a, b = places(HS)
        bts = [dot(kts[h] * es[h], inverses[h], NN, 3) for h in heads]
        decays = [jnp.where(a == b, 1.0, 0.0) - dot(bts[h], ks[h], NN, 3) for h in heads]
        offsets = [dot(bts[h], v_all[:, span(h)], NN, 3) for h in heads]
        firsts = [dot(decays[h], init_ref[h], NN, 3) + offsets[h] for h in heads]
        v_ref[...] = v_all
        for h in heads:
            send_ref[h] = jnp.where(pos_ref[4] == 0, firsts[h], offsets[h])
            d_ref[h] = decays[h]
            o_ref[h] = offsets[h]
            k_ref[:, span(h)] = ks[h]
            ninv_ref[h] = jnp.broadcast_to(ninvs[h], (n, HS))
            gram_ref[h] = grams[h]
            inv_ref[h] = inverses[h]
            bt_ref[h] = bts[h]


def reach_kernel(
    pos_ref, base_ref, tok_ref, wq_ref, gate_ref, k_ref, v_ref, inv_ref,
    q_ref, score_ref, rv_ref, y_ref, qt_ref, zv_ref, tokt_ref,
):
    half = tok_ref.shape[2] // 2
    columns = pl.ds(pl.multiple_of(pos_ref[0] * half, half), half)
    tokt_ref[...] = tok_ref[0, :, columns].astype(F32).T.astype(BF)
    q_all = jnp.dot(tok_ref[0], wq_ref[0], preferred_element_type=F32).astype(BF).astype(F32)
    n = q_all.shape[0]
    i, j = places(n)
    q_ref[...] = q_all
    for h in range(inv_ref.shape[0]):
        q = q_all[:, span(h)]
        k = k_ref[:, span(h)]
        _, e = rates_of(base_ref, gate_ref, h)
        score = dot(q, k, NT, 3)
        mix = jnp.where(i >= j, score * e, 0.0)
        inv = inv_ref[h]
        rv = dot(inv, v_ref[:, span(h)], NN, 3)
        y = dot(inv, k, NN, 3)
        score_ref[h] = score
        rv_ref[:, span(h)] = rv
        y_ref[:, span(h)] = y
        qt_ref[:, span(h)] = q - dot(mix, y, NN, 3)
        zv_ref[:, span(h)] = dot(mix, rv, NN, 3)


def step_kernel(d_ref, w_ref, o_ref, after_ref, out_ref):
    del after_ref
    for h in range(d_ref.shape[0]):
        out_ref[h] = o_ref[h] + dot(d_ref[h], w_ref[h], NN, 3)


def norm_kernel(
    pos_ref, init_ref, near_ref, mid_ref, far_ref, rd_ref, qt_ref, zv_ref, up_ref, gain_ref, after_ref,
    w_ref, h_ref, p_ref, dgain_ref,
):
    del after_ref
    ctx = pos_ref[4]
    heads = range(init_ref.shape[0])
    lasts = [dot(rd_ref[h], far_ref[h], NN, 3) + near_ref[h] for h in heads]
    starts = [
        jnp.where(
            ctx == 0, init_ref[h], jnp.where(ctx == 1, near_ref[h], jnp.where(ctx == 2, mid_ref[h], lasts[h]))
        )
        for h in heads
    ]
    qts = [qt_ref[:, span(h)] for h in heads]
    zs = [dot(qts[h], starts[h], NN, 3) + zv_ref[:, span(h)] for h in heads]
    ups = [up_ref[0, :, span(h)].astype(F32) for h in heads]
    centred = [z - jnp.mean(z, -1, keepdims=True) for z in zs]
    inv_stds = [lax.rsqrt(jnp.mean(c * c, -1, keepdims=True) + 1e-05) for c in centred]
    normed = [c * inv_std for c, inv_std in zip(centred, inv_stds)]
    weighted = [ups[h] * gain_ref[h : h + 1, :] for h in heads]
    backs = [
        inv_stds[h]
        * (
            weighted[h]
            - jnp.mean(weighted[h], -1, keepdims=True)
            - normed[h] * jnp.mean(weighted[h] * normed[h], -1, keepdims=True)
        )
        for h in heads
    ]
    pulled = [dot(qts[h], backs[h], TN, 3) for h in heads]
    for h in heads:
        w_ref[h] = starts[h]
        h_ref[:, span(h)] = backs[h]
        p_ref[h] = pulled[h]
        dgain_ref[h : h + 1, :] = jnp.sum(ups[h] * normed[h], axis=0, keepdims=True)


def query_kernel(
    base_ref, gate_ref, w_ref, h_ref, up_ref, q_ref, score_ref, rv_ref, y_ref, k_ref, inv_ref,
    dq_ref, r_ref, x_ref, dk_ref, de_ref,
):
    n = h_ref.shape[0]
    i, j = places(n)
    for h in range(w_ref.shape[0]):
        w = w_ref[h]
        back = h_ref[:, span(h)]
        k = k_ref[:, span(h)]
        q = q_ref[:, span(h)]
        score = score_ref[h]
        _, e = rates_of(base_ref, gate_ref, h)
        mix = jnp.where(i >= j, score * e, 0.0)
        r = rv_ref[:, span(h)] - dot(y_ref[:, span(h)], w, NN, 3)
        r_ref[:, span(h)] = r
        d_mix = jnp.where(i >= j, dot(back, r, NT, 3), 0.0)
        d_score = d_mix * e
        dq = up_ref[0, :, span(h)].astype(F32) + dot(back, w, NT, 3) + dot(d_score, k, NN, 3)
        dq_ref[:, span(h)] = dq.astype(BF).astype(F32)
        x_ref[:, span(h)] = dot(inv_ref[h], dot(mix, back, TN, 3), TN, 3)
        dk_ref[:, span(h)] = dot(d_score, q, TN, 3)
        de_ref[h : h + 1, :] = jnp.sum(d_mix * score, axis=0, keepdims=True)


def keys_kernel(
    pos_ref, base_ref, gate_ref, one_ref, two_ref, three_ref, rd_ref, rd_one_ref, rd_two_ref, p_ref, d_ref, w_ref, k_ref, ninv_ref,
    gram_ref, bt_ref, r_ref, x_ref, dk_ref, de_ref, dgain_ref, dq_ref,
    all_ref, gates_ref,
):
    ctx = pos_ref[4]
    n = k_ref.shape[0]
    i, j = places(n)
    strict = (i // MB) > (j // MB)
    heads = range(w_ref.shape[0])
    steps = [jnp.where(ctx == 0, rd_ref[h], rd_one_ref[h]) for h in heads]
    inner = [two_ref[h] + dot(rd_two_ref[h], three_ref[h], TN, 3) for h in heads]
    ends = [one_ref[h] + dot(steps[h], inner[h], TN, 3) for h in heads]
    ks = [k_ref[:, span(h)] for h in heads]
    rs = [r_ref[:, span(h)] for h in heads]
    rates = [rates_of(base_ref, gate_ref, h) for h in heads]
    xs = [x_ref[:, span(h)] + dot(bt_ref[h], ends[h], TN, 3) for h in heads]
    d_lows = [jnp.where(strict, -dot(xs[h], rs[h], NT, 3), 0.0) for h in heads]
    begins = [jnp.where(ctx == 0, p_ref[h] + dot(d_ref[h], ends[h], TN, 3), 0.0) for h in heads]
    pulls = [to_row(jnp.sum(rs[h] * dot(ks[h], ends[h], NN, 3), axis=1, keepdims=True)) for h in heads]
    dks = [
        dk_ref[:, span(h)] - dot(xs[h], w_ref[h], NT, 3) + to_col(rates[h][1]) * dot(rs[h], ends[h], NT, 3)
        for h in heads
    ]
    d_grams = [d_lows[h] * rates[h][1] for h in heads]
    dks = [dks[h] + dot(d_grams[h] + d_grams[h].T, ks[h], NN, 3) for h in heads]
    draws = [ninv_ref[h] * (dks[h] - ks[h] * jnp.sum(ks[h] * dks[h], -1, keepdims=True)) for h in heads]
    des = [
        de_ref[h : h + 1, :] + jnp.sum(d_lows[h] * gram_ref[h], axis=0, keepdims=True) + pulls[h] for h in heads
    ]
    all_ref[0:n, :] = dq_ref[...]
    all_ref[3 * n + HS : 3 * n + EXTRA, :] = jnp.zeros((EXTRA - HS, all_ref.shape[1]), F32)
    for h in heads:
        boost = rates[h][0]
        all_ref[n : 2 * n, span(h)] = draws[h].astype(BF).astype(F32)
        all_ref[2 * n : 3 * n, span(h)] = xs[h].astype(BF).astype(F32)
        all_ref[3 * n : 3 * n + HS, span(h)] = begins[h]
        d_boost = des[h] / ((1.0 + boost) * (1.0 + boost))
        gates_ref[0, h : h + 1, :] = d_boost * base_ref[h]
        all_ref[3 * n + HS : 3 * n + HS + 1, span(h)] = dgain_ref[h : h + 1, :]
        all_ref[3 * n + HS + 1 : 3 * n + HS + 2, span(h)] = jnp.broadcast_to(
            jnp.sum(d_boost * gate_ref[0, h : h + 1, :], axis=1, keepdims=True), (1, HS)
        )


def turn_kernel(other_ref, out_ref):
    out_ref[...] = other_ref[...].T.astype(BF)


def product_kernel(pos_ref, tokt_ref, other_tokt_ref, own_ref, other_ref, *refs):
    out_refs = refs[2 : 2 + RING]
    n = tokt_ref.shape[1]
    for turn, out_ref in zip(TURNS, out_refs):
        at = (pos_ref[1] + turn) & (RING - 1)
        rows = pl.ds(pl.multiple_of(at * CHUNK, CHUNK), CHUNK)
        for m in range(3):
            out_ref[m * CHUNK : (m + 1) * CHUNK, :] = jnp.dot(
                tokt_ref[rows, :], own_ref[m * n : (m + 1) * n, :].astype(BF), preferred_element_type=F32
            ) + jnp.dot(
                other_tokt_ref[rows, :], other_ref[m * n : (m + 1) * n, :].astype(BF), preferred_element_type=F32
            )
        extra = pl.ds(pl.multiple_of(3 * n + (pos_ref[0] * RING + at) * PIECE, 8), PIECE)
        out_ref[3 * CHUNK : 3 * CHUNK + PIECE, :] = own_ref[extra, :] + other_ref[extra, :]


def token_kernel(pos_ref, w_ref, all_ref, *out_refs):
    n = out_refs[0].shape[0]
    ds = [all_ref[m * n : (m + 1) * n, :].astype(BF) for m in range(3)]
    quarter = w_ref.shape[1] // RING
    for turn, out_ref in zip(TURNS, out_refs):
        at = (pos_ref[3] + turn) & (RING - 1)
        rows = pl.ds(pl.multiple_of(at * quarter, quarter), quarter)
        total = lax.dot_general(ds[0], w_ref[0, rows, :], NT, preferred_element_type=F32)
        total = total + lax.dot_general(ds[1], w_ref[1, rows, :], NT, preferred_element_type=F32)
        out_ref[...] = total + lax.dot_general(ds[2], w_ref[2, rows, :], NT, preferred_element_type=F32)


def sum_kernel(own_ref, back_ref, ahead_ref, far_ref, *refs):
    refs[-1][...] = (own_ref[...] + far_ref[...]) + (back_ref[...] + ahead_ref[...])


def place_kernel(pos_ref, *refs, which, passed):
    pieces = refs[: len(which)]
    out_ref, sem = refs[-3 if passed else -2], refs[-1]
    copies = []
    for g, ((half, m), piece) in enumerate(zip(which, pieces)):
        core = pos_ref[0] if half == 0 else 1 - pos_ref[0]
        at = core * RING + ((pos_ref[1 + half] + TURNS[m]) & (RING - 1))
        rows = pl.ds(pl.multiple_of(at * CHUNK, CHUNK), CHUNK)
        for s in range(3):
            copies.append(
                pltpu.make_async_copy(piece.at[pl.ds(s * CHUNK, CHUNK), :], out_ref.at[s, rows, :], sem.at[s, g])
            )
    for copy in copies:
        copy.start()
    if passed:
        refs[-2][...] = pieces[0][...]
    for copy in copies:
        copy.wait()


def last_kernel(pos_ref, *refs, which):
    pieces = refs[: 2 * RING]
    out_ref, init_ref, gain_ref, rates_ref, extra_ref, sem = refs[-6:]
    copies = []
    for g, (half, m) in enumerate(which):
        core = pos_ref[0] if half == 0 else 1 - pos_ref[0]
        at = core * RING + ((pos_ref[1 + half] + TURNS[m]) & (RING - 1))
        rows = pl.ds(pl.multiple_of(at * CHUNK, CHUNK), CHUNK)
        for s in range(3):
            copies.append(
                pltpu.make_async_copy(
                    pieces[half * RING + m].at[pl.ds(s * CHUNK, CHUNK), :], out_ref.at[s, rows, :], sem.at[s, g]
                )
            )
    for copy in copies:
        copy.start()
    for p, piece in enumerate(pieces):
        core = pos_ref[0] if p < RING else 1 - pos_ref[0]
        at = core * RING + ((pos_ref[1 + p // RING] + TURNS[p % RING]) & (RING - 1))
        extra_ref[pl.ds(pl.multiple_of(at * PIECE, 8), PIECE), :] = piece[3 * CHUNK : 3 * CHUNK + PIECE, :]
    for h in range(init_ref.shape[0]):
        init_ref[h] = extra_ref[0:HS, span(h)]
        gain_ref[h : h + 1, :] = extra_ref[HS : HS + 1, span(h)]
        rates_ref[h] = extra_ref[HS + 1, h * HS]
    for copy in copies:
        copy.wait()


def moves(first, by):
    pairs = []
    for x in range(RING):
        for core in range(2):
            for y in range(RING):
                along_x = (core == 0) == first
                to_x = (x + by) % RING if along_x else x
                to_y = y if along_x else (y + by) % RING
                pairs.append(((x * 2 + core) * RING + y, (to_x * 2 + core) * RING + to_y))
    return pairs


def round_turn(chunks, first):
    return [
        lax.ppermute(chunk, ("dp", "ctx"), moves(first, turn)) for chunk, turn in zip(chunks, TURNS[1:])
    ]


def swap(value):
    return lax.ppermute(value, "dp", [(i, i ^ 1) for i in range(2 * RING)])


VM = pl.BlockSpec(memory_space=pltpu.VMEM)
SM = pl.BlockSpec(memory_space=pltpu.SMEM)
PARAMS = pltpu.CompilerParams(vmem_limit_bytes=20 * 1024 * 1024)


def shape(*dims, dtype=F32):
    return jax.ShapeDtypeStruct(dims, dtype)


def vmem(*dims, dtype=F32):
    return pltpu.VMEM(dims, dtype)


def hbm(value):
    return pltpu.with_memory_space_constraint(value, pltpu.HBM)


def whole(kernel, outs, specs, aliases=None):
    return pl.pallas_call(
        kernel,
        out_shape=outs,
        in_specs=specs,
        out_specs=tuple(VM for _ in outs) if isinstance(outs, tuple) else VM,
        input_output_aliases=aliases or {},
        compiler_params=PARAMS,
    )


def part(which, dims):
    return pl.BlockSpec((1,) + dims, lambda i: (which, 0, 0))


def full(*dims):
    return pl.BlockSpec(dims, lambda i: (0,) * len(dims))


def body(tokens, proj_weights, init_weight, base_rates, gate_values, out_gain, cotangent):
    n = tokens.shape[1]
    model = tokens.shape[2]
    heads = init_weight.shape[0]
    wide = heads * HS
    ctx = lax.axis_index("ctx")
    dp = lax.axis_index("dp")
    core, x_at = dp % 2, dp // 2
    pos = jnp.stack(
        [core, jnp.where(core == 0, x_at, ctx), jnp.where(core == 0, ctx, x_at), lax.axis_index("head"), ctx]
    ).astype(jnp.int32)
    half = model // 2

    wide_f32 = vmem(n, wide)
    square = vmem(heads, n, n)
    small = vmem(heads, HS, HS)
    wspec = functools.partial(part, dims=(model, wide))
    tokens = hbm(tokens)
    raw_weights = proj_weights
    proj_weights = hbm(proj_weights)
    anywhere = pl.BlockSpec(memory_space=pl.ANY)

    k, v, ninv, gram, inv, bt, decay, send, offset, other_half = pl.pallas_call(
        maps_kernel,
        grid=(STEPS,),
        out_shape=(
            wide_f32, wide_f32, vmem(heads, n, HS), square, square, vmem(heads, HS, n), small, small, small,
            vmem(n, half),
        ),
        in_specs=[
            SM, SM, pl.BlockSpec((1, n, model // STEPS), lambda i: (0, 0, i)),
            pl.BlockSpec((1, model // STEPS, wide), lambda i: (1, i, 0)),
            pl.BlockSpec((1, model // STEPS, wide), lambda i: (2, i, 0)),
            full(1, heads, n), full(heads, HS, HS),
        ],
        out_specs=(VM,) * 10,
        scratch_shapes=[pltpu.VMEM((n, wide), F32)] * 2,
        compiler_params=PARAMS,
    )(pos, hbm(base_rates), tokens, proj_weights, proj_weights, hbm(gate_values), hbm(init_weight))

    near = lax.ppermute(send, "ctx", [(0, 1), (2, 3)])
    moved = lax.ppermute(decay, "ctx", [(2, 3), (1, 0)])
    moved_one = lax.ppermute(decay, "ctx", [(2, 1)])
    moved_two = lax.ppermute(decay, "ctx", [(2, 0)])
    got_half = swap(other_half)

    q, score, rv, y, qt, zv, tokt = pl.pallas_call(
        reach_kernel,
        grid=(1,),
        out_shape=(wide_f32, square, wide_f32, wide_f32, wide_f32, wide_f32, vmem(half, n, dtype=BF)),
        in_specs=[SM, SM, full(1, n, model), wspec(0), full(1, heads, n), VM, VM, VM],
        out_specs=(VM,) * 7,
        compiler_params=PARAMS,
    )(pos, base_rates, tokens, proj_weights, gate_values, k, v, inv)

    second = whole(step_kernel, small, [VM] * 3 + [anywhere])(
        decay, near, offset, qt
    )
    mid = lax.ppermute(second, "ctx", [(1, 2)])
    far = lax.ppermute(second, "ctx", [(1, 3)])
    other_tokt = whole(turn_kernel, vmem(half, n, dtype=BF), [VM])(got_half)

    w, back, pulled, dgain = whole(
        norm_kernel, (small, wide_f32, small, vmem(heads, HS)), [SM] + [VM] * 9 + [anywhere]
    )(pos, init_weight, near, mid, far, moved, qt, zv, cotangent, out_gain, other_tokt)

    back_one = lax.ppermute(pulled, "ctx", [(3, 2), (2, 1), (1, 0)])
    back_two = lax.ppermute(pulled, "ctx", [(3, 1), (2, 0)])
    back_three = lax.ppermute(pulled, "ctx", [(3, 0)])

    dq, r, x, dk, de = whole(
        query_kernel, (wide_f32, wide_f32, wide_f32, wide_f32, vmem(heads, n)), [SM] + [VM] * 10
    )(base_rates, gate_values, w, back, cotangent, q, score, rv, y, k, inv)

    grads, grad_gates = whole(
        keys_kernel, (vmem(3 * n + EXTRA, wide), shape(1, heads, n)), [SM, SM] + [VM] * 20
    )(pos, base_rates, gate_values, back_one, back_two, back_three, moved, moved_one, moved_two, pulled, decay, w, k, ninv, gram, bt, r, x,
      dk, de, dgain, dq)

    chunk = vmem(3 * CHUNK + PIECE, wide)
    quarter = vmem(n, model // RING)
    quarters = whole(token_kernel, (quarter,) * RING, [SM, VM, VM])(pos, raw_weights, grads)

    def along_head(terms, turn):
        return lax.ppermute(terms, "head", [(i, (i + turn) % RING) for i in range(RING)])

    *chunks, near_one, near_two = whole(
        product_kernel, (chunk,) * RING + (quarter,) * 2, [SM] + [VM] * 6, {5: RING, 6: RING + 1}
    )(pos, tokt, other_tokt, grads, swap(grads), *quarters[1:3])
    own, away = chunks[0], round_turn(chunks[1:], True)
    from_back, from_ahead, from_far = along_head(near_one, 1), along_head(near_two, 3), along_head(quarters[3], 2)

    part_sum = whole(sum_kernel, chunk, [VM] * 4 + [anywhere] * 2)(own, *away, from_back, from_ahead)
    grad_tokens = ((quarters[0] + from_far) + (from_back + from_ahead)).astype(BF).reshape(1, n, -1)
    total = whole(sum_kernel, chunk, [VM] * 4 + [anywhere])(
        part_sum, *round_turn([part_sum] * 3, False), grad_tokens
    )
    from_back, from_ahead, from_far = round_turn([total] * 3, True)
    out = shape(3, model, wide)

    def place(which, passed, *placed):
        given = [sides[half][m] for half, m in which]
        return pl.pallas_call(
            functools.partial(place_kernel, which=which, passed=passed),
            out_shape=(out, chunk) if passed else (out,),
            in_specs=[SM] + [VM] * len(given) + [anywhere] * len(placed),
            out_specs=(anywhere, VM) if passed else (anywhere,),
            scratch_shapes=[pltpu.SemaphoreType.DMA((3, len(which)))],
            input_output_aliases={len(given) + 1: 0} if placed else {},
            compiler_params=PARAMS,
        )(pos, *given, *placed)

    mine, others = [total, from_ahead, from_back, from_far], []
    sides = (mine, others)
    placed, own_piece = place(((0, 0), (0, 3)), True)
    others += [swap(given) for given in [own_piece] + mine[1:]]
    (placed,) = place(((0, 1), (0, 2), (1, 0), (1, 3)), False, placed)
    which = ((1, 1), (1, 2))
    grad_proj, grad_init, grad_gain, grad_rates = pl.pallas_call(
        functools.partial(last_kernel, which=which),
        out_shape=(out, shape(heads, HS, HS), shape(heads, HS), shape(heads)),
        in_specs=[SM] + [VM] * 8 + [anywhere],
        out_specs=(anywhere, VM, VM, SM),
        scratch_shapes=[pltpu.VMEM((EXTRA, wide), F32), pltpu.SemaphoreType.DMA((3, len(which)))],
        input_output_aliases={9: 0},
        compiler_params=PARAMS,
    )(pos, *mine, *others, placed)
    return (grad_tokens, grad_proj, grad_init, grad_gain, grad_rates, grad_gates)


def solution(mesh):
    in_specs = (
        P("dp", "ctx", None),
        P(None, None, "head"),
        P("head", None, None),
        P("head"),
        P("dp", "head", "ctx"),
        P("head", None),
        P("dp", "ctx", "head"),
    )
    out_specs = (
        P("dp", "ctx", "head"),
        P(None, None, "head"),
        P("head", None, None),
        P("head", None),
        P("head"),
        P("dp", "head", "ctx"),
    )
    return jax.shard_map(body, mesh=mesh, in_specs=in_specs, out_specs=out_specs, check_vma=False)
```

```python
import functools

import jax
import jax.numpy as jnp
from jax import lax
from jax.experimental import pallas as pl
from jax.experimental.pallas import tpu as pltpu
from jax.sharding import PartitionSpec as P

MB = 16
HS = 128
RING = 4
TURNS = (0, 1, 3, 2)
CHUNK = 256
PIECE = 24
EXTRA = 2 * RING * PIECE
F32 = jnp.float32
BF = jnp.bfloat16
NN = (((1,), (0,)), ((), ()))
NT = (((1,), (1,)), ((), ()))
TN = (((0,), (0,)), ((), ()))


def dot(a, b, dims, passes):
    ah = a.astype(BF)
    bh = b.astype(BF)
    result = lax.dot_general(ah, bh, dims, preferred_element_type=F32)
    if passes == 3:
        al = (a - ah.astype(F32)).astype(BF)
        bl = (b - bh.astype(F32)).astype(BF)
        result = result + (
            lax.dot_general(ah, bl, dims, preferred_element_type=F32)
            + lax.dot_general(al, bh, dims, preferred_element_type=F32)
        )
    return result


def places(n):
    return (
        lax.broadcasted_iota(jnp.int32, (n, n), 0),
        lax.broadcasted_iota(jnp.int32, (n, n), 1),
    )


def to_col(row):
    i, j = places(row.shape[1])
    return jnp.sum(jnp.where(i == j, row, 0.0), axis=1, keepdims=True)


def to_row(col):
    i, j = places(col.shape[0])
    return jnp.sum(jnp.where(i == j, col, 0.0), axis=0, keepdims=True)


def unit_lower_inverses(lowers):
    n = lowers[0].shape[0]
    i, j = places(n)
    size = 2 * MB
    same = (i // size) == (j // size)
    inverses = [jnp.where(i == j, 1.0, 0.0) - jnp.where(same, low, 0.0) for low in lowers]
    while size < n:
        pair = ((i // (2 * size)) == (j // (2 * size))) & ((i // size) != (j // size))
        corners = [jnp.where(pair, low, 0.0) for low in lowers]
        halves = [dot(inv, corner, NN, 3) for inv, corner in zip(inverses, corners)]
        inverses = [inv - dot(half, inv, NN, 3) for inv, half in zip(inverses, halves)]
        size *= 2
    return inverses


def span(h):
    return slice(h * HS, (h + 1) * HS)


def rates_of(base_ref, gate_ref, h):
    boost = base_ref[h] * gate_ref[0, h : h + 1, :]
    return boost, boost / (1.0 + boost)


def maps_kernel(
    pos_ref, base_ref, tok_ref, wk_ref, wv_ref, gate_ref, init_ref,
    k_ref, v_ref, ninv_ref, gram_ref, inv_ref, bt_ref, d_ref, send_ref, o_ref, half_ref,
):
    half = tok_ref.shape[2] // 2
    columns = pl.ds(pl.multiple_of((1 - pos_ref[0]) * half, half), half)
    half_ref[...] = tok_ref[0, :, columns].astype(F32)
    tok = tok_ref[0]
    kraw_all = jnp.dot(tok, wk_ref[0], preferred_element_type=F32).astype(BF).astype(F32)
    v_all = jnp.dot(tok, wv_ref[0], preferred_element_type=F32).astype(BF).astype(F32)
    n = kraw_all.shape[0]
    i, j = places(n)
    strict = (i // MB) > (j // MB)
    heads = range(init_ref.shape[0])
    kraws = [kraw_all[:, span(h)] for h in heads]
    ninvs = [lax.rsqrt(jnp.sum(kraw * kraw, -1, keepdims=True) + 1e-06) for kraw in kraws]
    ks = [kraw * ninv for kraw, ninv in zip(kraws, ninvs)]
    kts = [k.T for k in ks]
    es = [rates_of(base_ref, gate_ref, h)[1] for h in heads]
    grams = [dot(k, kt, NN, 3) for k, kt in zip(ks, kts)]
    inverses = unit_lower_inverses([jnp.where(strict, gram * e, 0.0) for gram, e in zip(grams, es)])
    a, b = places(HS)
    bts = [dot(kts[h] * es[h], inverses[h], NN, 3) for h in heads]
    decays = [jnp.where(a == b, 1.0, 0.0) - dot(bts[h], ks[h], NN, 3) for h in heads]
    offsets = [dot(bts[h], v_all[:, span(h)], NN, 3) for h in heads]
    firsts = [dot(decays[h], init_ref[h], NN, 3) + offsets[h] for h in heads]
    v_ref[...] = v_all
    for h in heads:
        send_ref[h] = jnp.where(pos_ref[4] == 0, firsts[h], decays[h])
        d_ref[h] = decays[h]
        o_ref[h] = offsets[h]
        k_ref[:, span(h)] = ks[h]
        ninv_ref[h] = jnp.broadcast_to(ninvs[h], (n, HS))
        gram_ref[h] = grams[h]
        inv_ref[h] = inverses[h]
        bt_ref[h] = bts[h]


def reach_kernel(
    pos_ref, base_ref, tok_ref, wq_ref, gate_ref, k_ref, v_ref, inv_ref,
    q_ref, score_ref, rv_ref, y_ref, qt_ref, zv_ref, tokt_ref,
):
    half = tok_ref.shape[2] // 2
    columns = pl.ds(pl.multiple_of(pos_ref[0] * half, half), half)
    tokt_ref[...] = tok_ref[0, :, columns].astype(F32).T.astype(BF)
    q_all = jnp.dot(tok_ref[0], wq_ref[0], preferred_element_type=F32).astype(BF).astype(F32)
    n = q_all.shape[0]
    i, j = places(n)
    q_ref[...] = q_all
    for h in range(inv_ref.shape[0]):
        q = q_all[:, span(h)]
        k = k_ref[:, span(h)]
        _, e = rates_of(base_ref, gate_ref, h)
        score = dot(q, k, NT, 3)
        mix = jnp.where(i >= j, score * e, 0.0)
        inv = inv_ref[h]
        rv = dot(inv, v_ref[:, span(h)], NN, 3)
        y = dot(inv, k, NN, 3)
        score_ref[h] = score
        rv_ref[:, span(h)] = rv
        y_ref[:, span(h)] = y
        qt_ref[:, span(h)] = q - dot(mix, y, NN, 3)
        zv_ref[:, span(h)] = dot(mix, rv, NN, 3)


def norm_kernel(
    pos_ref, init_ref, map_one_ref, add_one_ref, map_two_ref, add_two_ref, map_three_ref, qt_ref, zv_ref, up_ref,
    gain_ref, after_ref,
    w_ref, h_ref, p_ref, dgain_ref,
):
    del after_ref
    ctx = pos_ref[4]
    heads = range(init_ref.shape[0])
    seconds = [dot(map_two_ref[h], map_three_ref[h], NN, 3) + add_two_ref[h] for h in heads]
    seconds = [jnp.where(ctx == 3, seconds[h], map_two_ref[h]) for h in heads]
    lasts = [dot(map_one_ref[h], seconds[h], NN, 3) + add_one_ref[h] for h in heads]
    starts = [
        jnp.where(ctx == 0, init_ref[h], jnp.where(ctx == 1, map_one_ref[h], lasts[h])) for h in heads
    ]
    qts = [qt_ref[:, span(h)] for h in heads]
    zs = [dot(qts[h], starts[h], NN, 3) + zv_ref[:, span(h)] for h in heads]
    ups = [up_ref[0, :, span(h)].astype(F32) for h in heads]
    centred = [z - jnp.mean(z, -1, keepdims=True) for z in zs]
    inv_stds = [lax.rsqrt(jnp.mean(c * c, -1, keepdims=True) + 1e-05) for c in centred]
    normed = [c * inv_std for c, inv_std in zip(centred, inv_stds)]
    weighted = [ups[h] * gain_ref[h : h + 1, :] for h in heads]
    backs = [
        inv_stds[h]
        * (
            weighted[h]
            - jnp.mean(weighted[h], -1, keepdims=True)
            - normed[h] * jnp.mean(weighted[h] * normed[h], -1, keepdims=True)
        )
        for h in heads
    ]
    pulled = [dot(qts[h], backs[h], TN, 3) for h in heads]
    for h in heads:
        w_ref[h] = starts[h]
        h_ref[:, span(h)] = backs[h]
        p_ref[h] = pulled[h]
        dgain_ref[h : h + 1, :] = jnp.sum(ups[h] * normed[h], axis=0, keepdims=True)


def query_kernel(
    base_ref, gate_ref, w_ref, h_ref, up_ref, q_ref, score_ref, rv_ref, y_ref, k_ref, inv_ref,
    dq_ref, r_ref, x_ref, dk_ref, de_ref,
):
    n = h_ref.shape[0]
    i, j = places(n)
    for h in range(w_ref.shape[0]):
        w = w_ref[h]
        back = h_ref[:, span(h)]
        k = k_ref[:, span(h)]
        q = q_ref[:, span(h)]
        score = score_ref[h]
        _, e = rates_of(base_ref, gate_ref, h)
        mix = jnp.where(i >= j, score * e, 0.0)
        r = rv_ref[:, span(h)] - dot(y_ref[:, span(h)], w, NN, 3)
        r_ref[:, span(h)] = r
        d_mix = jnp.where(i >= j, dot(back, r, NT, 3), 0.0)
        d_score = d_mix * e
        dq = up_ref[0, :, span(h)].astype(F32) + dot(back, w, NT, 3) + dot(d_score, k, NN, 3)
        dq_ref[:, span(h)] = dq.astype(BF).astype(F32)
        x_ref[:, span(h)] = dot(inv_ref[h], dot(mix, back, TN, 3), TN, 3)
        dk_ref[:, span(h)] = dot(d_score, q, TN, 3)
        de_ref[h : h + 1, :] = jnp.sum(d_mix * score, axis=0, keepdims=True)


def keys_kernel(
    pos_ref, base_ref, gate_ref, one_ref, two_ref, three_ref, rd_ref, rd_two_ref, p_ref, d_ref, w_ref, k_ref, ninv_ref,
    gram_ref, bt_ref, r_ref, x_ref, dk_ref, de_ref, dgain_ref, dq_ref,
    all_ref, gates_ref,
):
    ctx = pos_ref[4]
    n = k_ref.shape[0]
    i, j = places(n)
    strict = (i // MB) > (j // MB)
    heads = range(w_ref.shape[0])
    inner = [two_ref[h] + dot(rd_two_ref[h], three_ref[h], TN, 3) for h in heads]
    ends = [one_ref[h] + dot(rd_ref[h], inner[h], TN, 3) for h in heads]
    ks = [k_ref[:, span(h)] for h in heads]
    rs = [r_ref[:, span(h)] for h in heads]
    rates = [rates_of(base_ref, gate_ref, h) for h in heads]
    xs = [x_ref[:, span(h)] + dot(bt_ref[h], ends[h], TN, 3) for h in heads]
    d_lows = [jnp.where(strict, -dot(xs[h], rs[h], NT, 3), 0.0) for h in heads]
    begins = [jnp.where(ctx == 0, p_ref[h] + dot(d_ref[h], ends[h], TN, 3), 0.0) for h in heads]
    pulls = [to_row(jnp.sum(rs[h] * dot(ks[h], ends[h], NN, 3), axis=1, keepdims=True)) for h in heads]
    dks = [
        dk_ref[:, span(h)] - dot(xs[h], w_ref[h], NT, 3) + to_col(rates[h][1]) * dot(rs[h], ends[h], NT, 3)
        for h in heads
    ]
    d_grams = [d_lows[h] * rates[h][1] for h in heads]
    dks = [dks[h] + dot(d_grams[h] + d_grams[h].T, ks[h], NN, 3) for h in heads]
    draws = [ninv_ref[h] * (dks[h] - ks[h] * jnp.sum(ks[h] * dks[h], -1, keepdims=True)) for h in heads]
    des = [
        de_ref[h : h + 1, :] + jnp.sum(d_lows[h] * gram_ref[h], axis=0, keepdims=True) + pulls[h] for h in heads
    ]
    all_ref[0:n, :] = dq_ref[...]
    all_ref[3 * n + HS : 3 * n + EXTRA, :] = jnp.zeros((EXTRA - HS, all_ref.shape[1]), F32)
    for h in heads:
        boost = rates[h][0]
        all_ref[n : 2 * n, span(h)] = draws[h].astype(BF).astype(F32)
        all_ref[2 * n : 3 * n, span(h)] = xs[h].astype(BF).astype(F32)
        all_ref[3 * n : 3 * n + HS, span(h)] = begins[h]
        d_boost = des[h] / ((1.0 + boost) * (1.0 + boost))
        gates_ref[0, h : h + 1, :] = d_boost * base_ref[h]
        all_ref[3 * n + HS : 3 * n + HS + 1, span(h)] = dgain_ref[h : h + 1, :]
        all_ref[3 * n + HS + 1 : 3 * n + HS + 2, span(h)] = jnp.broadcast_to(
            jnp.sum(d_boost * gate_ref[0, h : h + 1, :], axis=1, keepdims=True), (1, HS)
        )


def turn_kernel(other_ref, out_ref):
    out_ref[...] = other_ref[...].T.astype(BF)


def product_kernel(pos_ref, tokt_ref, other_tokt_ref, own_ref, other_ref, *refs):
    out_refs = refs[2 : 2 + RING]
    n = tokt_ref.shape[1]
    for turn, out_ref in zip(TURNS, out_refs):
        at = (pos_ref[1] + turn) & (RING - 1)
        rows = pl.ds(pl.multiple_of(at * CHUNK, CHUNK), CHUNK)
        for m in range(3):
            out_ref[m * CHUNK : (m + 1) * CHUNK, :] = jnp.dot(
                tokt_ref[rows, :], own_ref[m * n : (m + 1) * n, :].astype(BF), preferred_element_type=F32
            ) + jnp.dot(
                other_tokt_ref[rows, :], other_ref[m * n : (m + 1) * n, :].astype(BF), preferred_element_type=F32
            )
        extra = pl.ds(pl.multiple_of(3 * n + (pos_ref[0] * RING + at) * PIECE, 8), PIECE)
        out_ref[3 * CHUNK : 3 * CHUNK + PIECE, :] = own_ref[extra, :] + other_ref[extra, :]


def token_kernel(pos_ref, w_ref, all_ref, *out_refs):
    n = out_refs[0].shape[0]
    ds = [all_ref[m * n : (m + 1) * n, :].astype(BF) for m in range(3)]
    quarter = w_ref.shape[1] // RING
    for turn, out_ref in zip(TURNS, out_refs):
        at = (pos_ref[3] + turn) & (RING - 1)
        rows = pl.ds(pl.multiple_of(at * quarter, quarter), quarter)
        total = lax.dot_general(ds[0], w_ref[0, rows, :], NT, preferred_element_type=F32)
        total = total + lax.dot_general(ds[1], w_ref[1, rows, :], NT, preferred_element_type=F32)
        out_ref[...] = total + lax.dot_general(ds[2], w_ref[2, rows, :], NT, preferred_element_type=F32)


def sum_kernel(own_ref, back_ref, ahead_ref, far_ref, *refs):
    refs[-1][...] = (own_ref[...] + far_ref[...]) + (back_ref[...] + ahead_ref[...])


def place_kernel(pos_ref, *refs, which, passed):
    pieces = refs[: len(which)]
    out_ref, sem = refs[-3 if passed else -2], refs[-1]
    copies = []
    for g, ((half, m), piece) in enumerate(zip(which, pieces)):
        core = pos_ref[0] if half == 0 else 1 - pos_ref[0]
        at = core * RING + ((pos_ref[1 + half] + TURNS[m]) & (RING - 1))
        rows = pl.ds(pl.multiple_of(at * CHUNK, CHUNK), CHUNK)
        for s in range(3):
            copies.append(
                pltpu.make_async_copy(piece.at[pl.ds(s * CHUNK, CHUNK), :], out_ref.at[s, rows, :], sem.at[s, g])
            )
    for copy in copies:
        copy.start()
    if passed:
        refs[-2][...] = pieces[0][...]
    for copy in copies:
        copy.wait()


def last_kernel(pos_ref, *refs, which):
    pieces = refs[: 2 * RING]
    out_ref, init_ref, gain_ref, rates_ref, extra_ref, sem = refs[-6:]
    copies = []
    for g, (half, m) in enumerate(which):
        core = pos_ref[0] if half == 0 else 1 - pos_ref[0]
        at = core * RING + ((pos_ref[1 + half] + TURNS[m]) & (RING - 1))
        rows = pl.ds(pl.multiple_of(at * CHUNK, CHUNK), CHUNK)
        for s in range(3):
            copies.append(
                pltpu.make_async_copy(
                    pieces[half * RING + m].at[pl.ds(s * CHUNK, CHUNK), :], out_ref.at[s, rows, :], sem.at[s, g]
                )
            )
    for copy in copies:
        copy.start()
    for p, piece in enumerate(pieces):
        core = pos_ref[0] if p < RING else 1 - pos_ref[0]
        at = core * RING + ((pos_ref[1 + p // RING] + TURNS[p % RING]) & (RING - 1))
        extra_ref[pl.ds(pl.multiple_of(at * PIECE, 8), PIECE), :] = piece[3 * CHUNK : 3 * CHUNK + PIECE, :]
    for h in range(init_ref.shape[0]):
        init_ref[h] = extra_ref[0:HS, span(h)]
        gain_ref[h : h + 1, :] = extra_ref[HS : HS + 1, span(h)]
        rates_ref[h] = extra_ref[HS + 1, h * HS]
    for copy in copies:
        copy.wait()


def moves(first, by):
    pairs = []
    for x in range(RING):
        for core in range(2):
            for y in range(RING):
                along_x = (core == 0) == first
                to_x = (x + by) % RING if along_x else x
                to_y = y if along_x else (y + by) % RING
                pairs.append(((x * 2 + core) * RING + y, (to_x * 2 + core) * RING + to_y))
    return pairs


def round_turn(chunks, first):
    return [
        lax.ppermute(chunk, ("dp", "ctx"), moves(first, turn)) for chunk, turn in zip(chunks, TURNS[1:])
    ]


def swap(value):
    return lax.ppermute(value, "dp", [(i, i ^ 1) for i in range(2 * RING)])


VM = pl.BlockSpec(memory_space=pltpu.VMEM)
SM = pl.BlockSpec(memory_space=pltpu.SMEM)
PARAMS = pltpu.CompilerParams(vmem_limit_bytes=20 * 1024 * 1024)


def shape(*dims, dtype=F32):
    return jax.ShapeDtypeStruct(dims, dtype)


def vmem(*dims, dtype=F32):
    return pltpu.VMEM(dims, dtype)


def hbm(value):
    return pltpu.with_memory_space_constraint(value, pltpu.HBM)


def whole(kernel, outs, specs, aliases=None):
    return pl.pallas_call(
        kernel,
        out_shape=outs,
        in_specs=specs,
        out_specs=tuple(VM for _ in outs) if isinstance(outs, tuple) else VM,
        input_output_aliases=aliases or {},
        compiler_params=PARAMS,
    )


def part(which, dims):
    return pl.BlockSpec((1,) + dims, lambda i: (which, 0, 0))


def full(*dims):
    return pl.BlockSpec(dims, lambda i: (0,) * len(dims))


def body(tokens, proj_weights, init_weight, base_rates, gate_values, out_gain, cotangent):
    n = tokens.shape[1]
    model = tokens.shape[2]
    heads = init_weight.shape[0]
    wide = heads * HS
    ctx = lax.axis_index("ctx")
    dp = lax.axis_index("dp")
    core, x_at = dp % 2, dp // 2
    pos = jnp.stack(
        [core, jnp.where(core == 0, x_at, ctx), jnp.where(core == 0, ctx, x_at), lax.axis_index("head"), ctx]
    ).astype(jnp.int32)
    half = model // 2

    wide_f32 = vmem(n, wide)
    square = vmem(heads, n, n)
    small = vmem(heads, HS, HS)
    wspec = functools.partial(part, dims=(model, wide))
    tokens = hbm(tokens)
    raw_weights = proj_weights
    proj_weights = hbm(proj_weights)
    anywhere = pl.BlockSpec(memory_space=pl.ANY)

    k, v, ninv, gram, inv, bt, decay, send, offset, other_half = pl.pallas_call(
        maps_kernel,
        grid=(1,),
        out_shape=(
            wide_f32, wide_f32, vmem(heads, n, HS), square, square, vmem(heads, HS, n), small, small, small,
            vmem(n, half),
        ),
        in_specs=[SM, SM, full(1, n, model), wspec(1), wspec(2), full(1, heads, n), full(heads, HS, HS)],
        out_specs=(VM,) * 10,
        compiler_params=PARAMS,
    )(pos, hbm(base_rates), tokens, proj_weights, proj_weights, hbm(gate_values), hbm(init_weight))

    map_one = lax.ppermute(send, "ctx", [(0, 1), (1, 2), (2, 3)])
    add_one = lax.ppermute(offset, "ctx", [(1, 2), (2, 3)])
    map_two = lax.ppermute(send, "ctx", [(0, 2), (1, 3)])
    add_two = lax.ppermute(offset, "ctx", [(1, 3)])
    map_three = lax.ppermute(send, "ctx", [(0, 3)])
    moved = lax.ppermute(decay, "ctx", [(1, 0), (2, 1)])
    moved_two = lax.ppermute(decay, "ctx", [(2, 0)])
    got_half = swap(other_half)

    q, score, rv, y, qt, zv, tokt = pl.pallas_call(
        reach_kernel,
        grid=(1,),
        out_shape=(wide_f32, square, wide_f32, wide_f32, wide_f32, wide_f32, vmem(half, n, dtype=BF)),
        in_specs=[SM, SM, full(1, n, model), wspec(0), full(1, heads, n), VM, VM, VM],
        out_specs=(VM,) * 7,
        compiler_params=PARAMS,
    )(pos, base_rates, tokens, proj_weights, gate_values, k, v, inv)

    other_tokt = whole(turn_kernel, vmem(half, n, dtype=BF), [VM])(got_half)

    w, back, pulled, dgain = whole(
        norm_kernel, (small, wide_f32, small, vmem(heads, HS)), [SM] + [VM] * 10 + [anywhere]
    )(pos, init_weight, map_one, add_one, map_two, add_two, map_three, qt, zv, cotangent, out_gain, other_tokt)

    back_one = lax.ppermute(pulled, "ctx", [(3, 2), (2, 1), (1, 0)])
    back_two = lax.ppermute(pulled, "ctx", [(3, 1), (2, 0)])
    back_three = lax.ppermute(pulled, "ctx", [(3, 0)])

    dq, r, x, dk, de = whole(
        query_kernel, (wide_f32, wide_f32, wide_f32, wide_f32, vmem(heads, n)), [SM] + [VM] * 10
    )(base_rates, gate_values, w, back, cotangent, q, score, rv, y, k, inv)

    grads, grad_gates = whole(
        keys_kernel, (vmem(3 * n + EXTRA, wide), shape(1, heads, n)), [SM, SM] + [VM] * 19
    )(pos, base_rates, gate_values, back_one, back_two, back_three, moved, moved_two, pulled, decay, w, k, ninv, gram, bt, r, x,
      dk, de, dgain, dq)

    chunk = vmem(3 * CHUNK + PIECE, wide)
    quarter = vmem(n, model // RING)
    quarters = whole(token_kernel, (quarter,) * RING, [SM, VM, VM])(pos, raw_weights, grads)

    def along_head(terms, turn):
        return lax.ppermute(terms, "head", [(i, (i + turn) % RING) for i in range(RING)])

    *chunks, near_one, near_two = whole(
        product_kernel, (chunk,) * RING + (quarter,) * 2, [SM] + [VM] * 6, {5: RING, 6: RING + 1}
    )(pos, tokt, other_tokt, grads, swap(grads), *quarters[1:3])
    own, away = chunks[0], round_turn(chunks[1:], True)
    from_back, from_ahead, from_far = along_head(near_one, 1), along_head(near_two, 3), along_head(quarters[3], 2)

    part_sum = whole(sum_kernel, chunk, [VM] * 4 + [anywhere] * 2)(own, *away, from_back, from_ahead)
    grad_tokens = ((quarters[0] + from_far) + (from_back + from_ahead)).astype(BF).reshape(1, n, -1)
    total = whole(sum_kernel, chunk, [VM] * 4 + [anywhere])(
        part_sum, *round_turn([part_sum] * 3, False), grad_tokens
    )
    from_back, from_ahead, from_far = round_turn([total] * 3, True)
    out = shape(3, model, wide)

    def place(which, passed, *placed):
        given = [sides[half][m] for half, m in which]
        return pl.pallas_call(
            functools.partial(place_kernel, which=which, passed=passed),
            out_shape=(out, chunk) if passed else (out,),
            in_specs=[SM] + [VM] * len(given) + [anywhere] * len(placed),
            out_specs=(anywhere, VM) if passed else (anywhere,),
            scratch_shapes=[pltpu.SemaphoreType.DMA((3, len(which)))],
            input_output_aliases={len(given) + 1: 0} if placed else {},
            compiler_params=PARAMS,
        )(pos, *given, *placed)

    mine, others = [total, from_ahead, from_back, from_far], []
    sides = (mine, others)
    placed, own_piece = place(((0, 0), (0, 3)), True)
    others += [swap(given) for given in [own_piece] + mine[1:]]
    (placed,) = place(((0, 1), (0, 2), (1, 0), (1, 3)), False, placed)
    which = ((1, 1), (1, 2))
    grad_proj, grad_init, grad_gain, grad_rates = pl.pallas_call(
        functools.partial(last_kernel, which=which),
        out_shape=(out, shape(heads, HS, HS), shape(heads, HS), shape(heads)),
        in_specs=[SM] + [VM] * 8 + [anywhere],
        out_specs=(anywhere, VM, VM, SM),
        scratch_shapes=[pltpu.VMEM((EXTRA, wide), F32), pltpu.SemaphoreType.DMA((3, len(which)))],
        input_output_aliases={9: 0},
        compiler_params=PARAMS,
    )(pos, *mine, *others, placed)
    return (grad_tokens, grad_proj, grad_init, grad_gain, grad_rates, grad_gates)


def solution(mesh):
    in_specs = (
        P("dp", "ctx", None),
        P(None, None, "head"),
        P("head", None, None),
        P("head"),
        P("dp", "head", "ctx"),
        P("head", None),
        P("dp", "ctx", "head"),
    )
    out_specs = (
        P("dp", "ctx", "head"),
        P(None, None, "head"),
        P("head", None, None),
        P("head", None),
        P("head"),
        P("dp", "head", "ctx"),
    )
    return jax.shard_map(body, mesh=mesh, in_specs=in_specs, out_specs=out_specs, check_vma=False)
```

```python
import functools

import jax
import jax.numpy as jnp
from jax import lax
from jax.experimental import pallas as pl
from jax.experimental.pallas import tpu as pltpu
from jax.sharding import PartitionSpec as P

MB = 16
HS = 128
RING = 4
TURNS = (0, 1, 3, 2)
CHUNK = 256
PIECE = 24
EXTRA = 2 * RING * PIECE
F32 = jnp.float32
BF = jnp.bfloat16
NN = (((1,), (0,)), ((), ()))
NT = (((1,), (1,)), ((), ()))
TN = (((0,), (0,)), ((), ()))


def dot(a, b, dims, passes):
    ah = a.astype(BF)
    bh = b.astype(BF)
    result = lax.dot_general(ah, bh, dims, preferred_element_type=F32)
    if passes == 3:
        al = (a - ah.astype(F32)).astype(BF)
        bl = (b - bh.astype(F32)).astype(BF)
        result = result + (
            lax.dot_general(ah, bl, dims, preferred_element_type=F32)
            + lax.dot_general(al, bh, dims, preferred_element_type=F32)
        )
    return result


def places(n):
    return (
        lax.broadcasted_iota(jnp.int32, (n, n), 0),
        lax.broadcasted_iota(jnp.int32, (n, n), 1),
    )


def to_col(row):
    i, j = places(row.shape[1])
    return jnp.sum(jnp.where(i == j, row, 0.0), axis=1, keepdims=True)


def to_row(col):
    i, j = places(col.shape[0])
    return jnp.sum(jnp.where(i == j, col, 0.0), axis=0, keepdims=True)


def unit_lower_inverses(lowers):
    n = lowers[0].shape[0]
    i, j = places(n)
    size = 2 * MB
    same = (i // size) == (j // size)
    inverses = [jnp.where(i == j, 1.0, 0.0) - jnp.where(same, low, 0.0) for low in lowers]
    while size < n:
        pair = ((i // (2 * size)) == (j // (2 * size))) & ((i // size) != (j // size))
        corners = [jnp.where(pair, low, 0.0) for low in lowers]
        halves = [dot(inv, corner, NN, 3) for inv, corner in zip(inverses, corners)]
        inverses = [inv - dot(half, inv, NN, 3) for inv, half in zip(inverses, halves)]
        size *= 2
    return inverses


def span(h):
    return slice(h * HS, (h + 1) * HS)


def rates_of(base_ref, gate_ref, h):
    boost = base_ref[h] * gate_ref[0, h : h + 1, :]
    return boost, boost / (1.0 + boost)


def maps_kernel(
    pos_ref, base_ref, tok_ref, wk_ref, wv_ref, gate_ref, init_ref,
    k_ref, v_ref, ninv_ref, gram_ref, inv_ref, bt_ref, d_ref, send_ref, o_ref, half_ref,
):
    half = tok_ref.shape[2] // 2
    columns = pl.ds(pl.multiple_of((1 - pos_ref[0]) * half, half), half)
    half_ref[...] = tok_ref[0, :, columns].astype(F32)
    tok = tok_ref[0]
    kraw_all = jnp.dot(tok, wk_ref[0], preferred_element_type=F32).astype(BF).astype(F32)
    v_all = jnp.dot(tok, wv_ref[0], preferred_element_type=F32).astype(BF).astype(F32)
    n = kraw_all.shape[0]
    i, j = places(n)
    strict = (i // MB) > (j // MB)
    heads = range(init_ref.shape[0])
    kraws = [kraw_all[:, span(h)] for h in heads]
    ninvs = [lax.rsqrt(jnp.sum(kraw * kraw, -1, keepdims=True) + 1e-06) for kraw in kraws]
    ks = [kraw * ninv for kraw, ninv in zip(kraws, ninvs)]
    kts = [k.T for k in ks]
    es = [rates_of(base_ref, gate_ref, h)[1] for h in heads]
    grams = [dot(k, kt, NN, 3) for k, kt in zip(ks, kts)]
    inverses = unit_lower_inverses([jnp.where(strict, gram * e, 0.0) for gram, e in zip(grams, es)])
    a, b = places(HS)
    bts = [dot(kts[h] * es[h], inverses[h], NN, 3) for h in heads]
    decays = [jnp.where(a == b, 1.0, 0.0) - dot(bts[h], ks[h], NN, 3) for h in heads]
    offsets = [dot(bts[h], v_all[:, span(h)], NN, 3) for h in heads]
    firsts = [dot(decays[h], init_ref[h], NN, 3) + offsets[h] for h in heads]
    v_ref[...] = v_all
    for h in heads:
        send_ref[h] = jnp.where(pos_ref[4] == 0, firsts[h], offsets[h])
        d_ref[h] = decays[h]
        o_ref[h] = offsets[h]
        k_ref[:, span(h)] = ks[h]
        ninv_ref[h] = jnp.broadcast_to(ninvs[h], (n, HS))
        gram_ref[h] = grams[h]
        inv_ref[h] = inverses[h]
        bt_ref[h] = bts[h]


def reach_kernel(
    pos_ref, base_ref, tok_ref, wq_ref, gate_ref, k_ref, v_ref, inv_ref,
    q_ref, score_ref, rv_ref, y_ref, qt_ref, zv_ref, tokt_ref,
):
    half = tok_ref.shape[2] // 2
    columns = pl.ds(pl.multiple_of(pos_ref[0] * half, half), half)
    tokt_ref[...] = tok_ref[0, :, columns].astype(F32).T.astype(BF)
    q_all = jnp.dot(tok_ref[0], wq_ref[0], preferred_element_type=F32).astype(BF).astype(F32)
    n = q_all.shape[0]
    i, j = places(n)
    q_ref[...] = q_all
    for h in range(inv_ref.shape[0]):
        q = q_all[:, span(h)]
        k = k_ref[:, span(h)]
        _, e = rates_of(base_ref, gate_ref, h)
        score = dot(q, k, NT, 3)
        mix = jnp.where(i >= j, score * e, 0.0)
        inv = inv_ref[h]
        rv = dot(inv, v_ref[:, span(h)], NN, 3)
        y = dot(inv, k, NN, 3)
        score_ref[h] = score
        rv_ref[:, span(h)] = rv
        y_ref[:, span(h)] = y
        qt_ref[:, span(h)] = q - dot(mix, y, NN, 3)
        zv_ref[:, span(h)] = dot(mix, rv, NN, 3)


def step_kernel(d_ref, w_ref, o_ref, after_ref, out_ref):
    del after_ref
    for h in range(d_ref.shape[0]):
        out_ref[h] = o_ref[h] + dot(d_ref[h], w_ref[h], NN, 3)


def norm_kernel(
    pos_ref, init_ref, near_ref, mid_ref, far_ref, rd_ref, qt_ref, zv_ref, up_ref, gain_ref, after_ref,
    w_ref, h_ref, p_ref, dgain_ref,
):
    del after_ref
    ctx = pos_ref[4]
    heads = range(init_ref.shape[0])
    lasts = [dot(rd_ref[h], far_ref[h], NN, 3) + near_ref[h] for h in heads]
    starts = [
        jnp.where(
            ctx == 0, init_ref[h], jnp.where(ctx == 1, near_ref[h], jnp.where(ctx == 2, mid_ref[h], lasts[h]))
        )
        for h in heads
    ]
    qts = [qt_ref[:, span(h)] for h in heads]
    zs = [dot(qts[h], starts[h], NN, 3) + zv_ref[:, span(h)] for h in heads]
    ups = [up_ref[0, :, span(h)].astype(F32) for h in heads]
    centred = [z - jnp.mean(z, -1, keepdims=True) for z in zs]
    inv_stds = [lax.rsqrt(jnp.mean(c * c, -1, keepdims=True) + 1e-05) for c in centred]
    normed = [c * inv_std for c, inv_std in zip(centred, inv_stds)]
    weighted = [ups[h] * gain_ref[h : h + 1, :] for h in heads]
    backs = [
        inv_stds[h]
        * (
            weighted[h]
            - jnp.mean(weighted[h], -1, keepdims=True)
            - normed[h] * jnp.mean(weighted[h] * normed[h], -1, keepdims=True)
        )
        for h in heads
    ]
    pulled = [dot(qts[h], backs[h], TN, 3) for h in heads]
    for h in heads:
        w_ref[h] = starts[h]
        h_ref[:, span(h)] = backs[h]
        p_ref[h] = pulled[h]
        dgain_ref[h : h + 1, :] = jnp.sum(ups[h] * normed[h], axis=0, keepdims=True)


def query_kernel(
    base_ref, gate_ref, w_ref, h_ref, up_ref, q_ref, score_ref, rv_ref, y_ref, k_ref, inv_ref,
    dq_ref, r_ref, x_ref, dk_ref, de_ref,
):
    n = h_ref.shape[0]
    i, j = places(n)
    for h in range(w_ref.shape[0]):
        w = w_ref[h]
        back = h_ref[:, span(h)]
        k = k_ref[:, span(h)]
        q = q_ref[:, span(h)]
        score = score_ref[h]
        _, e = rates_of(base_ref, gate_ref, h)
        mix = jnp.where(i >= j, score * e, 0.0)
        r = rv_ref[:, span(h)] - dot(y_ref[:, span(h)], w, NN, 3)
        r_ref[:, span(h)] = r
        d_mix = jnp.where(i >= j, dot(back, r, NT, 3), 0.0)
        d_score = d_mix * e
        dq = up_ref[0, :, span(h)].astype(F32) + dot(back, w, NT, 3) + dot(d_score, k, NN, 3)
        dq_ref[:, span(h)] = dq.astype(BF).astype(F32)
        x_ref[:, span(h)] = dot(inv_ref[h], dot(mix, back, TN, 3), TN, 3)
        dk_ref[:, span(h)] = dot(d_score, q, TN, 3)
        de_ref[h : h + 1, :] = jnp.sum(d_mix * score, axis=0, keepdims=True)


def keys_kernel(
    pos_ref, base_ref, gate_ref, one_ref, two_ref, three_ref, rd_ref, rd_one_ref, rd_two_ref, p_ref, d_ref, w_ref, k_ref, ninv_ref,
    gram_ref, bt_ref, r_ref, x_ref, dk_ref, de_ref, dgain_ref, dq_ref,
    all_ref, gates_ref,
):
    ctx = pos_ref[4]
    n = k_ref.shape[0]
    i, j = places(n)
    strict = (i // MB) > (j // MB)
    heads = range(w_ref.shape[0])
    steps = [jnp.where(ctx == 0, rd_ref[h], rd_one_ref[h]) for h in heads]
    inner = [two_ref[h] + dot(rd_two_ref[h], three_ref[h], TN, 3) for h in heads]
    ends = [one_ref[h] + dot(steps[h], inner[h], TN, 3) for h in heads]
    ks = [k_ref[:, span(h)] for h in heads]
    rs = [r_ref[:, span(h)] for h in heads]
    rates = [rates_of(base_ref, gate_ref, h) for h in heads]
    xs = [x_ref[:, span(h)] + dot(bt_ref[h], ends[h], TN, 3) for h in heads]
    d_lows = [jnp.where(strict, -dot(xs[h], rs[h], NT, 3), 0.0) for h in heads]
    begins = [jnp.where(ctx == 0, p_ref[h] + dot(d_ref[h], ends[h], TN, 3), 0.0) for h in heads]
    pulls = [to_row(jnp.sum(rs[h] * dot(ks[h], ends[h], NN, 3), axis=1, keepdims=True)) for h in heads]
    dks = [
        dk_ref[:, span(h)] - dot(xs[h], w_ref[h], NT, 3) + to_col(rates[h][1]) * dot(rs[h], ends[h], NT, 3)
        for h in heads
    ]
    d_grams = [d_lows[h] * rates[h][1] for h in heads]
    dks = [dks[h] + dot(d_grams[h] + d_grams[h].T, ks[h], NN, 3) for h in heads]
    draws = [ninv_ref[h] * (dks[h] - ks[h] * jnp.sum(ks[h] * dks[h], -1, keepdims=True)) for h in heads]
    des = [
        de_ref[h : h + 1, :] + jnp.sum(d_lows[h] * gram_ref[h], axis=0, keepdims=True) + pulls[h] for h in heads
    ]
    all_ref[0:n, :] = dq_ref[...]
    all_ref[3 * n + HS : 3 * n + EXTRA, :] = jnp.zeros((EXTRA - HS, all_ref.shape[1]), F32)
    for h in heads:
        boost = rates[h][0]
        all_ref[n : 2 * n, span(h)] = draws[h].astype(BF).astype(F32)
        all_ref[2 * n : 3 * n, span(h)] = xs[h].astype(BF).astype(F32)
        all_ref[3 * n : 3 * n + HS, span(h)] = begins[h]
        d_boost = des[h] / ((1.0 + boost) * (1.0 + boost))
        gates_ref[0, h : h + 1, :] = d_boost * base_ref[h]
        all_ref[3 * n + HS : 3 * n + HS + 1, span(h)] = dgain_ref[h : h + 1, :]
        all_ref[3 * n + HS + 1 : 3 * n + HS + 2, span(h)] = jnp.broadcast_to(
            jnp.sum(d_boost * gate_ref[0, h : h + 1, :], axis=1, keepdims=True), (1, HS)
        )


def turn_kernel(other_ref, out_ref):
    out_ref[...] = other_ref[...].T.astype(BF)


def product_kernel(pos_ref, tokt_ref, other_tokt_ref, own_ref, other_ref, *refs, turns, passed):
    skipped = passed + 1 if passed else 0
    out_refs = refs[skipped : skipped + len(turns)]
    n = tokt_ref.shape[1]
    for turn, out_ref in zip(turns, out_refs):
        at = (pos_ref[1] + turn) & (RING - 1)
        rows = pl.ds(pl.multiple_of(at * CHUNK, CHUNK), CHUNK)
        for m in range(3):
            out_ref[m * CHUNK : (m + 1) * CHUNK, :] = jnp.dot(
                tokt_ref[rows, :], own_ref[m * n : (m + 1) * n, :].astype(BF), preferred_element_type=F32
            ) + jnp.dot(
                other_tokt_ref[rows, :], other_ref[m * n : (m + 1) * n, :].astype(BF), preferred_element_type=F32
            )
        extra = pl.ds(pl.multiple_of(3 * n + (pos_ref[0] * RING + at) * PIECE, 8), PIECE)
        out_ref[3 * CHUNK : 3 * CHUNK + PIECE, :] = own_ref[extra, :] + other_ref[extra, :]


def token_kernel(pos_ref, w_ref, all_ref, *out_refs):
    n = out_refs[0].shape[0]
    ds = [all_ref[m * n : (m + 1) * n, :].astype(BF) for m in range(3)]
    quarter = w_ref.shape[1] // RING
    for turn, out_ref in zip(TURNS, out_refs):
        at = (pos_ref[3] + turn) & (RING - 1)
        rows = pl.ds(pl.multiple_of(at * quarter, quarter), quarter)
        total = lax.dot_general(ds[0], w_ref[0, rows, :], NT, preferred_element_type=F32)
        total = total + lax.dot_general(ds[1], w_ref[1, rows, :], NT, preferred_element_type=F32)
        out_ref[...] = total + lax.dot_general(ds[2], w_ref[2, rows, :], NT, preferred_element_type=F32)


def sum_kernel(own_ref, back_ref, ahead_ref, far_ref, *refs):
    refs[-1][...] = (own_ref[...] + far_ref[...]) + (back_ref[...] + ahead_ref[...])


def place_kernel(pos_ref, *refs, which, passed):
    pieces = refs[: len(which)]
    out_ref, sem = refs[-3 if passed else -2], refs[-1]
    copies = []
    for g, ((half, m), piece) in enumerate(zip(which, pieces)):
        core = pos_ref[0] if half == 0 else 1 - pos_ref[0]
        at = core * RING + ((pos_ref[1 + half] + TURNS[m]) & (RING - 1))
        rows = pl.ds(pl.multiple_of(at * CHUNK, CHUNK), CHUNK)
        for s in range(3):
            copies.append(
                pltpu.make_async_copy(piece.at[pl.ds(s * CHUNK, CHUNK), :], out_ref.at[s, rows, :], sem.at[s, g])
            )
    for copy in copies:
        copy.start()
    if passed:
        refs[-2][...] = pieces[0][...]
    for copy in copies:
        copy.wait()


def last_kernel(pos_ref, *refs, which):
    pieces = refs[: 2 * RING]
    out_ref, init_ref, gain_ref, rates_ref, extra_ref, sem = refs[-6:]
    copies = []
    for g, (half, m) in enumerate(which):
        core = pos_ref[0] if half == 0 else 1 - pos_ref[0]
        at = core * RING + ((pos_ref[1 + half] + TURNS[m]) & (RING - 1))
        rows = pl.ds(pl.multiple_of(at * CHUNK, CHUNK), CHUNK)
        for s in range(3):
            copies.append(
                pltpu.make_async_copy(
                    pieces[half * RING + m].at[pl.ds(s * CHUNK, CHUNK), :], out_ref.at[s, rows, :], sem.at[s, g]
                )
            )
    for copy in copies:
        copy.start()
    for p, piece in enumerate(pieces):
        core = pos_ref[0] if p < RING else 1 - pos_ref[0]
        at = core * RING + ((pos_ref[1 + p // RING] + TURNS[p % RING]) & (RING - 1))
        extra_ref[pl.ds(pl.multiple_of(at * PIECE, 8), PIECE), :] = piece[3 * CHUNK : 3 * CHUNK + PIECE, :]
    for h in range(init_ref.shape[0]):
        init_ref[h] = extra_ref[0:HS, span(h)]
        gain_ref[h : h + 1, :] = extra_ref[HS : HS + 1, span(h)]
        rates_ref[h] = extra_ref[HS + 1, h * HS]
    for copy in copies:
        copy.wait()


def moves(first, by):
    pairs = []
    for x in range(RING):
        for core in range(2):
            for y in range(RING):
                along_x = (core == 0) == first
                to_x = (x + by) % RING if along_x else x
                to_y = y if along_x else (y + by) % RING
                pairs.append(((x * 2 + core) * RING + y, (to_x * 2 + core) * RING + to_y))
    return pairs


def round_turn(chunks, first):
    return [
        lax.ppermute(chunk, ("dp", "ctx"), moves(first, turn)) for chunk, turn in zip(chunks, TURNS[1:])
    ]


def swap(value):
    return lax.ppermute(value, "dp", [(i, i ^ 1) for i in range(2 * RING)])


VM = pl.BlockSpec(memory_space=pltpu.VMEM)
SM = pl.BlockSpec(memory_space=pltpu.SMEM)
PARAMS = pltpu.CompilerParams(vmem_limit_bytes=20 * 1024 * 1024)


def shape(*dims, dtype=F32):
    return jax.ShapeDtypeStruct(dims, dtype)


def vmem(*dims, dtype=F32):
    return pltpu.VMEM(dims, dtype)


def hbm(value):
    return pltpu.with_memory_space_constraint(value, pltpu.HBM)


def whole(kernel, outs, specs, aliases=None):
    return pl.pallas_call(
        kernel,
        out_shape=outs,
        in_specs=specs,
        out_specs=tuple(VM for _ in outs) if isinstance(outs, tuple) else VM,
        input_output_aliases=aliases or {},
        compiler_params=PARAMS,
    )


def part(which, dims):
    return pl.BlockSpec((1,) + dims, lambda i: (which, 0, 0))


def full(*dims):
    return pl.BlockSpec(dims, lambda i: (0,) * len(dims))


def body(tokens, proj_weights, init_weight, base_rates, gate_values, out_gain, cotangent):
    n = tokens.shape[1]
    model = tokens.shape[2]
    heads = init_weight.shape[0]
    wide = heads * HS
    ctx = lax.axis_index("ctx")
    dp = lax.axis_index("dp")
    core, x_at = dp % 2, dp // 2
    pos = jnp.stack(
        [core, jnp.where(core == 0, x_at, ctx), jnp.where(core == 0, ctx, x_at), lax.axis_index("head"), ctx]
    ).astype(jnp.int32)
    half = model // 2

    wide_f32 = vmem(n, wide)
    square = vmem(heads, n, n)
    small = vmem(heads, HS, HS)
    wspec = functools.partial(part, dims=(model, wide))
    tokens = hbm(tokens)
    raw_weights = proj_weights
    proj_weights = hbm(proj_weights)
    anywhere = pl.BlockSpec(memory_space=pl.ANY)

    k, v, ninv, gram, inv, bt, decay, send, offset, other_half = pl.pallas_call(
        maps_kernel,
        grid=(1,),
        out_shape=(
            wide_f32, wide_f32, vmem(heads, n, HS), square, square, vmem(heads, HS, n), small, small, small,
            vmem(n, half),
        ),
        in_specs=[SM, SM, full(1, n, model), wspec(1), wspec(2), full(1, heads, n), full(heads, HS, HS)],
        out_specs=(VM,) * 10,
        compiler_params=PARAMS,
    )(pos, hbm(base_rates), tokens, proj_weights, proj_weights, hbm(gate_values), hbm(init_weight))

    near = lax.ppermute(send, "ctx", [(0, 1), (2, 3)])
    moved = lax.ppermute(decay, "ctx", [(2, 3), (1, 0)])
    moved_one = lax.ppermute(decay, "ctx", [(2, 1)])
    moved_two = lax.ppermute(decay, "ctx", [(2, 0)])
    got_half = swap(other_half)

    q, score, rv, y, qt, zv, tokt = pl.pallas_call(
        reach_kernel,
        grid=(1,),
        out_shape=(wide_f32, square, wide_f32, wide_f32, wide_f32, wide_f32, vmem(half, n, dtype=BF)),
        in_specs=[SM, SM, full(1, n, model), wspec(0), full(1, heads, n), VM, VM, VM],
        out_specs=(VM,) * 7,
        compiler_params=PARAMS,
    )(pos, base_rates, tokens, proj_weights, gate_values, k, v, inv)

    second = whole(step_kernel, small, [VM] * 3 + [anywhere])(
        decay, near, offset, qt
    )
    mid = lax.ppermute(second, "ctx", [(1, 2)])
    far = lax.ppermute(second, "ctx", [(1, 3)])
    other_tokt = whole(turn_kernel, vmem(half, n, dtype=BF), [VM])(got_half)

    w, back, pulled, dgain = whole(
        norm_kernel, (small, wide_f32, small, vmem(heads, HS)), [SM] + [VM] * 9 + [anywhere]
    )(pos, init_weight, near, mid, far, moved, qt, zv, cotangent, out_gain, other_tokt)

    back_one = lax.ppermute(pulled, "ctx", [(3, 2), (2, 1), (1, 0)])
    back_two = lax.ppermute(pulled, "ctx", [(3, 1), (2, 0)])
    back_three = lax.ppermute(pulled, "ctx", [(3, 0)])

    dq, r, x, dk, de = whole(
        query_kernel, (wide_f32, wide_f32, wide_f32, wide_f32, vmem(heads, n)), [SM] + [VM] * 10
    )(base_rates, gate_values, w, back, cotangent, q, score, rv, y, k, inv)

    grads, grad_gates = whole(
        keys_kernel, (vmem(3 * n + EXTRA, wide), shape(1, heads, n)), [SM, SM] + [VM] * 20
    )(pos, base_rates, gate_values, back_one, back_two, back_three, moved, moved_one, moved_two, pulled, decay, w, k, ninv, gram, bt, r, x,
      dk, de, dgain, dq)

    chunk = vmem(3 * CHUNK + PIECE, wide)
    quarter = vmem(n, model // RING)
    quarters = whole(token_kernel, (quarter,) * RING, [SM, VM, VM])(pos, raw_weights, grads)

    def along_head(terms, turn):
        return lax.ppermute(terms, "head", [(i, (i + turn) % RING) for i in range(RING)])

    given = (pos, tokt, other_tokt, grads, swap(grads))
    far_chunk = whole(
        functools.partial(product_kernel, turns=(2,), passed=0), chunk, [SM] + [VM] * 4
    )(*given)
    own, one_chunk, three_chunk, near_one, near_two = whole(
        functools.partial(product_kernel, turns=(0, 1, 3), passed=2),
        (chunk,) * 3 + (quarter,) * 2, [SM] + [VM] * 6 + [anywhere], {5: 3, 6: 4},
    )(*given, *quarters[1:3], far_chunk)
    away = round_turn([one_chunk, three_chunk, far_chunk], True)
    from_back, from_ahead, from_far = along_head(near_one, 1), along_head(near_two, 3), along_head(quarters[3], 2)

    part_sum = whole(sum_kernel, chunk, [VM] * 4 + [anywhere] * 2)(own, *away, from_back, from_ahead)
    grad_tokens = ((quarters[0] + from_far) + (from_back + from_ahead)).astype(BF).reshape(1, n, -1)
    total = whole(sum_kernel, chunk, [VM] * 4 + [anywhere])(
        part_sum, *round_turn([part_sum] * 3, False), grad_tokens
    )
    from_back, from_ahead, from_far = round_turn([total] * 3, True)
    out = shape(3, model, wide)

    def place(which, passed, *placed):
        given = [sides[half][m] for half, m in which]
        return pl.pallas_call(
            functools.partial(place_kernel, which=which, passed=passed),
            out_shape=(out, chunk) if passed else (out,),
            in_specs=[SM] + [VM] * len(given) + [anywhere] * len(placed),
            out_specs=(anywhere, VM) if passed else (anywhere,),
            scratch_shapes=[pltpu.SemaphoreType.DMA((3, len(which)))],
            input_output_aliases={len(given) + 1: 0} if placed else {},
            compiler_params=PARAMS,
        )(pos, *given, *placed)

    mine, others = [total, from_ahead, from_back, from_far], []
    sides = (mine, others)
    placed, own_piece = place(((0, 0), (0, 3)), True)
    others += [swap(given) for given in [own_piece] + mine[1:]]
    (placed,) = place(((0, 1), (0, 2), (1, 0), (1, 3)), False, placed)
    which = ((1, 1), (1, 2))
    grad_proj, grad_init, grad_gain, grad_rates = pl.pallas_call(
        functools.partial(last_kernel, which=which),
        out_shape=(out, shape(heads, HS, HS), shape(heads, HS), shape(heads)),
        in_specs=[SM] + [VM] * 8 + [anywhere],
        out_specs=(anywhere, VM, VM, SM),
        scratch_shapes=[pltpu.VMEM((EXTRA, wide), F32), pltpu.SemaphoreType.DMA((3, len(which)))],
        input_output_aliases={9: 0},
        compiler_params=PARAMS,
    )(pos, *mine, *others, placed)
    return (grad_tokens, grad_proj, grad_init, grad_gain, grad_rates, grad_gates)


def solution(mesh):
    in_specs = (
        P("dp", "ctx", None),
        P(None, None, "head"),
        P("head", None, None),
        P("head"),
        P("dp", "head", "ctx"),
        P("head", None),
        P("dp", "ctx", "head"),
    )
    out_specs = (
        P("dp", "ctx", "head"),
        P(None, None, "head"),
        P("head", None, None),
        P("head", None),
        P("head"),
        P("dp", "head", "ctx"),
    )
    return jax.shard_map(body, mesh=mesh, in_specs=in_specs, out_specs=out_specs, check_vma=False)
```

```python
import functools

import jax
import jax.numpy as jnp
from jax import lax
from jax.experimental import pallas as pl
from jax.experimental.pallas import tpu as pltpu
from jax.sharding import PartitionSpec as P

MB = 16
HS = 128
RING = 4
TURNS = (0, 1, 3, 2)
CHUNK = 256
PIECE = 24
EXTRA = 2 * RING * PIECE
F32 = jnp.float32
BF = jnp.bfloat16
NN = (((1,), (0,)), ((), ()))
NT = (((1,), (1,)), ((), ()))
TN = (((0,), (0,)), ((), ()))


def dot(a, b, dims, passes):
    ah = a.astype(BF)
    bh = b.astype(BF)
    result = lax.dot_general(ah, bh, dims, preferred_element_type=F32)
    if passes == 3:
        al = (a - ah.astype(F32)).astype(BF)
        bl = (b - bh.astype(F32)).astype(BF)
        result = result + (
            lax.dot_general(ah, bl, dims, preferred_element_type=F32)
            + lax.dot_general(al, bh, dims, preferred_element_type=F32)
        )
    return result


def places(n):
    return (
        lax.broadcasted_iota(jnp.int32, (n, n), 0),
        lax.broadcasted_iota(jnp.int32, (n, n), 1),
    )


def to_col(row):
    i, j = places(row.shape[1])
    return jnp.sum(jnp.where(i == j, row, 0.0), axis=1, keepdims=True)


def to_row(col):
    i, j = places(col.shape[0])
    return jnp.sum(jnp.where(i == j, col, 0.0), axis=0, keepdims=True)


def unit_lower_inverses(lowers):
    n = lowers[0].shape[0]
    i, j = places(n)
    size = 2 * MB
    same = (i // size) == (j // size)
    inverses = [jnp.where(i == j, 1.0, 0.0) - jnp.where(same, low, 0.0) for low in lowers]
    while size < n:
        pair = ((i // (2 * size)) == (j // (2 * size))) & ((i // size) != (j // size))
        corners = [jnp.where(pair, low, 0.0) for low in lowers]
        halves = [dot(inv, corner, NN, 3) for inv, corner in zip(inverses, corners)]
        inverses = [inv - dot(half, inv, NN, 3) for inv, half in zip(inverses, halves)]
        size *= 2
    return inverses


def span(h):
    return slice(h * HS, (h + 1) * HS)


def rates_of(base_ref, gate_ref, h):
    boost = base_ref[h] * gate_ref[0, h : h + 1, :]
    return boost, boost / (1.0 + boost)


def maps_kernel(
    pos_ref, base_ref, tok_ref, wk_ref, wv_ref, gate_ref, init_ref,
    k_ref, v_ref, ninv_ref, gram_ref, inv_ref, bt_ref, d_ref, send_ref, o_ref,
):
    tok = tok_ref[0]
    kraw_all = jnp.dot(tok, wk_ref[0], preferred_element_type=F32).astype(BF).astype(F32)
    v_all = jnp.dot(tok, wv_ref[0], preferred_element_type=F32).astype(BF).astype(F32)
    n = kraw_all.shape[0]
    i, j = places(n)
    strict = (i // MB) > (j // MB)
    heads = range(init_ref.shape[0])
    kraws = [kraw_all[:, span(h)] for h in heads]
    ninvs = [lax.rsqrt(jnp.sum(kraw * kraw, -1, keepdims=True) + 1e-06) for kraw in kraws]
    ks = [kraw * ninv for kraw, ninv in zip(kraws, ninvs)]
    kts = [k.T for k in ks]
    es = [rates_of(base_ref, gate_ref, h)[1] for h in heads]
    grams = [dot(k, kt, NN, 3) for k, kt in zip(ks, kts)]
    inverses = unit_lower_inverses([jnp.where(strict, gram * e, 0.0) for gram, e in zip(grams, es)])
    a, b = places(HS)
    bts = [dot(kts[h] * es[h], inverses[h], NN, 3) for h in heads]
    decays = [jnp.where(a == b, 1.0, 0.0) - dot(bts[h], ks[h], NN, 3) for h in heads]
    offsets = [dot(bts[h], v_all[:, span(h)], NN, 3) for h in heads]
    firsts = [dot(decays[h], init_ref[h], NN, 3) + offsets[h] for h in heads]
    v_ref[...] = v_all
    for h in heads:
        send_ref[h] = jnp.where(pos_ref[4] == 0, firsts[h], offsets[h])
        d_ref[h] = decays[h]
        o_ref[h] = offsets[h]
        k_ref[:, span(h)] = ks[h]
        ninv_ref[h] = jnp.broadcast_to(ninvs[h], (n, HS))
        gram_ref[h] = grams[h]
        inv_ref[h] = inverses[h]
        bt_ref[h] = bts[h]


def reach_kernel(
    pos_ref, base_ref, tok_ref, wq_ref, gate_ref, k_ref, v_ref, inv_ref,
    q_ref, score_ref, rv_ref, y_ref, qt_ref, zv_ref, tokt_ref, half_ref,
):
    half = tok_ref.shape[2] // 2
    columns = pl.ds(pl.multiple_of(pos_ref[0] * half, half), half)
    tokt_ref[...] = tok_ref[0, :, columns].astype(F32).T.astype(BF)
    columns = pl.ds(pl.multiple_of((1 - pos_ref[0]) * half, half), half)
    half_ref[...] = tok_ref[0, :, columns].astype(F32)
    q_all = jnp.dot(tok_ref[0], wq_ref[0], preferred_element_type=F32).astype(BF).astype(F32)
    n = q_all.shape[0]
    i, j = places(n)
    q_ref[...] = q_all
    for h in range(inv_ref.shape[0]):
        q = q_all[:, span(h)]
        k = k_ref[:, span(h)]
        _, e = rates_of(base_ref, gate_ref, h)
        score = dot(q, k, NT, 3)
        mix = jnp.where(i >= j, score * e, 0.0)
        inv = inv_ref[h]
        rv = dot(inv, v_ref[:, span(h)], NN, 3)
        y = dot(inv, k, NN, 3)
        score_ref[h] = score
        rv_ref[:, span(h)] = rv
        y_ref[:, span(h)] = y
        qt_ref[:, span(h)] = q - dot(mix, y, NN, 3)
        zv_ref[:, span(h)] = dot(mix, rv, NN, 3)


def step_kernel(d_ref, w_ref, o_ref, after_ref, out_ref):
    del after_ref
    for h in range(d_ref.shape[0]):
        out_ref[h] = o_ref[h] + dot(d_ref[h], w_ref[h], NN, 3)


def norm_kernel(
    pos_ref, init_ref, near_ref, mid_ref, far_ref, rd_ref, qt_ref, zv_ref, up_ref, gain_ref, after_ref,
    w_ref, h_ref, p_ref, dgain_ref,
):
    del after_ref
    ctx = pos_ref[4]
    heads = range(init_ref.shape[0])
    lasts = [dot(rd_ref[h], far_ref[h], NN, 3) + near_ref[h] for h in heads]
    starts = [
        jnp.where(
            ctx == 0, init_ref[h], jnp.where(ctx == 1, near_ref[h], jnp.where(ctx == 2, mid_ref[h], lasts[h]))
        )
        for h in heads
    ]
    qts = [qt_ref[:, span(h)] for h in heads]
    zs = [dot(qts[h], starts[h], NN, 3) + zv_ref[:, span(h)] for h in heads]
    ups = [up_ref[0, :, span(h)].astype(F32) for h in heads]
    centred = [z - jnp.mean(z, -1, keepdims=True) for z in zs]
    inv_stds = [lax.rsqrt(jnp.mean(c * c, -1, keepdims=True) + 1e-05) for c in centred]
    normed = [c * inv_std for c, inv_std in zip(centred, inv_stds)]
    weighted = [ups[h] * gain_ref[h : h + 1, :] for h in heads]
    backs = [
        inv_stds[h]
        * (
            weighted[h]
            - jnp.mean(weighted[h], -1, keepdims=True)
            - normed[h] * jnp.mean(weighted[h] * normed[h], -1, keepdims=True)
        )
        for h in heads
    ]
    pulled = [dot(qts[h], backs[h], TN, 3) for h in heads]
    for h in heads:
        w_ref[h] = starts[h]
        h_ref[:, span(h)] = backs[h]
        p_ref[h] = pulled[h]
        dgain_ref[h : h + 1, :] = jnp.sum(ups[h] * normed[h], axis=0, keepdims=True)


def query_kernel(
    base_ref, gate_ref, w_ref, h_ref, up_ref, q_ref, score_ref, rv_ref, y_ref, k_ref, inv_ref,
    dq_ref, r_ref, x_ref, dk_ref, de_ref,
):
    n = h_ref.shape[0]
    i, j = places(n)
    for h in range(w_ref.shape[0]):
        w = w_ref[h]
        back = h_ref[:, span(h)]
        k = k_ref[:, span(h)]
        q = q_ref[:, span(h)]
        score = score_ref[h]
        _, e = rates_of(base_ref, gate_ref, h)
        mix = jnp.where(i >= j, score * e, 0.0)
        r = rv_ref[:, span(h)] - dot(y_ref[:, span(h)], w, NN, 3)
        r_ref[:, span(h)] = r
        d_mix = jnp.where(i >= j, dot(back, r, NT, 3), 0.0)
        d_score = d_mix * e
        dq = up_ref[0, :, span(h)].astype(F32) + dot(back, w, NT, 3) + dot(d_score, k, NN, 3)
        dq_ref[:, span(h)] = dq.astype(BF).astype(F32)
        x_ref[:, span(h)] = dot(inv_ref[h], dot(mix, back, TN, 3), TN, 3)
        dk_ref[:, span(h)] = dot(d_score, q, TN, 3)
        de_ref[h : h + 1, :] = jnp.sum(d_mix * score, axis=0, keepdims=True)


def keys_kernel(
    pos_ref, base_ref, gate_ref, one_ref, two_ref, three_ref, rd_ref, rd_one_ref, rd_two_ref, p_ref, d_ref, w_ref, k_ref, ninv_ref,
    gram_ref, bt_ref, r_ref, x_ref, dk_ref, de_ref, dgain_ref, dq_ref,
    all_ref, gates_ref,
):
    ctx = pos_ref[4]
    n = k_ref.shape[0]
    i, j = places(n)
    strict = (i // MB) > (j // MB)
    heads = range(w_ref.shape[0])
    steps = [jnp.where(ctx == 0, rd_ref[h], rd_one_ref[h]) for h in heads]
    inner = [two_ref[h] + dot(rd_two_ref[h], three_ref[h], TN, 3) for h in heads]
    ends = [one_ref[h] + dot(steps[h], inner[h], TN, 3) for h in heads]
    ks = [k_ref[:, span(h)] for h in heads]
    rs = [r_ref[:, span(h)] for h in heads]
    rates = [rates_of(base_ref, gate_ref, h) for h in heads]
    xs = [x_ref[:, span(h)] + dot(bt_ref[h], ends[h], TN, 3) for h in heads]
    d_lows = [jnp.where(strict, -dot(xs[h], rs[h], NT, 3), 0.0) for h in heads]
    begins = [jnp.where(ctx == 0, p_ref[h] + dot(d_ref[h], ends[h], TN, 3), 0.0) for h in heads]
    pulls = [to_row(jnp.sum(rs[h] * dot(ks[h], ends[h], NN, 3), axis=1, keepdims=True)) for h in heads]
    dks = [
        dk_ref[:, span(h)] - dot(xs[h], w_ref[h], NT, 3) + to_col(rates[h][1]) * dot(rs[h], ends[h], NT, 3)
        for h in heads
    ]
    d_grams = [d_lows[h] * rates[h][1] for h in heads]
    dks = [dks[h] + dot(d_grams[h] + d_grams[h].T, ks[h], NN, 3) for h in heads]
    draws = [ninv_ref[h] * (dks[h] - ks[h] * jnp.sum(ks[h] * dks[h], -1, keepdims=True)) for h in heads]
    des = [
        de_ref[h : h + 1, :] + jnp.sum(d_lows[h] * gram_ref[h], axis=0, keepdims=True) + pulls[h] for h in heads
    ]
    all_ref[0:n, :] = dq_ref[...]
    all_ref[3 * n + HS : 3 * n + EXTRA, :] = jnp.zeros((EXTRA - HS, all_ref.shape[1]), F32)
    for h in heads:
        boost = rates[h][0]
        all_ref[n : 2 * n, span(h)] = draws[h].astype(BF).astype(F32)
        all_ref[2 * n : 3 * n, span(h)] = xs[h].astype(BF).astype(F32)
        all_ref[3 * n : 3 * n + HS, span(h)] = begins[h]
        d_boost = des[h] / ((1.0 + boost) * (1.0 + boost))
        gates_ref[0, h : h + 1, :] = d_boost * base_ref[h]
        all_ref[3 * n + HS : 3 * n + HS + 1, span(h)] = dgain_ref[h : h + 1, :]
        all_ref[3 * n + HS + 1 : 3 * n + HS + 2, span(h)] = jnp.broadcast_to(
            jnp.sum(d_boost * gate_ref[0, h : h + 1, :], axis=1, keepdims=True), (1, HS)
        )


def turn_kernel(other_ref, out_ref):
    out_ref[...] = other_ref[...].T.astype(BF)


def product_kernel(pos_ref, tokt_ref, other_tokt_ref, own_ref, other_ref, *refs, turns, passed):
    skipped = passed + 1 if passed else 0
    out_refs = refs[skipped : skipped + len(turns)]
    n = tokt_ref.shape[1]
    for turn, out_ref in zip(turns, out_refs):
        at = (pos_ref[1] + turn) & (RING - 1)
        rows = pl.ds(pl.multiple_of(at * CHUNK, CHUNK), CHUNK)
        for m in range(3):
            out_ref[m * CHUNK : (m + 1) * CHUNK, :] = jnp.dot(
                tokt_ref[rows, :], own_ref[m * n : (m + 1) * n, :].astype(BF), preferred_element_type=F32
            ) + jnp.dot(
                other_tokt_ref[rows, :], other_ref[m * n : (m + 1) * n, :].astype(BF), preferred_element_type=F32
            )
        extra = pl.ds(pl.multiple_of(3 * n + (pos_ref[0] * RING + at) * PIECE, 8), PIECE)
        out_ref[3 * CHUNK : 3 * CHUNK + PIECE, :] = own_ref[extra, :] + other_ref[extra, :]


def token_kernel(pos_ref, w_ref, all_ref, *out_refs):
    n = out_refs[0].shape[0]
    ds = [all_ref[m * n : (m + 1) * n, :].astype(BF) for m in range(3)]
    quarter = w_ref.shape[1] // RING
    for turn, out_ref in zip(TURNS, out_refs):
        at = (pos_ref[3] + turn) & (RING - 1)
        rows = pl.ds(pl.multiple_of(at * quarter, quarter), quarter)
        total = lax.dot_general(ds[0], w_ref[0, rows, :], NT, preferred_element_type=F32)
        total = total + lax.dot_general(ds[1], w_ref[1, rows, :], NT, preferred_element_type=F32)
        out_ref[...] = total + lax.dot_general(ds[2], w_ref[2, rows, :], NT, preferred_element_type=F32)


def sum_kernel(own_ref, back_ref, ahead_ref, far_ref, *refs):
    refs[-1][...] = (own_ref[...] + far_ref[...]) + (back_ref[...] + ahead_ref[...])


def place_kernel(pos_ref, *refs, which, passed):
    pieces = refs[: len(which)]
    out_ref, sem = refs[-3 if passed else -2], refs[-1]
    copies = []
    for g, ((half, m), piece) in enumerate(zip(which, pieces)):
        core = pos_ref[0] if half == 0 else 1 - pos_ref[0]
        at = core * RING + ((pos_ref[1 + half] + TURNS[m]) & (RING - 1))
        rows = pl.ds(pl.multiple_of(at * CHUNK, CHUNK), CHUNK)
        for s in range(3):
            copies.append(
                pltpu.make_async_copy(piece.at[pl.ds(s * CHUNK, CHUNK), :], out_ref.at[s, rows, :], sem.at[s, g])
            )
    for copy in copies:
        copy.start()
    if passed:
        refs[-2][...] = pieces[0][...]
    for copy in copies:
        copy.wait()


def last_kernel(pos_ref, *refs, which):
    pieces = refs[: 2 * RING]
    out_ref, init_ref, gain_ref, rates_ref, extra_ref, sem = refs[-6:]
    copies = []
    for g, (half, m) in enumerate(which):
        core = pos_ref[0] if half == 0 else 1 - pos_ref[0]
        at = core * RING + ((pos_ref[1 + half] + TURNS[m]) & (RING - 1))
        rows = pl.ds(pl.multiple_of(at * CHUNK, CHUNK), CHUNK)
        for s in range(3):
            copies.append(
                pltpu.make_async_copy(
                    pieces[half * RING + m].at[pl.ds(s * CHUNK, CHUNK), :], out_ref.at[s, rows, :], sem.at[s, g]
                )
            )
    for copy in copies:
        copy.start()
    for p, piece in enumerate(pieces):
        core = pos_ref[0] if p < RING else 1 - pos_ref[0]
        at = core * RING + ((pos_ref[1 + p // RING] + TURNS[p % RING]) & (RING - 1))
        extra_ref[pl.ds(pl.multiple_of(at * PIECE, 8), PIECE), :] = piece[3 * CHUNK : 3 * CHUNK + PIECE, :]
    for h in range(init_ref.shape[0]):
        init_ref[h] = extra_ref[0:HS, span(h)]
        gain_ref[h : h + 1, :] = extra_ref[HS : HS + 1, span(h)]
        rates_ref[h] = extra_ref[HS + 1, h * HS]
    for copy in copies:
        copy.wait()


def moves(first, by):
    pairs = []
    for x in range(RING):
        for core in range(2):
            for y in range(RING):
                along_x = (core == 0) == first
                to_x = (x + by) % RING if along_x else x
                to_y = y if along_x else (y + by) % RING
                pairs.append(((x * 2 + core) * RING + y, (to_x * 2 + core) * RING + to_y))
    return pairs


def round_turn(chunks, first):
    return [
        lax.ppermute(chunk, ("dp", "ctx"), moves(first, turn)) for chunk, turn in zip(chunks, TURNS[1:])
    ]


def swap(value):
    return lax.ppermute(value, "dp", [(i, i ^ 1) for i in range(2 * RING)])


VM = pl.BlockSpec(memory_space=pltpu.VMEM)
SM = pl.BlockSpec(memory_space=pltpu.SMEM)
PARAMS = pltpu.CompilerParams(vmem_limit_bytes=20 * 1024 * 1024)


def shape(*dims, dtype=F32):
    return jax.ShapeDtypeStruct(dims, dtype)


def vmem(*dims, dtype=F32):
    return pltpu.VMEM(dims, dtype)


def hbm(value):
    return pltpu.with_memory_space_constraint(value, pltpu.HBM)


def whole(kernel, outs, specs, aliases=None):
    return pl.pallas_call(
        kernel,
        out_shape=outs,
        in_specs=specs,
        out_specs=tuple(VM for _ in outs) if isinstance(outs, tuple) else VM,
        input_output_aliases=aliases or {},
        compiler_params=PARAMS,
    )


def part(which, dims):
    return pl.BlockSpec((1,) + dims, lambda i: (which, 0, 0))


def full(*dims):
    return pl.BlockSpec(dims, lambda i: (0,) * len(dims))


def body(tokens, proj_weights, init_weight, base_rates, gate_values, out_gain, cotangent):
    n = tokens.shape[1]
    model = tokens.shape[2]
    heads = init_weight.shape[0]
    wide = heads * HS
    ctx = lax.axis_index("ctx")
    dp = lax.axis_index("dp")
    core, x_at = dp % 2, dp // 2
    pos = jnp.stack(
        [core, jnp.where(core == 0, x_at, ctx), jnp.where(core == 0, ctx, x_at), lax.axis_index("head"), ctx]
    ).astype(jnp.int32)
    half = model // 2

    wide_f32 = vmem(n, wide)
    square = vmem(heads, n, n)
    small = vmem(heads, HS, HS)
    wspec = functools.partial(part, dims=(model, wide))
    tokens = hbm(tokens)
    raw_weights = proj_weights
    proj_weights = hbm(proj_weights)
    anywhere = pl.BlockSpec(memory_space=pl.ANY)

    k, v, ninv, gram, inv, bt, decay, send, offset = pl.pallas_call(
        maps_kernel,
        grid=(1,),
        out_shape=(
            wide_f32, wide_f32, vmem(heads, n, HS), square, square, vmem(heads, HS, n), small, small, small,
        ),
        in_specs=[SM, SM, full(1, n, model), wspec(1), wspec(2), full(1, heads, n), full(heads, HS, HS)],
        out_specs=(VM,) * 9,
        compiler_params=PARAMS,
    )(pos, hbm(base_rates), tokens, proj_weights, proj_weights, hbm(gate_values), hbm(init_weight))

    near = lax.ppermute(send, "ctx", [(0, 1), (2, 3)])
    moved = lax.ppermute(decay, "ctx", [(2, 3), (1, 0)])
    moved_one = lax.ppermute(decay, "ctx", [(2, 1)])
    moved_two = lax.ppermute(decay, "ctx", [(2, 0)])

    q, score, rv, y, qt, zv, tokt, other_half = pl.pallas_call(
        reach_kernel,
        grid=(1,),
        out_shape=(wide_f32, square, wide_f32, wide_f32, wide_f32, wide_f32, vmem(half, n, dtype=BF), vmem(n, half)),
        in_specs=[SM, SM, full(1, n, model), wspec(0), full(1, heads, n), VM, VM, VM],
        out_specs=(VM,) * 8,
        compiler_params=PARAMS,
    )(pos, base_rates, tokens, proj_weights, gate_values, k, v, inv)

    second = whole(step_kernel, small, [VM] * 3 + [anywhere])(
        decay, near, offset, qt
    )
    mid = lax.ppermute(second, "ctx", [(1, 2)])
    far = lax.ppermute(second, "ctx", [(1, 3)])
    got_half = swap(other_half)
    other_tokt = whole(turn_kernel, vmem(half, n, dtype=BF), [VM])(got_half)

    w, back, pulled, dgain = whole(
        norm_kernel, (small, wide_f32, small, vmem(heads, HS)), [SM] + [VM] * 9 + [anywhere]
    )(pos, init_weight, near, mid, far, moved, qt, zv, cotangent, out_gain, other_tokt)

    back_one = lax.ppermute(pulled, "ctx", [(3, 2), (2, 1), (1, 0)])
    back_two = lax.ppermute(pulled, "ctx", [(3, 1), (2, 0)])
    back_three = lax.ppermute(pulled, "ctx", [(3, 0)])

    dq, r, x, dk, de = whole(
        query_kernel, (wide_f32, wide_f32, wide_f32, wide_f32, vmem(heads, n)), [SM] + [VM] * 10
    )(base_rates, gate_values, w, back, cotangent, q, score, rv, y, k, inv)

    grads, grad_gates = whole(
        keys_kernel, (vmem(3 * n + EXTRA, wide), shape(1, heads, n)), [SM, SM] + [VM] * 20
    )(pos, base_rates, gate_values, back_one, back_two, back_three, moved, moved_one, moved_two, pulled, decay, w, k, ninv, gram, bt, r, x,
      dk, de, dgain, dq)

    chunk = vmem(3 * CHUNK + PIECE, wide)
    quarter = vmem(n, model // RING)
    quarters = whole(token_kernel, (quarter,) * RING, [SM, VM, VM])(pos, raw_weights, grads)

    def along_head(terms, turn):
        return lax.ppermute(terms, "head", [(i, (i + turn) % RING) for i in range(RING)])

    given = (pos, tokt, other_tokt, grads, swap(grads))
    far_chunk = whole(
        functools.partial(product_kernel, turns=(2,), passed=0), chunk, [SM] + [VM] * 4
    )(*given)
    own, one_chunk, three_chunk, near_one, near_two = whole(
        functools.partial(product_kernel, turns=(0, 1, 3), passed=2),
        (chunk,) * 3 + (quarter,) * 2, [SM] + [VM] * 6 + [anywhere], {5: 3, 6: 4},
    )(*given, *quarters[1:3], far_chunk)
    away = round_turn([one_chunk, three_chunk, far_chunk], True)
    from_back, from_ahead, from_far = along_head(near_one, 1), along_head(near_two, 3), along_head(quarters[3], 2)

    part_sum = whole(sum_kernel, chunk, [VM] * 4 + [anywhere] * 2)(own, *away, from_back, from_ahead)
    grad_tokens = ((quarters[0] + from_far) + (from_back + from_ahead)).astype(BF).reshape(1, n, -1)
    total = whole(sum_kernel, chunk, [VM] * 4 + [anywhere])(
        part_sum, *round_turn([part_sum] * 3, False), grad_tokens
    )
    from_back, from_ahead, from_far = round_turn([total] * 3, True)
    out = shape(3, model, wide)

    def place(which, passed, *placed):
        given = [sides[half][m] for half, m in which]
        return pl.pallas_call(
            functools.partial(place_kernel, which=which, passed=passed),
            out_shape=(out, chunk) if passed else (out,),
            in_specs=[SM] + [VM] * len(given) + [anywhere] * len(placed),
            out_specs=(anywhere, VM) if passed else (anywhere,),
            scratch_shapes=[pltpu.SemaphoreType.DMA((3, len(which)))],
            input_output_aliases={len(given) + 1: 0} if placed else {},
            compiler_params=PARAMS,
        )(pos, *given, *placed)

    mine, others = [total, from_ahead, from_back, from_far], []
    sides = (mine, others)
    placed, own_piece = place(((0, 0), (0, 3)), True)
    others += [swap(given) for given in [own_piece] + mine[1:]]
    (placed,) = place(((0, 1), (0, 2), (1, 0), (1, 3)), False, placed)
    which = ((1, 1), (1, 2))
    grad_proj, grad_init, grad_gain, grad_rates = pl.pallas_call(
        functools.partial(last_kernel, which=which),
        out_shape=(out, shape(heads, HS, HS), shape(heads, HS), shape(heads)),
        in_specs=[SM] + [VM] * 8 + [anywhere],
        out_specs=(anywhere, VM, VM, SM),
        scratch_shapes=[pltpu.VMEM((EXTRA, wide), F32), pltpu.SemaphoreType.DMA((3, len(which)))],
        input_output_aliases={9: 0},
        compiler_params=PARAMS,
    )(pos, *mine, *others, placed)
    return (grad_tokens, grad_proj, grad_init, grad_gain, grad_rates, grad_gates)


def solution(mesh):
    in_specs = (
        P("dp", "ctx", None),
        P(None, None, "head"),
        P("head", None, None),
        P("head"),
        P("dp", "head", "ctx"),
        P("head", None),
        P("dp", "ctx", "head"),
    )
    out_specs = (
        P("dp", "ctx", "head"),
        P(None, None, "head"),
        P("head", None, None),
        P("head", None),
        P("head"),
        P("dp", "head", "ctx"),
    )
    return jax.shard_map(body, mesh=mesh, in_specs=in_specs, out_specs=out_specs, check_vma=False)
```
